32 devices in a mesh: gx: 8 (over y, x, core), gz: 4 (over z).
Axes of the slice: x: 2, y: 2, z: 4, core: 2. Of those that a mesh axis runs over, the one named last changes fastest.
Arguments:
- factor: float32 [3, 256, 4, 32, 256], P(None, 'gz', None, 'gx'), may hold values from -6 to 6
- gain: float32 [3, 256, 4, 32, 256], P(None, 'gz', None, 'gx'), may hold values from -6 to 6
- base_flow: float32 [256, 32, 256], P('gz', 'gx'), may hold values from 0.25 to 2
- shift_index: int32 [1], replicated, may hold values from 0 to 7
- sensor_cells: int32 [4, 4], replicated, may hold values from 0 to 255, as said below
Outputs:
- new_factor: float32 [3, 256, 4, 32, 256], P(None, 'gz', None, 'gx')
- new_gain: float32 [3, 256, 4, 32, 256], P(None, 'gz', None, 'gx')
- gram: float32 [4, 4], replicated
The draws below stay inside these ranges and needn't reach their ends.
Inputs may be any that keep to these rules, and one draw needn't show every extreme that they name: `sensor_cells`: row i gives sensor i's velocity component (0 to 2), spanwise index (0 to 255), streamwise index (0 to 31) and wall-normal index (0 to 255); in every draw some sensor sits at spanwise index 255, some at streamwise index 31 and some at wall-normal index 255.
All inputs are finite; a program needn't handle non-finite values.
Results may differ from the reference program's by a relative error of at most 0.03.
Values sent between devices are 32-bit elements; how exact they have to be, the bound alone decides.
No kernel may reach another device: no remote copies, remote signals or barrier semaphores. Data moves between devices by JAX's collectives and lax.ppermute only.
A program may use at most 64 MiB of HBM per device.

```python
import math
import jax
import jax.numpy as jnp
from jax import lax

COLS = 4
NZ = 256
NY = 256
SWEEPS = 3
POISSON = 4
SHIFTS = 8
NX = 32


def draw_sensor_cells(key, part):
    subkeys = jax.random.split(key, 7)
    rows = jnp.arange(COLS)
    component = jax.random.randint(subkeys[0], (COLS,), 0, 3)
    spanwise = jax.random.randint(subkeys[1], (COLS,), 0, NZ)
    streamwise = jax.random.randint(subkeys[2], (COLS,), 0, NX)
    normal = jax.random.randint(subkeys[3], (COLS,), 0, NY)
    span_row = jax.random.randint(subkeys[4], (), 0, COLS)
    stream_row = jax.random.randint(subkeys[5], (), 0, COLS)
    normal_row = jax.random.randint(subkeys[6], (), 0, COLS)
    spanwise = jnp.where(rows == span_row, NZ - 1, spanwise)
    streamwise = jnp.where(rows == stream_row, NX - 1, streamwise)
    normal = jnp.where(rows == normal_row, NY - 1, normal)
    return jnp.stack([component, spanwise, streamwise, normal], axis=1).astype(jnp.int32)


def block_levels(stream_key, dims, cuts, smallest, top_value):
    level = 1.0
    for dim, blocks in cuts:
        steps = jax.random.uniform(jax.random.fold_in(jax.random.fold_in(stream_key, 6), dim), (blocks,), jnp.float32, smallest / len(cuts), top_value / len(cuts))
        level = level * jnp.repeat(jnp.exp(steps), dims[dim] // blocks).reshape((-1,) + (1,) * (len(dims) - 1 - dim))
    return level


def normal_values(own_key, dims, deviation, most, pieces=(), kind=jnp.bfloat16):
    entries = deviation * jax.random.normal(own_key, dims, jnp.float32)
    if pieces:
        entries = entries * block_levels(own_key, dims, pieces, -0.22, 0.18)
    return jnp.clip(entries, -most, most).astype(kind)


def setup_inputs(seed: int = 0) -> dict:
    key_list = jax.random.split(jax.random.key(seed), 6)
    return {
        "factor": normal_values(key_list[0], (3, NZ, COLS, NX, NY), 1.0, 6.0, ((1, 4), (3, 8)), jnp.float32),
        "gain": normal_values(key_list[1], (3, NZ, COLS, NX, NY), 1.0, 6.0, ((1, 4), (3, 8)), jnp.float32),
        "base_flow": jnp.clip(jnp.exp(math.log(2.0) - 2.0794415 * jax.random.uniform(key_list[2], (NZ, NX, NY), jnp.float32) ** block_levels(key_list[2], (NZ, NX, NY), ((0, 4), (1, 8)), -0.2, 0.2)), 0.25, 2.0),
        "shift_index": jax.random.randint(key_list[3], (1,), 0, SHIFTS).astype(jnp.int32),
        "sensor_cells": draw_sensor_cells(jax.random.fold_in(key_list[5], 71), 0),
    }


viscosity = 0.4
shift_table = (0.6, 0.8, 1.0, 1.25, 1.6, 2.0, 2.5, 3.2)
chebyshev_weights = (1.0 / 1.9352976, 1.0 / 1.4752809, 1.0 / 0.8247191, 1.0 / 0.3647024)
highest = lax.Precision.HIGHEST

def neighbours(grid_field):
    padded = jnp.pad(grid_field, ((0, 0), (0, 0), (0, 0), (1, 1), (1, 1)))
    summed = padded[:, :, :, 2:, 1:-1] + padded[:, :, :, :-2, 1:-1]
    summed = summed + padded[:, :, :, 1:-1, 2:] + padded[:, :, :, 1:-1, :-2]
    summed = summed + jnp.roll(grid_field, 1, axis=1) + jnp.roll(grid_field, -1, axis=1)
    return (summed, padded[:, :, :, :-2, 1:-1])

def hartley(grid_field):
    spectrum = jnp.fft.fft(grid_field, axis=0)
    return (jnp.real(spectrum) - jnp.imag(spectrum)) / math.sqrt(NZ)

def reference(factor, gain, base_flow, shift_index, sensor_cells):
    shift_value = jnp.asarray(shift_table, jnp.float32)[shift_index[0]]
    base_field = base_flow[None, :, None, :, :]
    diagonal = shift_value + 6.0 * viscosity + base_field
    source = -factor
    velocity = source / diagonal
    for sweep_index in range(SWEEPS):
        beside_all, behind = neighbours(velocity)
        velocity = (source + viscosity * beside_all + base_field * behind) / diagonal
    stream = velocity[0]
    normal = velocity[1]
    spanwise = velocity[2]
    divergence = 2.0 * (stream - jnp.pad(stream, ((0, 0), (0, 0), (1, 0), (0, 0)))[:, :, :-1, :])
    divergence = divergence + (normal - jnp.pad(normal, ((0, 0), (0, 0), (0, 0), (1, 0)))[:, :, :, :-1])
    divergence = divergence + (spanwise - jnp.roll(spanwise, 1, axis=0))
    modes_rhs = -hartley(divergence)
    wavenumber = 2.0 * math.pi * jnp.arange(NZ).astype(jnp.float32) / NZ
    mode_diagonal = (10.0 + (2.0 - 2.0 * jnp.cos(wavenumber)))[:, None, None, None]
    pressure = chebyshev_weights[0] * modes_rhs / mode_diagonal
    for sweep_level in range(1, POISSON):
        padded = jnp.pad(pressure, ((0, 0), (0, 0), (1, 1), (1, 1)))
        beside_all = 4.0 * (padded[:, :, 2:, 1:-1] + padded[:, :, :-2, 1:-1]) + padded[:, :, 1:-1, 2:] + padded[:, :, 1:-1, :-2]
        pressure = pressure + chebyshev_weights[sweep_level] * (modes_rhs - (mode_diagonal * pressure - beside_all)) / mode_diagonal
    pressure = hartley(pressure)
    padded = jnp.pad(pressure, ((0, 0), (0, 0), (0, 1), (0, 1)))
    gradient = jnp.stack([2.0 * (padded[:, :, 1:, :-1] - pressure), padded[:, :, :-1, 1:] - pressure, jnp.roll(pressure, -1, axis=0) - pressure])
    solved = velocity - gradient
    new_factor = factor + 2.0 * shift_value * solved
    readout = solved[sensor_cells[:, 0], sensor_cells[:, 1], :, sensor_cells[:, 2], sensor_cells[:, 3]]
    new_gain = gain + 2.0 * shift_value * jnp.einsum('czjxy,ij->czixy', solved, readout, precision=highest)
    gram = jnp.einsum('czixy,czjxy->ij', new_factor, new_factor, precision=highest) / (3.0 * NX * NY * NZ)
    return (new_factor, new_gain, gram)
```

```python
import math

import jax
import jax.numpy as jnp
import numpy as np
from jax import lax
from jax.experimental import pallas as pl
from jax.experimental.pallas import tpu as pltpu
from jax.sharding import PartitionSpec as P

SWEEPS = 3
POISSON = 4
SHIFTS = 8


viscosity = 0.4
shift_table = (0.6, 0.8, 1.0, 1.25, 1.6, 2.0, 2.5, 3.2)
chebyshev_weights = (1.0 / 1.9352976, 1.0 / 1.4752809, 1.0 / 0.8247191, 1.0 / 0.3647024)
highest = lax.Precision.HIGHEST


def padded_2(cells, sides, width, closed):
    for axis, dim in sides:
        count = lax.axis_size(axis)
        ends = count if closed else count - 1
        head = lax.slice_in_dim(cells, 0, width, axis=dim)
        tail = lax.slice_in_dim(cells, cells.shape[dim] - width, cells.shape[dim], axis=dim)
        cells = jnp.concatenate(
            [
                lax.ppermute(tail, axis, [(i, (i + 1) % count) for i in range(ends)]),
                cells,
                lax.ppermute(head, axis, [((i + 1) % count, i) for i in range(ends)]),
            ],
            axis=dim,
        )
    return cells


def around_sum(padded):
    summed = padded[:, 1:-1, :, 2:, 1:-1] + padded[:, 1:-1, :, :-2, 1:-1]
    summed = summed + padded[:, 1:-1, :, 1:-1, 2:] + padded[:, 1:-1, :, 1:-1, :-2]
    return summed + padded[:, 2:, :, 1:-1, 1:-1] + padded[:, :-2, :, 1:-1, 1:-1]


def shards(factor, gain, base_flow, shift_index, sensor_cells):
    components, span_cells, columns, stream_cells, normal_cells = factor.shape
    stream_start = lax.axis_index("gx") * stream_cells
    span_start = lax.axis_index("gz") * span_cells
    stream_total = stream_cells * lax.axis_size("gx")
    span_total = span_cells * lax.axis_size("gz")
    shift_values = jnp.asarray(shift_table, jnp.float32)
    shift_value = jnp.sum(jnp.where(jnp.arange(SHIFTS) == shift_index[0], shift_values, 0.0))
    base_field = base_flow[None, :, None, :, :]
    diagonal = shift_value + 6.0 * viscosity + base_field
    source = -factor

    def stream_inside(extent, margin):
        positions = stream_start - margin + jnp.arange(extent)
        return ((positions >= 0) & (positions < stream_total)).astype(jnp.float32)

    def extend(grid_field):
        padded = padded_2(grid_field, (("gx", 3), ("gz", 1)), 1, True)
        padded = padded * stream_inside(stream_cells + 2, 1)[None, None, None, :, None]
        return jnp.pad(padded, ((0, 0), (0, 0), (0, 0), (0, 0), (1, 1)))

    velocity = source / diagonal
    for sweep_index in range(SWEEPS):
        padded = extend(velocity)
        velocity = (
            source + viscosity * around_sum(padded) + base_field * padded[:, 1:-1, :, :-2, 1:-1]
        ) / diagonal
    padded = extend(velocity)
    divergence = 2.0 * (velocity[0] - padded[0, 1:-1, :, :-2, 1:-1])
    divergence = divergence + (velocity[1] - padded[1, 1:-1, :, 1:-1, :-2])
    divergence = divergence + (velocity[2] - padded[2, :-2, :, 1:-1, 1:-1])
    span_index = jnp.arange(span_total)
    products = span_index[:, None] * span_index[None, :] % span_total
    angles = 2.0 * math.pi * products.astype(jnp.float32) / span_total
    hartley_table = (jnp.cos(angles) + jnp.sin(angles)) / math.sqrt(span_total)

    def turn_modes(exchanged):
        turned = jnp.einsum("kz,zay->kay", hartley_table, exchanged, precision=highest)
        return lax.all_to_all(turned, "gz", split_axis=0, concat_axis=1, tiled=True)

    def transform(grid_field):
        flat = grid_field.reshape(span_cells, columns * stream_cells, normal_cells)
        result = turn_modes(lax.all_to_all(flat, "gz", split_axis=1, concat_axis=0, tiled=True))
        return result.reshape(span_cells, columns, stream_cells, normal_cells)

    modes_rhs = -transform(divergence)
    wave_index = span_start + jnp.arange(span_cells)
    wavenumber = 2.0 * math.pi * wave_index.astype(jnp.float32) / span_total
    mode_diagonal = (10.0 + (2.0 - 2.0 * jnp.cos(wavenumber)))[:, None, None, None]
    pressure = chebyshev_weights[0] * modes_rhs / mode_diagonal
    for sweep_level in range(1, POISSON):
        padded = padded_2(pressure, (("gx", 2),), 1, False)
        padded = jnp.pad(padded, ((0, 0), (0, 0), (0, 0), (1, 1)))
        beside_all = (
            4.0 * (padded[:, :, 2:, 1:-1] + padded[:, :, :-2, 1:-1])
            + padded[:, :, 1:-1, 2:]
            + padded[:, :, 1:-1, :-2]
        )
        pressure = (
            pressure
            + chebyshev_weights[sweep_level]
            * (modes_rhs - (mode_diagonal * pressure - beside_all))
            / mode_diagonal
        )
    pressure = transform(pressure)
    padded = extend(pressure[None])[0]
    gradient = jnp.stack(
        [
            2.0 * (padded[1:-1, :, 2:, 1:-1] - pressure),
            padded[1:-1, :, 1:-1, 2:] - pressure,
            padded[2:, :, 1:-1, 1:-1] - pressure,
        ]
    )
    solved = velocity - gradient
    span_ids = span_start + jnp.arange(span_cells)
    stream_ids = stream_start + jnp.arange(stream_cells)
    normal_ids = jnp.arange(normal_cells)
    located = span_ids[None, :, None, None] == sensor_cells[:, 1][:, None, None, None]
    located = located & (stream_ids[None, None, :, None] == sensor_cells[:, 2][:, None, None, None])
    located = located & (normal_ids[None, None, None, :] == sensor_cells[:, 3][:, None, None, None])
    picked = jnp.einsum("szxy,czjxy->scj", located.astype(jnp.float32), solved, precision=highest)
    chooser = (jnp.arange(3)[None, :] == sensor_cells[:, 0:1]).astype(jnp.float32)
    readout_local = jnp.sum(picked * chooser[:, :, None], axis=1)
    new_factor = factor + 2.0 * shift_value * solved
    gram_local = jnp.einsum("czixy,czjxy->ij", new_factor, new_factor, precision=highest)
    gram_total, readout = lax.psum((gram_local, readout_local), ("gx", "gz"))
    gram = gram_total / (3.0 * stream_total * normal_cells * span_total)
    new_gain = gain + 2.0 * shift_value * jnp.einsum(
        "czjxy,ij->czixy", solved, readout, precision=highest
    )
    return (new_factor, new_gain, gram)


HALF = 32
PAIRS = 8


def recurrence_tables(centre, weights):
    ratio = centre / 2.0 - math.sqrt(centre * centre / 4.0 - 1.0)
    order = len(weights)
    step = ratio * np.tril(np.ones((order, order)))
    half = np.linalg.matrix_power(step, HALF)
    whole = np.linalg.matrix_power(step, 2 * HALF)
    angles = 2.0 * np.pi * np.arange(4096) / 4096
    series = [weights[0]]
    for weight in weights[1:]:
        longer = [0.0] + [weight * entry for entry in series]
        for place, entry in enumerate(series):
            longer[place] += (1.0 - weight) * entry
        longer[0] += weight
        series = longer
    mixes = []
    for power in range(1, order + 1):
        symbol = 1.0 / (centre - 2.0 * np.cos(angles)) ** power
        kernel = [np.mean(symbol * np.cos(angles * n)) for n in range(order + 1)]
        matrix = [[math.comb(n + i - 1, i - 1) for i in range(1, power + 1)] for n in range(1, power + 1)]
        sides = np.linalg.solve(
            np.array(matrix, np.float64), [kernel[n] / ratio**n for n in range(1, power + 1)]
        )
        middle = kernel[0] - 2.0 * np.sum(sides)
        mixes.append([float(series[power - 1] * entry) for entry in [middle, *sides]])
    return float(ratio), half.tolist(), whole, mixes


RATIO, HALF_TABLE, WHOLE_TABLE, MIXES = recurrence_tables(12.0, chebyshev_weights)


def lower_half():
    return lax.broadcasted_iota(jnp.int32, (8, 256), 0) < 4


def swap(cells):
    return pltpu.roll(cells, 4, 0)


def below(cells):
    lanes = lax.broadcasted_iota(jnp.int32, (8, 256), 1)
    return jnp.where(lanes > 0, pltpu.roll(cells, 1, 1), 0.0)


def above(cells):
    lanes = lax.broadcasted_iota(jnp.int32, (8, 256), 1)
    return jnp.where(lanes < 255, pltpu.roll(cells, 255, 1), 0.0)


def shift_of(index_ref):
    index = index_ref[0]
    value = jnp.float32(shift_table[0])
    for place in range(1, SHIFTS):
        value = jnp.where(index == place, jnp.float32(shift_table[place]), value)
    return value


def x_odd():
    return lax.rem(lax.axis_index("gx"), 2)


def z_even():
    return lax.rem(lax.axis_index("gz"), 2) == 0


def cascade(state, cells):
    grown = []
    for entry in state:
        cells = RATIO * entry + cells
        grown.append(cells)
    return tuple(grown)


def half_states(read):
    zero = jnp.zeros((8, 256), jnp.float32)

    def body(t, carry):
        forward, backward = carry
        return cascade(forward, read(t)), cascade(backward, read(HALF - 1 - t))

    return lax.fori_loop(0, HALF, body, ((zero,) * POISSON, (zero,) * POISSON), unroll=8)


def turned(table, states, row):
    total = None
    for column in range(row + 1):
        term = table[row][column] * states[column]
        total = term if total is None else total + term
    return total


FACTOR_AT = 24
PART = 152
CORNERS = [(c, dx, side, 0) for c in range(3) for dx in (1, 2) for side in (0, 1)]
CORNERS += [(2, 1, 0, 1), (2, 3, 0, 0)]


def pack_kernel(factor_ref, base_ref, own_ref, a_ref, b1_ref, b2_ref, z1_ref, z2_ref):
    odd = x_odd()
    even = 1 - odd
    low = lax.broadcasted_iota(jnp.int32, (8, 128), 0) < 4
    scale = -1.0 / viscosity
    for component in range(3):

        def load(m, _, component=component):
            for x in range(4):
                for tile in range(2):
                    row = (component * 64 + 2 * m) * 32 + tile * 4 + x
                    first = factor_ref[pl.ds(row, 8, stride=8), :] * scale
                    second = factor_ref[pl.ds(row + 1024, 8, stride=8), :] * scale
                    lanes = slice(tile * 128, tile * 128 + 128)
                    own_ref[component, x, 2 * m, :, lanes] = jnp.where(low, first, swap(second))
                    own_ref[component, x, 2 * m + 1, :, lanes] = jnp.where(low, swap(first), second)
            return 0

        lax.fori_loop(0, 16, load, 0)

    def edges(zz, _):
        for component in range(3):
            for layer in range(3):
                at = FACTOR_AT + (component * 3 + layer) * HALF
                a_ref[at + zz] = own_ref[component, layer + even, zz]
                cells = own_ref[component, layer + odd, zz]
                if at < PART:
                    b1_ref[at + zz] = cells
                else:
                    b2_ref[at - PART + zz] = cells
        return 0

    lax.fori_loop(0, HALF, edges, 0)
    for layer in range(3):
        for group in range(8):
            for tile in range(2):
                lanes = slice(tile * 128, tile * 128 + 128)
                row = group * 64 + tile * 4 + layer
                a_ref[layer * 8 + group, :, lanes] = base_ref[pl.ds(row + even, 8, stride=8), :]
                b1_ref[layer * 8 + group, :, lanes] = base_ref[pl.ds(row + odd, 8, stride=8), :]
    lower = lower_half()
    rightward = z_even()
    for component in range(3):
        for x in range(4):
            for pair in range(2):
                cells = lambda zz: own_ref[component, x, zz]
                up = jnp.where(lower, swap(cells(31 - 2 * pair)), cells(30 - 2 * pair))
                down = jnp.where(lower, cells(2 * pair), swap(cells(2 * pair + 1)))
                at = (component * 4 + x) * 2 + pair
                z1_ref[at] = jnp.where(rightward, up, down)
                z2_ref[at] = jnp.where(rightward, down, up)
    for k in range(4):
        for tile in range(2):
            lanes = slice(tile * 128, tile * 128 + 128)
            up = base_ref[(63 - k) * 8 + tile * 4 : (63 - k) * 8 + tile * 4 + 4, :]
            down = base_ref[k * 8 + tile * 4 : k * 8 + tile * 4 + 4, :]
            rows = slice((k % 2) * 4, (k % 2) * 4 + 4)
            z1_ref[24 + k // 2, rows, lanes] = jnp.where(rightward, up, down)
            z2_ref[24 + k // 2, rows, lanes] = jnp.where(rightward, down, up)


def corner_kernel(z1_ref, z2_ref, a_ref, b_ref):
    odd = x_odd()
    rightward = z_even()

    def fill(behind_ref, ahead_ref):
        for place, (component, dx, side, pair) in enumerate(CORNERS):
            source = (behind_ref, ahead_ref)[side]
            right_x = 4 - dx
            left_x = dx - 1
            a_x = jnp.where(odd == 1, left_x, right_x)
            b_x = jnp.where(odd == 1, right_x, left_x)
            a_ref[place] = source[(component * 4 + a_x) * 2 + pair]
            b_ref[place] = source[(component * 4 + b_x) * 2 + pair]
        for dx in (1, 2, 3):
            for k in range(4):
                for side, source in enumerate((behind_ref, ahead_ref)):
                    from_right = source[24 + k // 2, (k % 2) * 4 + 4 - dx, :]
                    from_left = source[24 + k // 2, (k % 2) * 4 + dx - 1, :]
                    at = len(CORNERS) + dx - 1
                    a_ref[at, side * 4 + k, :] = jnp.where(odd == 1, from_left, from_right)
                    b_ref[at, side * 4 + k, :] = jnp.where(odd == 1, from_right, from_left)

    @pl.when(rightward)
    def _():
        fill(z2_ref, z1_ref)

    @pl.when(jnp.logical_not(rightward))
    def _():
        fill(z1_ref, z2_ref)


def velocity_kernel(
    index_ref, own_ref, base_ref, a_ref, b1_ref, b3_ref, b2_ref, ca_ref, cb_ref, z1_ref, z2_ref,
    v_ref, bw_ref, s_ref,
    flow_ref, a1_ref, r_ref, v0_ref, va_ref, vb_ref,
):
    odd = x_odd()
    stream = lax.axis_index("gx")
    last = lax.axis_size("gx") - 1
    mask_left = jnp.where(stream > 0, 1.0, 0.0)
    mask_right = jnp.where(stream < last, 1.0, 0.0)
    relayed = jnp.logical_or(stream == 3, stream == 4)
    rightward = z_even()
    lower = lower_half()
    shift = shift_of(index_ref)

    def each_z(step):
        @pl.when(rightward)
        def _():
            step(z2_ref, z1_ref)

        @pl.when(jnp.logical_not(rightward))
        def _():
            step(z1_ref, z2_ref)

    def inside(at):
        return lambda zz: a_ref[at + zz]

    def outside(first_ref):
        def pick(at):
            if at < PART:
                return lambda zz: first_ref[at + zz]
            return lambda zz: b2_ref[at - PART + zz]

        return pick

    def each_x(step):
        @pl.when(jnp.logical_and(odd == 0, relayed))
        def _():
            step(outside(b3_ref), cb_ref, inside, ca_ref)

        @pl.when(jnp.logical_and(odd == 0, jnp.logical_not(relayed)))
        def _():
            step(outside(b1_ref), cb_ref, inside, ca_ref)

        @pl.when(jnp.logical_and(odd == 1, relayed))
        def _():
            step(inside, ca_ref, outside(b3_ref), cb_ref)

        @pl.when(jnp.logical_and(odd == 1, jnp.logical_not(relayed)))
        def _():
            step(inside, ca_ref, outside(b1_ref), cb_ref)

    for x in range(4):
        for group in range(8):
            for tile in range(2):
                lanes = slice(tile * 128, tile * 128 + 128)
                flow_ref[x + 3, 8 + 8 * group : 16 + 8 * group, lanes] = base_ref[
                    pl.ds(group * 64 + tile * 4 + x, 8, stride=8), :
                ]

    def flow_span(behind_ref, ahead_ref):
        for x in range(4):
            for k in range(4):
                at = 24 + k // 2
                row = (k % 2) * 4 + x
                flow_ref[x + 3, 7 - k, :] = behind_ref[at, row, :]
                flow_ref[x + 3, 72 + k, :] = ahead_ref[at, row, :]

    each_z(flow_span)

    def flow_stream(left, left_corner, right, right_corner):
        for dx in (1, 2, 3):
            for place, layer, read, corner in (
                (3 - dx, 3 - dx, left, left_corner),
                (6 + dx, dx - 1, right, right_corner),
            ):
                for group in range(8):
                    flow_ref[place, 8 + 8 * group : 16 + 8 * group, :] = read(layer * 8)(group)
                for k in range(4):
                    flow_ref[place, 7 - k, :] = corner[len(CORNERS) + dx - 1, k, :]
                    flow_ref[place, 72 + k, :] = corner[len(CORNERS) + dx - 1, 4 + k, :]

    each_x(flow_stream)

    def coefficients(zz, _):
        for x in range(10):
            first = jnp.broadcast_to(flow_ref[x, pl.ds(zz + 4, 1), :], (8, 256))
            second = jnp.broadcast_to(flow_ref[x, pl.ds(zz + 36, 1), :], (8, 256))
            flow = jnp.where(lower, first, second)
            scale = viscosity * (mask_left if x < 3 else mask_right if x > 6 else 1.0)
            a1_ref[x, zz] = scale / (shift + 6.0 * viscosity + flow)
            r_ref[x, zz] = 1.0 + flow * (1.0 / viscosity)
        return 0

    lax.fori_loop(0, 39, coefficients, 0)
    zero = jnp.zeros((8, 256), jnp.float32)
    for x in (0, 1, 2, 7, 8, 9):
        for zz in (0, 1, 2, 3, 36, 37, 38):
            v0_ref[x, zz] = zero

    def sweep(source, target, margin):
        def body(zz, _):
            layers = {x: source[x, zz] for x in range(2 - margin, 8 + margin)}
            for x in range(3 - margin, 7 + margin):
                centre = layers[x]
                total = layers[x + 1] + (below(centre) + above(centre))
                total = total + (source[x, zz + 1] + source[x, zz - 1])
                target[x, zz] = v0_ref[x, zz] + a1_ref[x, zz] * (total + r_ref[x, zz] * layers[x - 1])
            return 0

        lax.fori_loop(3 - margin, 36 + margin, body, 0)

    for component in range(3):

        def interior(zz, _, component=component):
            for x in range(4):
                v0_ref[x + 3, zz + 4] = own_ref[component, x, zz] * a1_ref[x + 3, zz + 4]
            return 0

        lax.fori_loop(0, HALF, interior, 0)

        def before(cells, halo, k):
            if k % 2 == 0:
                return jnp.where(lower, halo, swap(cells))
            return swap(jnp.where(lower, cells, halo))

        def after(cells, halo, k):
            if k % 2 == 0:
                return swap(jnp.where(lower, halo, cells))
            return jnp.where(lower, swap(cells), halo)

        def span(behind_ref, ahead_ref, component=component):
            for x in range(4):
                at = (component * 4 + x) * 2
                for k in range(4):
                    cells = before(own_ref[component, x, 31 - k], behind_ref[at + k // 2], k)
                    v0_ref[x + 3, 3 - k] = cells * a1_ref[x + 3, 3 - k]
                for k in range(3):
                    cells = after(own_ref[component, x, k], ahead_ref[at + k // 2], k)
                    v0_ref[x + 3, 36 + k] = cells * a1_ref[x + 3, 36 + k]

        each_z(span)

        def sides(left, left_corner, right, right_corner, component=component):
            for dx in (1, 2, 3):
                for place, layer, pick, corner in (
                    (3 - dx, 3 - dx, left, left_corner),
                    (6 + dx, dx - 1, right, right_corner),
                ):
                    read = pick(FACTOR_AT + (component * 3 + layer) * HALF)

                    def body(zz, _, read=read, place=place):
                        v0_ref[place, zz + 4] = read(zz) * a1_ref[place, zz + 4]
                        return 0

                    lax.fori_loop(0, HALF, body, 0, unroll=4)
                    for entry, (c, away, side, pair) in enumerate(CORNERS):
                        if c != component or away != dx:
                            continue
                        for k in (2 * pair, 2 * pair + 1):
                            if side == 0:
                                cells = before(read(31 - k), corner[entry], k)
                                v0_ref[place, 3 - k] = cells * a1_ref[place, 3 - k]
                            else:
                                cells = after(read(k), corner[entry], k)
                                v0_ref[place, 36 + k] = cells * a1_ref[place, 36 + k]

        each_x(sides)
        sweep(v0_ref, va_ref, 2)
        sweep(va_ref, vb_ref, 1)
        sweep(vb_ref, va_ref, 0)

        def diverge(zz, _, component=component):
            for x in range(4):
                cells = va_ref[x + 3, zz + 4]
                v_ref[component, x, zz] = cells
                if component == 0:
                    inner = cells if x == 0 else cells - va_ref[x + 2, zz + 4]
                    bw_ref[x, zz] = -2.0 * inner
                elif component == 1:
                    bw_ref[x, zz] = bw_ref[x, zz] - (cells - below(cells))
                else:
                    bw_ref[x, zz] = bw_ref[x, zz] - (cells - va_ref[x + 3, zz + 3])
            if component == 0:
                bw_ref[4, zz] = va_ref[6, zz + 4]
            return 0

        lax.fori_loop(0, HALF, diverge, 0)

    def states(layer, _):
        forward, backward = half_states(lambda t: bw_ref[layer, t])
        swapped_forward = [swap(entry) for entry in forward]
        swapped_backward = [swap(entry) for entry in backward]
        for i in range(POISSON):
            onward = forward[i] + turned(HALF_TABLE, swapped_forward, i)
            back = backward[i] + turned(HALF_TABLE, swapped_backward, i)
            s_ref[i, layer] = jnp.where(lower, back, onward)
        s_ref[POISSON, layer] = bw_ref[layer, 0]
        return 0

    lax.fori_loop(0, 5, states, 0)


def pressure_kernel(
    index_ref, cells_ref, v_ref, bw_ref, ba_ref, bb_ref, inc_ref, ia_ref, ib_ref, factor_ref,
    nf_ref, solved_ref, sums_ref,
    f_ref, i_ref, u_ref, q_ref, t_ref,
):
    odd = x_odd()
    stream = lax.axis_index("gx")
    span = lax.axis_index("gz")
    last = lax.axis_size("gx") - 1
    mask_left = jnp.where(stream > 0, 1.0, 0.0)
    mask_right = jnp.where(stream < last, 1.0, 0.0)
    lower = lower_half()
    shift = shift_of(index_ref)

    def gather(left_ref, right_ref, left_inc, right_inc):
        def body(zz, _):
            for x in range(3):
                f_ref[x, zz] = left_ref[x, zz]
                f_ref[x + 4, zz] = bw_ref[x + 1, zz]
                f_ref[x + 8, zz] = right_ref[x + 1, zz]
            f_ref[3, zz] = bw_ref[0, zz] + 2.0 * left_ref[3, zz]
            f_ref[7, zz] = mask_right * (right_ref[0, zz] + 2.0 * bw_ref[4, zz])
            return 0

        lax.fori_loop(0, HALF, body, 0)
        for i in range(POISSON + 1):
            for x in range(3):
                i_ref[i, x] = left_inc[i, x]
                i_ref[i, x + 4] = inc_ref[i, x + 1]
                i_ref[i, x + 8] = right_inc[i, x + 1]
            i_ref[i, 3] = inc_ref[i, 0] + 2.0 * left_inc[i, 3]
            i_ref[i, 7] = mask_right * (right_inc[i, 0] + 2.0 * inc_ref[i, 4])
        for x in range(11):
            f_ref[x, HALF] = swap(jnp.where(lower, i_ref[POISSON, x], f_ref[x, 0]))

    @pl.when(odd == 0)
    def _():
        gather(bb_ref, ba_ref, ib_ref, ia_ref)

    @pl.when(odd == 1)
    def _():
        gather(ba_ref, bb_ref, ia_ref, ib_ref)

    def solve(x, _):
        forward, backward = half_states(lambda t: f_ref[x, t])
        arriving = [i_ref[i, x] for i in range(POISSON)]
        swapped = [swap(entry) for entry in arriving]
        onward = []
        back = []
        for i in range(POISSON):
            carried = turned(HALF_TABLE, swapped, i)
            onward.append(swap(jnp.where(lower, forward[i] + carried, arriving[i])))
            back.append(swap(jnp.where(lower, arriving[i], backward[i] + carried)))

        def ahead(zz, state):
            state = cascade(state, f_ref[x, zz])
            for i in range(POISSON):
                u_ref[i, zz] = state[i]
            return state

        lax.fori_loop(0, HALF, ahead, tuple(onward), unroll=8)
        end = cascade([u_ref[i, HALF - 1] for i in range(POISSON)], f_ref[x, HALF])
        for i in range(POISSON):
            u_ref[i, HALF] = end[i]

        def mix(zz, state):
            both = [f_ref[x, zz]] + [u_ref[i, zz] + state[i] for i in range(POISSON)]
            for power in range(POISSON):
                total = MIXES[power][0] * both[0]
                for i in range(1, power + 2):
                    total = total + MIXES[power][i] * both[i]
                q_ref[power, x, zz] = total

        mix(HALF, back)

        def behind(t, state):
            zz = HALF - 1 - t
            state = cascade(state, f_ref[x, zz])
            mix(zz, state)
            return state

        lax.fori_loop(0, HALF, behind, tuple(back), unroll=8)
        return 0

    lax.fori_loop(0, 11, solve, 0)
    for power in (2, 1, 0):

        def apply(zz, _, power=power):
            edge = 2 - power
            layers = {x: q_ref[power + 1, x, zz] for x in range(edge, 11 - edge)}
            for x in range(edge + 1, 10 - edge if power else 8):
                beside = 4.0 * (layers[x - 1] + layers[x + 1]) + (below(layers[x]) + above(layers[x]))
                if x < 3:
                    beside = mask_left * beside
                if x > 6:
                    beside = mask_right * beside
                q_ref[power, x, zz] = q_ref[power, x, zz] + beside
            return 0

        lax.fori_loop(0, HALF + 1, apply, 0)

    def correct(m, _):
        for x in range(4):
            pair = []
            for zz in (2 * m, 2 * m + 1):
                centre = q_ref[0, x + 3, zz]
                pair.append(
                    (
                        v_ref[0, x, zz] - 2.0 * (q_ref[0, x + 4, zz] - centre),
                        v_ref[1, x, zz] - (above(centre) - centre),
                        v_ref[2, x, zz] - (q_ref[0, x + 3, zz + 1] - centre),
                    )
                )
            for component in range(3):
                first, second = pair[0][component], pair[1][component]
                early = jnp.where(lower, first, swap(second))
                late = jnp.where(lower, swap(first), second)
                for tile in range(2):
                    row = (component * 64 + 2 * m) * 32 + tile * 4 + x
                    lanes = slice(tile * 128, tile * 128 + 128)
                    solved_ref[pl.ds(row, 8, stride=8), :] = early[:, lanes]
                    solved_ref[pl.ds(row + 1024, 8, stride=8), :] = late[:, lanes]
        return 0

    lax.fori_loop(0, 16, correct, 0)
    couples = [(i, j) for i in range(4) for j in range(i, 4)]

    def update(block, sums):
        columns = []
        for i in range(4):
            rows = pl.ds(pl.multiple_of(block * 32 + 8 * i, 8), 8)
            cells = factor_ref[rows, :] + (2.0 * shift) * solved_ref[rows, :]
            nf_ref[rows, :] = cells
            columns.append(cells)
        return tuple(s + columns[i] * columns[j] for s, (i, j) in zip(sums, couples))

    zero = jnp.zeros((8, 128), jnp.float32)
    sums = lax.fori_loop(0, 192, update, (zero,) * len(couples), unroll=4)
    t_ref[...] = jnp.zeros((32, 128), jnp.float32)
    for total, (i, j) in zip(sums, couples):
        t_ref[4 * i + j : 4 * i + j + 1, :] = jnp.sum(total, axis=0, keepdims=True)
    lanes = lax.broadcasted_iota(jnp.int32, (1, 128), 1)
    for sensor in range(4):
        component = cells_ref[sensor, 0]
        z = cells_ref[sensor, 1] - span * 64
        x = cells_ref[sensor, 2] - stream * 4
        y = cells_ref[sensor, 3]
        held = (z >= 0) & (z < 64) & (x >= 0) & (x < 4)
        z = jnp.clip(z, 0, 63)
        x = jnp.clip(x, 0, 3)
        tile = jnp.where(y >= 128, 1, 0)
        lane = jnp.where(held, y - 128 * tile, -1)
        for column in range(4):
            row = (component * 64 + z) * 32 + column * 8 + tile * 4 + x
            cells = solved_ref[pl.ds(row, 1), :]
            at = 16 + 4 * sensor + column
            t_ref[at : at + 1, :] = jnp.where(lanes == lane, cells, 0.0)
    totals = jnp.sum(t_ref[...], axis=1, keepdims=True)
    spread = lax.broadcasted_iota(jnp.int32, (32, 128), 1) == lax.broadcasted_iota(jnp.int32, (32, 128), 0)
    sums_ref[...] = jnp.sum(jnp.where(spread, totals, 0.0), axis=0, keepdims=True)


def gain_kernel(index_ref, sums_ref, gain_ref, solved_ref, out_ref, gram_ref, c_ref):
    @pl.when(pl.program_id(0) == 0)
    def _():
        totals = jnp.sum(sums_ref[...], axis=0, keepdims=True)
        lanes = lax.broadcasted_iota(jnp.int32, (1, 128), 1)
        shift = shift_of(index_ref)
        for i in range(4):
            for j in range(4):
                c_ref[i, j] = 2.0 * shift * jnp.sum(jnp.where(lanes == 16 + 4 * i + j, totals, 0.0))
                at = 4 * min(i, j) + max(i, j)
                gram_ref[i, j] = jnp.sum(jnp.where(lanes == at, totals, 0.0)) / 6291456.0

    table = [[c_ref[i, j] for j in range(4)] for i in range(4)]

    def body(block, _):
        rows = [pl.ds(pl.multiple_of(block * 32 + 8 * j, 8), 8) for j in range(4)]
        columns = [solved_ref[rows[j], :] for j in range(4)]
        for i in range(4):
            total = gain_ref[rows[i], :]
            for j in range(4):
                total = total + table[i][j] * columns[j]
            out_ref[rows[i], :] = total
        return 0

    lax.fori_loop(0, out_ref.shape[0] // 32, body, 0, unroll=2)


def call(kernel, outputs, scratch, operands, smalls, flops):
    arrays = [jax.ShapeDtypeStruct(shape, jnp.float32) for shape in outputs]
    places = [pl.BlockSpec(memory_space=pltpu.SMEM)] * smalls
    places += [pl.BlockSpec(memory_space=pltpu.VMEM)] * (len(operands) - smalls)
    moved = sum(4 * math.prod(shape) for shape in outputs) + sum(4 * math.prod(o.shape) for o in operands)
    return pl.pallas_call(
        kernel,
        out_shape=arrays,
        in_specs=places,
        out_specs=[pl.BlockSpec(memory_space=pltpu.VMEM)] * len(outputs),
        scratch_shapes=[pltpu.VMEM(shape, jnp.float32) for shape in scratch],
        compiler_params=pltpu.CompilerParams(vmem_limit_bytes=56 << 20),
        cost_estimate=pl.CostEstimate(flops=flops, bytes_accessed=moved, transcendentals=0),
    )(*operands)


def to_rows(cells):
    head = cells.shape[:-2]
    order = tuple(range(len(head)))
    split = cells.reshape(*head, 4, 2, 128).transpose(*order, len(head) + 1, len(head), len(head) + 2)
    return split.reshape(-1, 128)


def from_rows(rows, head):
    order = tuple(range(len(head)))
    split = rows.reshape(*head, 2, 4, 128).transpose(*order, len(head) + 1, len(head), len(head) + 2)
    return split.reshape(*head, 4, 256)


def mixed(table, states):
    table = np.asarray(table).astype(np.float32)
    return jnp.stack(
        [sum(float(table[i, k]) * states[k] for k in range(i + 1)) for i in range(POISSON)]
    )


def ring_states(states, own_even):
    near = [(0, 1), (1, 0), (2, 3), (3, 2)]
    far = [(1, 2), (2, 1), (3, 0), (0, 3)]
    upper = jnp.arange(8)[None, None, :, None] >= 4
    partner = lax.ppermute(states, "gz", near)
    first = upper == own_even
    nearer = jnp.where(first, partner, states)
    farther = jnp.where(first, states, partner)
    joined = nearer[:POISSON] + mixed(WHOLE_TABLE, farther[:POISSON])
    other = lax.ppermute(jnp.concatenate([joined, states[POISSON:]]), "gz", far)
    square = WHOLE_TABLE @ WHOLE_TABLE
    cube = square @ WHOLE_TABLE
    around = np.linalg.inv(np.eye(POISSON) - square @ square)
    entering = jnp.where(
        first[0],
        other[:POISSON] + mixed(square, partner[:POISSON]),
        partner[:POISSON] + mixed(WHOLE_TABLE, other[:POISSON]),
    )
    entering = entering + mixed(cube, states[:POISSON])
    entering = mixed(around, entering)
    ahead = jnp.where(own_even, partner[POISSON:], other[POISSON:])
    return jnp.concatenate([entering, ahead])


def fast_shards(factor, gain, base_flow, shift_index, sensor_cells):
    swap_in = [(0, 1), (1, 0), (2, 3), (3, 2), (4, 5), (5, 4), (6, 7), (7, 6)]
    swap_out = [(1, 2), (2, 1), (3, 4), (4, 3), (5, 6), (6, 5)]
    send_round = [(1, 2), (2, 1), (5, 6), (6, 5), (3, 7), (4, 0)]
    forward_round = [(7, 4), (0, 3)]
    near = [(0, 1), (1, 0), (2, 3), (3, 2)]
    far = [(1, 2), (2, 1), (3, 0), (0, 3)]
    odd = lax.axis_index("gx") % 2
    own_even = lax.axis_index("gz") % 2 == 0
    factor_rows = to_rows(factor)
    base_rows = to_rows(base_flow)
    gain_rows = to_rows(gain)
    cell = (8, 256)
    own, a, b1, b2, z1, z2 = call(
        pack_kernel,
        [(3, 4, HALF, *cell), (312, *cell), (PART, *cell), (312 - PART, *cell), (26, *cell), (26, *cell)],
        [], [factor_rows, base_rows], 0, 10**6,
    )
    b1_in = lax.ppermute(b1, "gx", send_round)
    z1 = lax.ppermute(z1, "gz", near)
    z2 = lax.ppermute(z2, "gz", far)
    b2_in = lax.ppermute(b2, "gx", swap_out)
    a_in = lax.ppermute(a, "gx", swap_in)
    corners = len(CORNERS) + 3
    ca, cb = call(corner_kernel, [(corners, *cell)] * 2, [], [z1, z2], 0, 10**5)
    ca = lax.ppermute(ca, "gx", swap_in)
    cb = lax.ppermute(cb, "gx", swap_out)
    b3_in = lax.ppermute(b1_in, "gx", forward_round)
    block = (10, 39, *cell)
    velocity, sides, states = call(
        velocity_kernel,
        [(3, 4, HALF, *cell), (5, HALF, *cell), (POISSON + 1, 5, *cell)],
        [(10, 80, 256)] + [block] * 5,
        [shift_index, own, base_rows, a_in, b1_in, b3_in, b2_in, ca, cb, z1, z2], 1, 10**8,
    )
    side_b = lax.ppermute(lax.dynamic_slice_in_dim(sides, odd, 4, axis=0), "gx", swap_out)
    side_a = lax.ppermute(lax.dynamic_slice_in_dim(sides, 1 - odd, 4, axis=0), "gx", swap_in)
    entering = ring_states(states, own_even)
    enter_b = lax.ppermute(lax.dynamic_slice_in_dim(entering, odd, 4, axis=1), "gx", swap_out)
    enter_a = lax.ppermute(lax.dynamic_slice_in_dim(entering, 1 - odd, 4, axis=1), "gx", swap_in)
    block = (11, HALF + 1, *cell)
    new_rows, solved, sums = call(
        pressure_kernel,
        [factor_rows.shape, factor_rows.shape, (1, 128)],
        [block, (POISSON + 1, 11, *cell), (POISSON, HALF + 1, *cell), (POISSON, *block), (32, 128)],
        [shift_index, sensor_cells, velocity, sides, side_a, side_b, entering, enter_a, enter_b, factor_rows],
        2, 10**8,
    )
    devices = lax.axis_size("gx") * lax.axis_size("gz")
    shared = lax.all_to_all(
        jnp.broadcast_to(sums[None], (devices, 1, 128)), ("gx", "gz"), split_axis=0, concat_axis=0, tiled=True
    )
    chunk = 768
    whole = pl.BlockSpec(memory_space=pltpu.SMEM)
    rows = pl.BlockSpec((chunk, 128), lambda i: (i, 0))
    new_gain, gram = pl.pallas_call(
        gain_kernel,
        grid=(gain_rows.shape[0] // chunk,),
        in_specs=[whole, pl.BlockSpec((devices, 128), lambda i: (0, 0)), rows, rows],
        out_specs=[rows, whole],
        out_shape=[
            jax.ShapeDtypeStruct(gain_rows.shape, jnp.float32),
            jax.ShapeDtypeStruct((4, 4), jnp.float32),
        ],
        scratch_shapes=[pltpu.SMEM((4, 4), jnp.float32)],
    )(shift_index, shared.reshape(devices, 128), gain_rows, solved)
    head = factor.shape[:3]
    return (from_rows(new_rows, head), from_rows(new_gain, head), gram)


def solution(mesh):
    placed = (
        P(None, "gz", None, "gx", None),
        P(None, "gz", None, "gx", None),
        P("gz", "gx", None),
        P(),
        P(),
    )
    fits = mesh.shape["gx"] == 8 and mesh.shape["gz"] == 4
    return jax.shard_map(
        fast_shards if fits else shards,
        mesh=mesh,
        in_specs=placed,
        out_specs=(P(None, "gz", None, "gx", None), P(None, "gz", None, "gx", None), P()),
        check_vma=False,
    )
```

```python
import math

import jax
import jax.numpy as jnp
import numpy as np
from jax import lax
from jax.experimental import pallas as pl
from jax.experimental.pallas import tpu as pltpu
from jax.sharding import PartitionSpec as P

SWEEPS = 3
POISSON = 4
SHIFTS = 8


viscosity = 0.4
shift_table = (0.6, 0.8, 1.0, 1.25, 1.6, 2.0, 2.5, 3.2)
chebyshev_weights = (1.0 / 1.9352976, 1.0 / 1.4752809, 1.0 / 0.8247191, 1.0 / 0.3647024)
highest = lax.Precision.HIGHEST


def padded_2(cells, sides, width, closed):
    for axis, dim in sides:
        count = lax.axis_size(axis)
        ends = count if closed else count - 1
        head = lax.slice_in_dim(cells, 0, width, axis=dim)
        tail = lax.slice_in_dim(cells, cells.shape[dim] - width, cells.shape[dim], axis=dim)
        cells = jnp.concatenate(
            [
                lax.ppermute(tail, axis, [(i, (i + 1) % count) for i in range(ends)]),
                cells,
                lax.ppermute(head, axis, [((i + 1) % count, i) for i in range(ends)]),
            ],
            axis=dim,
        )
    return cells


def around_sum(padded):
    summed = padded[:, 1:-1, :, 2:, 1:-1] + padded[:, 1:-1, :, :-2, 1:-1]
    summed = summed + padded[:, 1:-1, :, 1:-1, 2:] + padded[:, 1:-1, :, 1:-1, :-2]
    return summed + padded[:, 2:, :, 1:-1, 1:-1] + padded[:, :-2, :, 1:-1, 1:-1]


def shards(factor, gain, base_flow, shift_index, sensor_cells):
    components, span_cells, columns, stream_cells, normal_cells = factor.shape
    stream_start = lax.axis_index("gx") * stream_cells
    span_start = lax.axis_index("gz") * span_cells
    stream_total = stream_cells * lax.axis_size("gx")
    span_total = span_cells * lax.axis_size("gz")
    shift_values = jnp.asarray(shift_table, jnp.float32)
    shift_value = jnp.sum(jnp.where(jnp.arange(SHIFTS) == shift_index[0], shift_values, 0.0))
    base_field = base_flow[None, :, None, :, :]
    diagonal = shift_value + 6.0 * viscosity + base_field
    source = -factor

    def stream_inside(extent, margin):
        positions = stream_start - margin + jnp.arange(extent)
        return ((positions >= 0) & (positions < stream_total)).astype(jnp.float32)

    def extend(grid_field):
        padded = padded_2(grid_field, (("gx", 3), ("gz", 1)), 1, True)
        padded = padded * stream_inside(stream_cells + 2, 1)[None, None, None, :, None]
        return jnp.pad(padded, ((0, 0), (0, 0), (0, 0), (0, 0), (1, 1)))

    velocity = source / diagonal
    for sweep_index in range(SWEEPS):
        padded = extend(velocity)
        velocity = (
            source + viscosity * around_sum(padded) + base_field * padded[:, 1:-1, :, :-2, 1:-1]
        ) / diagonal
    padded = extend(velocity)
    divergence = 2.0 * (velocity[0] - padded[0, 1:-1, :, :-2, 1:-1])
    divergence = divergence + (velocity[1] - padded[1, 1:-1, :, 1:-1, :-2])
    divergence = divergence + (velocity[2] - padded[2, :-2, :, 1:-1, 1:-1])
    span_index = jnp.arange(span_total)
    products = span_index[:, None] * span_index[None, :] % span_total
    angles = 2.0 * math.pi * products.astype(jnp.float32) / span_total
    hartley_table = (jnp.cos(angles) + jnp.sin(angles)) / math.sqrt(span_total)

    def turn_modes(exchanged):
        turned = jnp.einsum("kz,zay->kay", hartley_table, exchanged, precision=highest)
        return lax.all_to_all(turned, "gz", split_axis=0, concat_axis=1, tiled=True)

    def transform(grid_field):
        flat = grid_field.reshape(span_cells, columns * stream_cells, normal_cells)
        result = turn_modes(lax.all_to_all(flat, "gz", split_axis=1, concat_axis=0, tiled=True))
        return result.reshape(span_cells, columns, stream_cells, normal_cells)

    modes_rhs = -transform(divergence)
    wave_index = span_start + jnp.arange(span_cells)
    wavenumber = 2.0 * math.pi * wave_index.astype(jnp.float32) / span_total
    mode_diagonal = (10.0 + (2.0 - 2.0 * jnp.cos(wavenumber)))[:, None, None, None]
    pressure = chebyshev_weights[0] * modes_rhs / mode_diagonal
    for sweep_level in range(1, POISSON):
        padded = padded_2(pressure, (("gx", 2),), 1, False)
        padded = jnp.pad(padded, ((0, 0), (0, 0), (0, 0), (1, 1)))
        beside_all = (
            4.0 * (padded[:, :, 2:, 1:-1] + padded[:, :, :-2, 1:-1])
            + padded[:, :, 1:-1, 2:]
            + padded[:, :, 1:-1, :-2]
        )
        pressure = (
            pressure
            + chebyshev_weights[sweep_level]
            * (modes_rhs - (mode_diagonal * pressure - beside_all))
            / mode_diagonal
        )
    pressure = transform(pressure)
    padded = extend(pressure[None])[0]
    gradient = jnp.stack(
        [
            2.0 * (padded[1:-1, :, 2:, 1:-1] - pressure),
            padded[1:-1, :, 1:-1, 2:] - pressure,
            padded[2:, :, 1:-1, 1:-1] - pressure,
        ]
    )
    solved = velocity - gradient
    span_ids = span_start + jnp.arange(span_cells)
    stream_ids = stream_start + jnp.arange(stream_cells)
    normal_ids = jnp.arange(normal_cells)
    located = span_ids[None, :, None, None] == sensor_cells[:, 1][:, None, None, None]
    located = located & (stream_ids[None, None, :, None] == sensor_cells[:, 2][:, None, None, None])
    located = located & (normal_ids[None, None, None, :] == sensor_cells[:, 3][:, None, None, None])
    picked = jnp.einsum("szxy,czjxy->scj", located.astype(jnp.float32), solved, precision=highest)
    chooser = (jnp.arange(3)[None, :] == sensor_cells[:, 0:1]).astype(jnp.float32)
    readout_local = jnp.sum(picked * chooser[:, :, None], axis=1)
    new_factor = factor + 2.0 * shift_value * solved
    gram_local = jnp.einsum("czixy,czjxy->ij", new_factor, new_factor, precision=highest)
    gram_total, readout = lax.psum((gram_local, readout_local), ("gx", "gz"))
    gram = gram_total / (3.0 * stream_total * normal_cells * span_total)
    new_gain = gain + 2.0 * shift_value * jnp.einsum(
        "czjxy,ij->czixy", solved, readout, precision=highest
    )
    return (new_factor, new_gain, gram)


HALF = 32
PAIRS = 8


def recurrence_tables(centre, weights):
    ratio = centre / 2.0 - math.sqrt(centre * centre / 4.0 - 1.0)
    order = len(weights)
    step = ratio * np.tril(np.ones((order, order)))
    half = np.linalg.matrix_power(step, HALF)
    whole = np.linalg.matrix_power(step, 2 * HALF)
    angles = 2.0 * np.pi * np.arange(4096) / 4096
    series = [weights[0]]
    for weight in weights[1:]:
        longer = [0.0] + [weight * entry for entry in series]
        for place, entry in enumerate(series):
            longer[place] += (1.0 - weight) * entry
        longer[0] += weight
        series = longer
    mixes = []
    for power in range(1, order + 1):
        symbol = 1.0 / (centre - 2.0 * np.cos(angles)) ** power
        kernel = [np.mean(symbol * np.cos(angles * n)) for n in range(order + 1)]
        matrix = [[math.comb(n + i - 1, i - 1) for i in range(1, power + 1)] for n in range(1, power + 1)]
        sides = np.linalg.solve(
            np.array(matrix, np.float64), [kernel[n] / ratio**n for n in range(1, power + 1)]
        )
        middle = kernel[0] - 2.0 * np.sum(sides)
        mixes.append([float(series[power - 1] * entry) for entry in [middle, *sides]])
    return float(ratio), half.tolist(), whole, mixes


RATIO, HALF_TABLE, WHOLE_TABLE, MIXES = recurrence_tables(12.0, chebyshev_weights)


def lower_half():
    return lax.broadcasted_iota(jnp.int32, (8, 256), 0) < 4


def swap(cells):
    return pltpu.roll(cells, 4, 0)


def below(cells):
    lanes = lax.broadcasted_iota(jnp.int32, (8, 128), 1)
    low, high = pltpu.roll(cells[:, :128], 1, 1), pltpu.roll(cells[:, 128:], 1, 1)
    return jnp.concatenate([jnp.where(lanes > 0, low, 0.0), jnp.where(lanes > 0, high, low)], axis=1)


def above(cells):
    lanes = lax.broadcasted_iota(jnp.int32, (8, 128), 1)
    low, high = pltpu.roll(cells[:, :128], 127, 1), pltpu.roll(cells[:, 128:], 127, 1)
    return jnp.concatenate([jnp.where(lanes < 127, low, high), jnp.where(lanes < 127, high, 0.0)], axis=1)


def either_side(cells):
    lanes = lax.broadcasted_iota(jnp.int32, (8, 128), 1)
    low, high = cells[:, :128], cells[:, 128:]
    low_up, high_up = pltpu.roll(low, 1, 1), pltpu.roll(high, 1, 1)
    low_down, high_down = pltpu.roll(low, 127, 1), pltpu.roll(high, 127, 1)
    first = jnp.where(lanes > 0, low_up, 0.0) + jnp.where(lanes < 127, low_down, high_down)
    second = jnp.where(lanes > 0, high_up, low_up) + jnp.where(lanes < 127, high_down, 0.0)
    return jnp.concatenate([first, second], axis=1)


def shift_of(index_ref):
    index = index_ref[0]
    value = jnp.float32(shift_table[0])
    for place in range(1, SHIFTS):
        value = jnp.where(index == place, jnp.float32(shift_table[place]), value)
    return value


def x_odd():
    return lax.rem(lax.axis_index("gx"), 2)


def z_even():
    return lax.rem(lax.axis_index("gz"), 2) == 0


def cascade(state, cells):
    grown = []
    for entry in state:
        cells = RATIO * entry + cells
        grown.append(cells)
    return tuple(grown)


def half_states(read):
    zero = jnp.zeros((8, 256), jnp.float32)

    def body(t, carry):
        forward, backward = carry
        return cascade(forward, read(t)), cascade(backward, read(HALF - 1 - t))

    return lax.fori_loop(0, HALF, body, ((zero,) * POISSON, (zero,) * POISSON), unroll=8)


def turned(table, states, row):
    total = None
    for column in range(row + 1):
        term = table[row][column] * states[column]
        total = term if total is None else total + term
    return total


FACTOR_AT = 24
PART = 152
CORNERS = [(c, dx, side, 0) for c in range(3) for dx in (1, 2) for side in (0, 1)]
CORNERS += [(2, 1, 0, 1), (2, 3, 0, 0)]


def pack_kernel(factor_ref, base_ref, own_ref, a_ref, b1_ref, b2_ref, z1_ref, z2_ref):
    odd = x_odd()
    even = 1 - odd
    low = lax.broadcasted_iota(jnp.int32, (8, 128), 0) < 4
    scale = -1.0 / viscosity
    for component in range(3):

        def load(m, _, component=component):
            for x in range(4):
                for tile in range(2):
                    row = (component * 64 + 2 * m) * 32 + tile * 4 + x
                    first = factor_ref[pl.ds(row, 8, stride=8), :] * scale
                    second = factor_ref[pl.ds(row + 1024, 8, stride=8), :] * scale
                    lanes = slice(tile * 128, tile * 128 + 128)
                    own_ref[component, x, 2 * m, :, lanes] = jnp.where(low, first, swap(second))
                    own_ref[component, x, 2 * m + 1, :, lanes] = jnp.where(low, swap(first), second)
            return 0

        lax.fori_loop(0, 16, load, 0)

    def edges(zz, _):
        for component in range(3):
            for layer in range(3):
                at = FACTOR_AT + (component * 3 + layer) * HALF
                a_ref[at + zz] = own_ref[component, layer + even, zz]
                cells = own_ref[component, layer + odd, zz]
                if at < PART:
                    b1_ref[at + zz] = cells
                else:
                    b2_ref[at - PART + zz] = cells
        return 0

    lax.fori_loop(0, HALF, edges, 0, unroll=2)
    for layer in range(3):
        for group in range(8):
            for tile in range(2):
                lanes = slice(tile * 128, tile * 128 + 128)
                row = group * 64 + tile * 4 + layer
                a_ref[layer * 8 + group, :, lanes] = base_ref[pl.ds(row + even, 8, stride=8), :]
                b1_ref[layer * 8 + group, :, lanes] = base_ref[pl.ds(row + odd, 8, stride=8), :]
    lower = lower_half()
    rightward = z_even()
    for component in range(3):
        for x in range(4):
            for pair in range(2):
                cells = lambda zz: own_ref[component, x, zz]
                up = jnp.where(lower, swap(cells(31 - 2 * pair)), cells(30 - 2 * pair))
                down = jnp.where(lower, cells(2 * pair), swap(cells(2 * pair + 1)))
                at = (component * 4 + x) * 2 + pair
                z1_ref[at] = jnp.where(rightward, up, down)
                z2_ref[at] = jnp.where(rightward, down, up)
    for k in range(4):
        for tile in range(2):
            lanes = slice(tile * 128, tile * 128 + 128)
            up = base_ref[(63 - k) * 8 + tile * 4 : (63 - k) * 8 + tile * 4 + 4, :]
            down = base_ref[k * 8 + tile * 4 : k * 8 + tile * 4 + 4, :]
            rows = slice((k % 2) * 4, (k % 2) * 4 + 4)
            z1_ref[24 + k // 2, rows, lanes] = jnp.where(rightward, up, down)
            z2_ref[24 + k // 2, rows, lanes] = jnp.where(rightward, down, up)


def corner_kernel(z1_ref, z2_ref, a_ref, b_ref):
    odd = x_odd()
    rightward = z_even()

    def fill(behind_ref, ahead_ref):
        for place, (component, dx, side, pair) in enumerate(CORNERS):
            source = (behind_ref, ahead_ref)[side]
            right_x = 4 - dx
            left_x = dx - 1
            a_x = jnp.where(odd == 1, left_x, right_x)
            b_x = jnp.where(odd == 1, right_x, left_x)
            a_ref[place] = source[(component * 4 + a_x) * 2 + pair]
            b_ref[place] = source[(component * 4 + b_x) * 2 + pair]
        for dx in (1, 2, 3):
            for k in range(4):
                for side, source in enumerate((behind_ref, ahead_ref)):
                    from_right = source[24 + k // 2, (k % 2) * 4 + 4 - dx, :]
                    from_left = source[24 + k // 2, (k % 2) * 4 + dx - 1, :]
                    at = len(CORNERS) + dx - 1
                    a_ref[at, side * 4 + k, :] = jnp.where(odd == 1, from_left, from_right)
                    b_ref[at, side * 4 + k, :] = jnp.where(odd == 1, from_right, from_left)

    @pl.when(rightward)
    def _():
        fill(z2_ref, z1_ref)

    @pl.when(jnp.logical_not(rightward))
    def _():
        fill(z1_ref, z2_ref)


def velocity_kernel(
    index_ref, own_ref, base_ref, a_ref, b1_ref, b3_ref, b2_ref, ca_ref, cb_ref, z1_ref, z2_ref,
    v_ref, bw_ref, s_ref,
    flow_ref, a1_ref, r_ref, v0_ref, va_ref, vb_ref,
):
    odd = x_odd()
    stream = lax.axis_index("gx")
    last = lax.axis_size("gx") - 1
    mask_left = jnp.where(stream > 0, 1.0, 0.0)
    mask_right = jnp.where(stream < last, 1.0, 0.0)
    relayed = jnp.logical_or(stream == 3, stream == 4)
    rightward = z_even()
    lower = lower_half()
    shift = shift_of(index_ref)

    def each_z(step):
        @pl.when(rightward)
        def _():
            step(z2_ref, z1_ref)

        @pl.when(jnp.logical_not(rightward))
        def _():
            step(z1_ref, z2_ref)

    def inside(at):
        return lambda zz: a_ref[at + zz]

    def outside(first_ref):
        def pick(at):
            if at < PART:
                return lambda zz: first_ref[at + zz]
            return lambda zz: b2_ref[at - PART + zz]

        return pick

    def each_x(step):
        @pl.when(jnp.logical_and(odd == 0, relayed))
        def _():
            step(outside(b3_ref), cb_ref, inside, ca_ref)

        @pl.when(jnp.logical_and(odd == 0, jnp.logical_not(relayed)))
        def _():
            step(outside(b1_ref), cb_ref, inside, ca_ref)

        @pl.when(jnp.logical_and(odd == 1, relayed))
        def _():
            step(inside, ca_ref, outside(b3_ref), cb_ref)

        @pl.when(jnp.logical_and(odd == 1, jnp.logical_not(relayed)))
        def _():
            step(inside, ca_ref, outside(b1_ref), cb_ref)

    for x in range(4):
        for group in range(8):
            for tile in range(2):
                lanes = slice(tile * 128, tile * 128 + 128)
                flow_ref[x + 3, 8 + 8 * group : 16 + 8 * group, lanes] = base_ref[
                    pl.ds(group * 64 + tile * 4 + x, 8, stride=8), :
                ]

    def flow_span(behind_ref, ahead_ref):
        for x in range(4):
            for k in range(4):
                at = 24 + k // 2
                row = (k % 2) * 4 + x
                flow_ref[x + 3, 7 - k, :] = behind_ref[at, row, :]
                flow_ref[x + 3, 72 + k, :] = ahead_ref[at, row, :]

    each_z(flow_span)

    def flow_stream(left, left_corner, right, right_corner):
        for dx in (1, 2, 3):
            for place, layer, read, corner in (
                (3 - dx, 3 - dx, left, left_corner),
                (6 + dx, dx - 1, right, right_corner),
            ):
                for group in range(8):
                    flow_ref[place, 8 + 8 * group : 16 + 8 * group, :] = read(layer * 8)(group)
                for k in range(4):
                    flow_ref[place, 7 - k, :] = corner[len(CORNERS) + dx - 1, k, :]
                    flow_ref[place, 72 + k, :] = corner[len(CORNERS) + dx - 1, 4 + k, :]

    each_x(flow_stream)

    def coefficients(zz, _):
        for x in range(10):
            first = jnp.broadcast_to(flow_ref[x, pl.ds(zz + 4, 1), :], (8, 256))
            second = jnp.broadcast_to(flow_ref[x, pl.ds(zz + 36, 1), :], (8, 256))
            flow = jnp.where(lower, first, second)
            scale = viscosity * (mask_left if x < 3 else mask_right if x > 6 else 1.0)
            a1_ref[x, zz] = scale / (shift + 6.0 * viscosity + flow)
            r_ref[x, zz] = 1.0 + flow * (1.0 / viscosity)
        return 0

    lax.fori_loop(0, 39, coefficients, 0, unroll=3)
    zero = jnp.zeros((8, 256), jnp.float32)
    for x in (0, 1, 2, 7, 8, 9):
        for zz in (0, 1, 2, 3, 36, 37, 38):
            v0_ref[x, zz] = zero

    def swept(source, zz, margin):
        layers = {x: source[x, zz] for x in range(2 - margin, 8 + margin)}
        result = {}
        for x in range(3 - margin, 7 + margin):
            centre = layers[x]
            total = layers[x + 1] + either_side(centre)
            total = total + (source[x, zz + 1] + source[x, zz - 1])
            result[x] = v0_ref[x, zz] + a1_ref[x, zz] * (total + r_ref[x, zz] * layers[x - 1])
        return result

    def sweep(source, target, margin):
        def body(zz, _):
            for x, cells in swept(source, zz, margin).items():
                target[x, zz] = cells
            return 0

        lax.fori_loop(3 - margin, 36 + margin, body, 0, unroll=6)

    for component in range(3):

        def interior(zz, _, component=component):
            for x in range(4):
                v0_ref[x + 3, zz + 4] = own_ref[component, x, zz] * a1_ref[x + 3, zz + 4]
            return 0

        lax.fori_loop(0, HALF, interior, 0, unroll=4)

        def before(cells, halo, k):
            if k % 2 == 0:
                return jnp.where(lower, halo, swap(cells))
            return swap(jnp.where(lower, cells, halo))

        def after(cells, halo, k):
            if k % 2 == 0:
                return swap(jnp.where(lower, halo, cells))
            return jnp.where(lower, swap(cells), halo)

        def span(behind_ref, ahead_ref, component=component):
            for x in range(4):
                at = (component * 4 + x) * 2
                for k in range(4):
                    cells = before(own_ref[component, x, 31 - k], behind_ref[at + k // 2], k)
                    v0_ref[x + 3, 3 - k] = cells * a1_ref[x + 3, 3 - k]
                for k in range(3):
                    cells = after(own_ref[component, x, k], ahead_ref[at + k // 2], k)
                    v0_ref[x + 3, 36 + k] = cells * a1_ref[x + 3, 36 + k]

        each_z(span)

        def sides(left, left_corner, right, right_corner, component=component):
            for dx in (1, 2, 3):
                for place, layer, pick, corner in (
                    (3 - dx, 3 - dx, left, left_corner),
                    (6 + dx, dx - 1, right, right_corner),
                ):
                    read = pick(FACTOR_AT + (component * 3 + layer) * HALF)

                    def body(zz, _, read=read, place=place):
                        v0_ref[place, zz + 4] = read(zz) * a1_ref[place, zz + 4]
                        return 0

                    lax.fori_loop(0, HALF, body, 0, unroll=4)
                    for entry, (c, away, side, pair) in enumerate(CORNERS):
                        if c != component or away != dx:
                            continue
                        for k in (2 * pair, 2 * pair + 1):
                            if side == 0:
                                cells = before(read(31 - k), corner[entry], k)
                                v0_ref[place, 3 - k] = cells * a1_ref[place, 3 - k]
                            else:
                                cells = after(read(k), corner[entry], k)
                                v0_ref[place, 36 + k] = cells * a1_ref[place, 36 + k]

        each_x(sides)
        sweep(v0_ref, va_ref, 2)
        sweep(va_ref, vb_ref, 1)

        def diverge(zz, before, component=component):
            cells = [swept(vb_ref, zz + 4, 0)[x + 3] for x in range(4)]
            for x in range(4):
                v_ref[component, x, zz] = cells[x]
                if component == 0:
                    bw_ref[x, zz] = -2.0 * (cells[x] if x == 0 else cells[x] - cells[x - 1])
                elif component == 1:
                    bw_ref[x, zz] = bw_ref[x, zz] - (cells[x] - below(cells[x]))
                else:
                    bw_ref[x, zz] = bw_ref[x, zz] - (cells[x] - before[x])
            if component == 0:
                bw_ref[4, zz] = cells[3]
            return tuple(cells) if component == 2 else 0

        start = 0
        if component == 2:
            start = tuple(swept(vb_ref, 3, 0)[x + 3] for x in range(4))
        lax.fori_loop(0, HALF, diverge, start, unroll=4)

    def states(layer, _):
        forward, backward = half_states(lambda t: bw_ref[layer, t])
        swapped_forward = [swap(entry) for entry in forward]
        swapped_backward = [swap(entry) for entry in backward]
        for i in range(POISSON):
            onward = forward[i] + turned(HALF_TABLE, swapped_forward, i)
            back = backward[i] + turned(HALF_TABLE, swapped_backward, i)
            s_ref[i, layer] = jnp.where(lower, back, onward)
        s_ref[POISSON, layer] = bw_ref[layer, 0]
        return 0

    lax.fori_loop(0, 5, states, 0)


def pressure_kernel(
    index_ref, cells_ref, v_ref, bw_ref, ba_ref, bb_ref, inc_ref, ia_ref, ib_ref, factor_ref,
    nf_ref, solved_ref, sums_ref,
    f_ref, i_ref, u_ref, q_ref, t_ref,
):
    odd = x_odd()
    stream = lax.axis_index("gx")
    span = lax.axis_index("gz")
    last = lax.axis_size("gx") - 1
    mask_left = jnp.where(stream > 0, 1.0, 0.0)
    mask_right = jnp.where(stream < last, 1.0, 0.0)
    lower = lower_half()
    shift = shift_of(index_ref)

    def gather(left_ref, right_ref, left_inc, right_inc):
        def body(zz, _):
            for x in range(3):
                f_ref[x, zz] = left_ref[x, zz]
                f_ref[x + 4, zz] = bw_ref[x + 1, zz]
                f_ref[x + 8, zz] = right_ref[x + 1, zz]
            f_ref[3, zz] = bw_ref[0, zz] + 2.0 * left_ref[3, zz]
            f_ref[7, zz] = mask_right * (right_ref[0, zz] + 2.0 * bw_ref[4, zz])
            return 0

        lax.fori_loop(0, HALF, body, 0)
        for i in range(POISSON + 1):
            for x in range(3):
                i_ref[i, x] = left_inc[i, x]
                i_ref[i, x + 4] = inc_ref[i, x + 1]
                i_ref[i, x + 8] = right_inc[i, x + 1]
            i_ref[i, 3] = inc_ref[i, 0] + 2.0 * left_inc[i, 3]
            i_ref[i, 7] = mask_right * (right_inc[i, 0] + 2.0 * inc_ref[i, 4])
        for x in range(11):
            f_ref[x, HALF] = swap(jnp.where(lower, i_ref[POISSON, x], f_ref[x, 0]))

    @pl.when(odd == 0)
    def _():
        gather(bb_ref, ba_ref, ib_ref, ia_ref)

    @pl.when(odd == 1)
    def _():
        gather(ba_ref, bb_ref, ia_ref, ib_ref)

    def solve(x, _):
        forward, backward = half_states(lambda t: f_ref[x, t])
        arriving = [i_ref[i, x] for i in range(POISSON)]
        swapped = [swap(entry) for entry in arriving]
        onward = []
        back = []
        for i in range(POISSON):
            carried = turned(HALF_TABLE, swapped, i)
            onward.append(swap(jnp.where(lower, forward[i] + carried, arriving[i])))
            back.append(swap(jnp.where(lower, arriving[i], backward[i] + carried)))

        def ahead(zz, state):
            state = cascade(state, f_ref[x, zz])
            for i in range(POISSON):
                u_ref[i, zz] = state[i]
            return state

        lax.fori_loop(0, HALF, ahead, tuple(onward), unroll=8)
        end = cascade([u_ref[i, HALF - 1] for i in range(POISSON)], f_ref[x, HALF])
        for i in range(POISSON):
            u_ref[i, HALF] = end[i]

        def mix(zz, state):
            both = [f_ref[x, zz]] + [u_ref[i, zz] + state[i] for i in range(POISSON)]
            for power in range(POISSON):
                total = MIXES[power][0] * both[0]
                for i in range(1, power + 2):
                    total = total + MIXES[power][i] * both[i]
                q_ref[power, x, zz] = total

        mix(HALF, back)

        def behind(t, state):
            zz = HALF - 1 - t
            state = cascade(state, f_ref[x, zz])
            mix(zz, state)
            return state

        lax.fori_loop(0, HALF, behind, tuple(back), unroll=8)
        return 0

    lax.fori_loop(0, 11, solve, 0)
    for power in (2, 1, 0):

        def apply(zz, _, power=power):
            edge = 2 - power
            layers = {x: q_ref[power + 1, x, zz] for x in range(edge, 11 - edge)}
            for x in range(edge + 1, 10 - edge if power else 8):
                beside = 4.0 * (layers[x - 1] + layers[x + 1]) + either_side(layers[x])
                if x < 3:
                    beside = mask_left * beside
                if x > 6:
                    beside = mask_right * beside
                q_ref[power, x, zz] = q_ref[power, x, zz] + beside
            return 0

        lax.fori_loop(0, HALF + 1, apply, 0, unroll=3)

    def correct(m, _):
        for x in range(4):
            pair = []
            for zz in (2 * m, 2 * m + 1):
                centre = q_ref[0, x + 3, zz]
                pair.append(
                    (
                        v_ref[0, x, zz] - 2.0 * (q_ref[0, x + 4, zz] - centre),
                        v_ref[1, x, zz] - (above(centre) - centre),
                        v_ref[2, x, zz] - (q_ref[0, x + 3, zz + 1] - centre),
                    )
                )
            for component in range(3):
                first, second = pair[0][component], pair[1][component]
                early = jnp.where(lower, first, swap(second))
                late = jnp.where(lower, swap(first), second)
                for tile in range(2):
                    row = (component * 64 + 2 * m) * 32 + tile * 4 + x
                    lanes = slice(tile * 128, tile * 128 + 128)
                    solved_ref[pl.ds(row, 8, stride=8), :] = early[:, lanes]
                    solved_ref[pl.ds(row + 1024, 8, stride=8), :] = late[:, lanes]
        return 0

    lax.fori_loop(0, 16, correct, 0, unroll=2)
    couples = [(i, j) for i in range(4) for j in range(i, 4)]

    def update(block, sums):
        columns = []
        for i in range(4):
            rows = pl.ds(pl.multiple_of(block * 32 + 8 * i, 8), 8)
            cells = factor_ref[rows, :] + (2.0 * shift) * solved_ref[rows, :]
            nf_ref[rows, :] = cells
            columns.append(cells)
        return tuple(s + columns[i] * columns[j] for s, (i, j) in zip(sums, couples))

    zero = jnp.zeros((8, 128), jnp.float32)
    sums = lax.fori_loop(0, 192, update, (zero,) * len(couples), unroll=4)
    t_ref[...] = jnp.zeros((32, 128), jnp.float32)
    for total, (i, j) in zip(sums, couples):
        t_ref[4 * i + j : 4 * i + j + 1, :] = jnp.sum(total, axis=0, keepdims=True)
    lanes = lax.broadcasted_iota(jnp.int32, (1, 128), 1)
    for sensor in range(4):
        component = cells_ref[sensor, 0]
        z = cells_ref[sensor, 1] - span * 64
        x = cells_ref[sensor, 2] - stream * 4
        y = cells_ref[sensor, 3]
        held = (z >= 0) & (z < 64) & (x >= 0) & (x < 4)
        z = jnp.clip(z, 0, 63)
        x = jnp.clip(x, 0, 3)
        tile = jnp.where(y >= 128, 1, 0)
        lane = jnp.where(held, y - 128 * tile, -1)
        for column in range(4):
            row = (component * 64 + z) * 32 + column * 8 + tile * 4 + x
            cells = solved_ref[pl.ds(row, 1), :]
            at = 16 + 4 * sensor + column
            t_ref[at : at + 1, :] = jnp.where(lanes == lane, cells, 0.0)
    totals = jnp.sum(t_ref[...], axis=1, keepdims=True)
    spread = lax.broadcasted_iota(jnp.int32, (32, 128), 1) == lax.broadcasted_iota(jnp.int32, (32, 128), 0)
    sums_ref[...] = jnp.sum(jnp.where(spread, totals, 0.0), axis=0, keepdims=True)


def gain_kernel(index_ref, sums_ref, gain_ref, solved_ref, out_ref, gram_ref, c_ref):
    @pl.when(pl.program_id(0) == 0)
    def _():
        totals = jnp.sum(sums_ref[...], axis=0, keepdims=True)
        lanes = lax.broadcasted_iota(jnp.int32, (1, 128), 1)
        shift = shift_of(index_ref)
        for i in range(4):
            for j in range(4):
                c_ref[i, j] = 2.0 * shift * jnp.sum(jnp.where(lanes == 16 + 4 * i + j, totals, 0.0))
                at = 4 * min(i, j) + max(i, j)
                gram_ref[i, j] = jnp.sum(jnp.where(lanes == at, totals, 0.0)) / 6291456.0

    table = [[c_ref[i, j] for j in range(4)] for i in range(4)]

    def body(block, _):
        rows = [pl.ds(pl.multiple_of(block * 32 + 8 * j, 8), 8) for j in range(4)]
        columns = [solved_ref[rows[j], :] for j in range(4)]
        for i in range(4):
            total = gain_ref[rows[i], :]
            for j in range(4):
                total = total + table[i][j] * columns[j]
            out_ref[rows[i], :] = total
        return 0

    lax.fori_loop(0, out_ref.shape[0] // 32, body, 0, unroll=2)


def call(kernel, outputs, scratch, operands, smalls, flops):
    arrays = [jax.ShapeDtypeStruct(shape, jnp.float32) for shape in outputs]
    places = [pl.BlockSpec(memory_space=pltpu.SMEM)] * smalls
    places += [pl.BlockSpec(memory_space=pltpu.VMEM)] * (len(operands) - smalls)
    moved = sum(4 * math.prod(shape) for shape in outputs) + sum(4 * math.prod(o.shape) for o in operands)
    return pl.pallas_call(
        kernel,
        out_shape=arrays,
        in_specs=places,
        out_specs=[pl.BlockSpec(memory_space=pltpu.VMEM)] * len(outputs),
        scratch_shapes=[pltpu.VMEM(shape, jnp.float32) for shape in scratch],
        compiler_params=pltpu.CompilerParams(vmem_limit_bytes=26 << 20),
        cost_estimate=pl.CostEstimate(flops=flops, bytes_accessed=moved, transcendentals=0),
    )(*operands)


def to_rows(cells):
    head = cells.shape[:-2]
    order = tuple(range(len(head)))
    split = cells.reshape(*head, 4, 2, 128).transpose(*order, len(head) + 1, len(head), len(head) + 2)
    return split.reshape(-1, 128)


def from_rows(rows, head):
    order = tuple(range(len(head)))
    split = rows.reshape(*head, 2, 4, 128).transpose(*order, len(head) + 1, len(head), len(head) + 2)
    return split.reshape(*head, 4, 256)


def mixed(table, states):
    table = np.asarray(table).astype(np.float32)
    return jnp.stack(
        [sum(float(table[i, k]) * states[k] for k in range(i + 1)) for i in range(POISSON)]
    )


def ring_states(states, own_even):
    near = [(0, 1), (1, 0), (2, 3), (3, 2)]
    far = [(1, 2), (2, 1), (3, 0), (0, 3)]
    upper = jnp.arange(8)[None, None, :, None] >= 4
    partner = lax.ppermute(states, "gz", near)
    first = upper == own_even
    nearer = jnp.where(first, partner, states)
    farther = jnp.where(first, states, partner)
    joined = nearer[:POISSON] + mixed(WHOLE_TABLE, farther[:POISSON])
    other = lax.ppermute(jnp.concatenate([joined, states[POISSON:]]), "gz", far)
    square = WHOLE_TABLE @ WHOLE_TABLE
    cube = square @ WHOLE_TABLE
    around = np.linalg.inv(np.eye(POISSON) - square @ square)
    entering = jnp.where(
        first[0],
        other[:POISSON] + mixed(square, partner[:POISSON]),
        partner[:POISSON] + mixed(WHOLE_TABLE, other[:POISSON]),
    )
    entering = entering + mixed(cube, states[:POISSON])
    entering = mixed(around, entering)
    ahead = jnp.where(own_even, partner[POISSON:], other[POISSON:])
    return jnp.concatenate([entering, ahead])


def fast_shards(factor, gain, base_flow, shift_index, sensor_cells):
    swap_in = [(0, 1), (1, 0), (2, 3), (3, 2), (4, 5), (5, 4), (6, 7), (7, 6)]
    swap_out = [(1, 2), (2, 1), (3, 4), (4, 3), (5, 6), (6, 5)]
    send_round = [(1, 2), (2, 1), (5, 6), (6, 5), (3, 7), (4, 0)]
    forward_round = [(7, 4), (0, 3)]
    near = [(0, 1), (1, 0), (2, 3), (3, 2)]
    far = [(1, 2), (2, 1), (3, 0), (0, 3)]
    odd = lax.axis_index("gx") % 2
    own_even = lax.axis_index("gz") % 2 == 0
    factor_rows = to_rows(factor)
    base_rows = to_rows(base_flow)
    gain_rows = to_rows(gain)
    cell = (8, 256)
    own, a, b1, b2, z1, z2 = call(
        pack_kernel,
        [(3, 4, HALF, *cell), (312, *cell), (PART, *cell), (312 - PART, *cell), (26, *cell), (26, *cell)],
        [], [factor_rows, base_rows], 0, 10**6,
    )
    b1_in = lax.ppermute(b1, "gx", send_round)
    z1 = lax.ppermute(z1, "gz", near)
    z2 = lax.ppermute(z2, "gz", far)
    b2_in = lax.ppermute(b2, "gx", swap_out)
    a_in = lax.ppermute(a, "gx", swap_in)
    corners = len(CORNERS) + 3
    ca, cb = call(corner_kernel, [(corners, *cell)] * 2, [], [z1, z2], 0, 10**5)
    ca = lax.ppermute(ca, "gx", swap_in)
    cb = lax.ppermute(cb, "gx", swap_out)
    b3_in = lax.ppermute(b1_in, "gx", forward_round)
    block = (10, 39, *cell)
    velocity, sides, states = call(
        velocity_kernel,
        [(3, 4, HALF, *cell), (5, HALF, *cell), (POISSON + 1, 5, *cell)],
        [(10, 80, 256)] + [block] * 5,
        [shift_index, own, base_rows, a_in, b1_in, b3_in, b2_in, ca, cb, z1, z2], 1, 10**8,
    )
    side_b = lax.ppermute(lax.dynamic_slice_in_dim(sides, odd, 4, axis=0), "gx", swap_out)
    side_a = lax.ppermute(lax.dynamic_slice_in_dim(sides, 1 - odd, 4, axis=0), "gx", swap_in)
    entering = ring_states(states, own_even)
    enter_b = lax.ppermute(lax.dynamic_slice_in_dim(entering, odd, 4, axis=1), "gx", swap_out)
    enter_a = lax.ppermute(lax.dynamic_slice_in_dim(entering, 1 - odd, 4, axis=1), "gx", swap_in)
    block = (11, HALF + 1, *cell)
    new_rows, solved, sums = call(
        pressure_kernel,
        [factor_rows.shape, factor_rows.shape, (1, 128)],
        [block, (POISSON + 1, 11, *cell), (POISSON, HALF + 1, *cell), (POISSON, *block), (32, 128)],
        [shift_index, sensor_cells, velocity, sides, side_a, side_b, entering, enter_a, enter_b, factor_rows],
        2, 10**8,
    )
    devices = lax.axis_size("gx") * lax.axis_size("gz")
    shared = lax.all_to_all(
        jnp.broadcast_to(sums[None], (devices, 1, 128)), ("gx", "gz"), split_axis=0, concat_axis=0, tiled=True
    )
    chunk = 768
    whole = pl.BlockSpec(memory_space=pltpu.SMEM)
    rows = pl.BlockSpec((chunk, 128), lambda i: (i, 0))
    new_gain, gram = pl.pallas_call(
        gain_kernel,
        grid=(gain_rows.shape[0] // chunk,),
        in_specs=[whole, pl.BlockSpec((devices, 128), lambda i: (0, 0)), rows, rows],
        out_specs=[rows, whole],
        out_shape=[
            jax.ShapeDtypeStruct(gain_rows.shape, jnp.float32),
            jax.ShapeDtypeStruct((4, 4), jnp.float32),
        ],
        scratch_shapes=[pltpu.SMEM((4, 4), jnp.float32)],
    )(shift_index, shared.reshape(devices, 128), gain_rows, solved)
    head = factor.shape[:3]
    return (from_rows(new_rows, head), from_rows(new_gain, head), gram)


def solution(mesh):
    placed = (
        P(None, "gz", None, "gx", None),
        P(None, "gz", None, "gx", None),
        P("gz", "gx", None),
        P(),
        P(),
    )
    fits = mesh.shape["gx"] == 8 and mesh.shape["gz"] == 4
    return jax.shard_map(
        fast_shards if fits else shards,
        mesh=mesh,
        in_specs=placed,
        out_specs=(P(None, "gz", None, "gx", None), P(None, "gz", None, "gx", None), P()),
        check_vma=False,
    )
```

```python
import math

import jax
import jax.numpy as jnp
import numpy as np
from jax import lax
from jax.experimental import pallas as pl
from jax.experimental.pallas import tpu as pltpu
from jax.sharding import PartitionSpec as P

SWEEPS = 3
POISSON = 4
SHIFTS = 8


viscosity = 0.4
shift_table = (0.6, 0.8, 1.0, 1.25, 1.6, 2.0, 2.5, 3.2)
chebyshev_weights = (1.0 / 1.9352976, 1.0 / 1.4752809, 1.0 / 0.8247191, 1.0 / 0.3647024)
highest = lax.Precision.HIGHEST


def padded_2(cells, sides, width, closed):
    for axis, dim in sides:
        count = lax.axis_size(axis)
        ends = count if closed else count - 1
        head = lax.slice_in_dim(cells, 0, width, axis=dim)
        tail = lax.slice_in_dim(cells, cells.shape[dim] - width, cells.shape[dim], axis=dim)
        cells = jnp.concatenate(
            [
                lax.ppermute(tail, axis, [(i, (i + 1) % count) for i in range(ends)]),
                cells,
                lax.ppermute(head, axis, [((i + 1) % count, i) for i in range(ends)]),
            ],
            axis=dim,
        )
    return cells


def around_sum(padded):
    summed = padded[:, 1:-1, :, 2:, 1:-1] + padded[:, 1:-1, :, :-2, 1:-1]
    summed = summed + padded[:, 1:-1, :, 1:-1, 2:] + padded[:, 1:-1, :, 1:-1, :-2]
    return summed + padded[:, 2:, :, 1:-1, 1:-1] + padded[:, :-2, :, 1:-1, 1:-1]


def shards(factor, gain, base_flow, shift_index, sensor_cells):
    components, span_cells, columns, stream_cells, normal_cells = factor.shape
    stream_start = lax.axis_index("gx") * stream_cells
    span_start = lax.axis_index("gz") * span_cells
    stream_total = stream_cells * lax.axis_size("gx")
    span_total = span_cells * lax.axis_size("gz")
    shift_values = jnp.asarray(shift_table, jnp.float32)
    shift_value = jnp.sum(jnp.where(jnp.arange(SHIFTS) == shift_index[0], shift_values, 0.0))
    base_field = base_flow[None, :, None, :, :]
    diagonal = shift_value + 6.0 * viscosity + base_field
    source = -factor

    def stream_inside(extent, margin):
        positions = stream_start - margin + jnp.arange(extent)
        return ((positions >= 0) & (positions < stream_total)).astype(jnp.float32)

    def extend(grid_field):
        padded = padded_2(grid_field, (("gx", 3), ("gz", 1)), 1, True)
        padded = padded * stream_inside(stream_cells + 2, 1)[None, None, None, :, None]
        return jnp.pad(padded, ((0, 0), (0, 0), (0, 0), (0, 0), (1, 1)))

    velocity = source / diagonal
    for sweep_index in range(SWEEPS):
        padded = extend(velocity)
        velocity = (
            source + viscosity * around_sum(padded) + base_field * padded[:, 1:-1, :, :-2, 1:-1]
        ) / diagonal
    padded = extend(velocity)
    divergence = 2.0 * (velocity[0] - padded[0, 1:-1, :, :-2, 1:-1])
    divergence = divergence + (velocity[1] - padded[1, 1:-1, :, 1:-1, :-2])
    divergence = divergence + (velocity[2] - padded[2, :-2, :, 1:-1, 1:-1])
    span_index = jnp.arange(span_total)
    products = span_index[:, None] * span_index[None, :] % span_total
    angles = 2.0 * math.pi * products.astype(jnp.float32) / span_total
    hartley_table = (jnp.cos(angles) + jnp.sin(angles)) / math.sqrt(span_total)

    def turn_modes(exchanged):
        turned = jnp.einsum("kz,zay->kay", hartley_table, exchanged, precision=highest)
        return lax.all_to_all(turned, "gz", split_axis=0, concat_axis=1, tiled=True)

    def transform(grid_field):
        flat = grid_field.reshape(span_cells, columns * stream_cells, normal_cells)
        result = turn_modes(lax.all_to_all(flat, "gz", split_axis=1, concat_axis=0, tiled=True))
        return result.reshape(span_cells, columns, stream_cells, normal_cells)

    modes_rhs = -transform(divergence)
    wave_index = span_start + jnp.arange(span_cells)
    wavenumber = 2.0 * math.pi * wave_index.astype(jnp.float32) / span_total
    mode_diagonal = (10.0 + (2.0 - 2.0 * jnp.cos(wavenumber)))[:, None, None, None]
    pressure = chebyshev_weights[0] * modes_rhs / mode_diagonal
    for sweep_level in range(1, POISSON):
        padded = padded_2(pressure, (("gx", 2),), 1, False)
        padded = jnp.pad(padded, ((0, 0), (0, 0), (0, 0), (1, 1)))
        beside_all = (
            4.0 * (padded[:, :, 2:, 1:-1] + padded[:, :, :-2, 1:-1])
            + padded[:, :, 1:-1, 2:]
            + padded[:, :, 1:-1, :-2]
        )
        pressure = (
            pressure
            + chebyshev_weights[sweep_level]
            * (modes_rhs - (mode_diagonal * pressure - beside_all))
            / mode_diagonal
        )
    pressure = transform(pressure)
    padded = extend(pressure[None])[0]
    gradient = jnp.stack(
        [
            2.0 * (padded[1:-1, :, 2:, 1:-1] - pressure),
            padded[1:-1, :, 1:-1, 2:] - pressure,
            padded[2:, :, 1:-1, 1:-1] - pressure,
        ]
    )
    solved = velocity - gradient
    span_ids = span_start + jnp.arange(span_cells)
    stream_ids = stream_start + jnp.arange(stream_cells)
    normal_ids = jnp.arange(normal_cells)
    located = span_ids[None, :, None, None] == sensor_cells[:, 1][:, None, None, None]
    located = located & (stream_ids[None, None, :, None] == sensor_cells[:, 2][:, None, None, None])
    located = located & (normal_ids[None, None, None, :] == sensor_cells[:, 3][:, None, None, None])
    picked = jnp.einsum("szxy,czjxy->scj", located.astype(jnp.float32), solved, precision=highest)
    chooser = (jnp.arange(3)[None, :] == sensor_cells[:, 0:1]).astype(jnp.float32)
    readout_local = jnp.sum(picked * chooser[:, :, None], axis=1)
    new_factor = factor + 2.0 * shift_value * solved
    gram_local = jnp.einsum("czixy,czjxy->ij", new_factor, new_factor, precision=highest)
    gram_total, readout = lax.psum((gram_local, readout_local), ("gx", "gz"))
    gram = gram_total / (3.0 * stream_total * normal_cells * span_total)
    new_gain = gain + 2.0 * shift_value * jnp.einsum(
        "czjxy,ij->czixy", solved, readout, precision=highest
    )
    return (new_factor, new_gain, gram)


HALF = 32
PAIRS = 8


def recurrence_tables(centre, weights):
    ratio = centre / 2.0 - math.sqrt(centre * centre / 4.0 - 1.0)
    order = len(weights)
    step = ratio * np.tril(np.ones((order, order)))
    half = np.linalg.matrix_power(step, HALF)
    whole = np.linalg.matrix_power(step, 2 * HALF)
    angles = 2.0 * np.pi * np.arange(4096) / 4096
    series = [weights[0]]
    for weight in weights[1:]:
        longer = [0.0] + [weight * entry for entry in series]
        for place, entry in enumerate(series):
            longer[place] += (1.0 - weight) * entry
        longer[0] += weight
        series = longer
    mixes = []
    for power in range(1, order + 1):
        symbol = 1.0 / (centre - 2.0 * np.cos(angles)) ** power
        kernel = [np.mean(symbol * np.cos(angles * n)) for n in range(order + 1)]
        matrix = [[math.comb(n + i - 1, i - 1) for i in range(1, power + 1)] for n in range(1, power + 1)]
        sides = np.linalg.solve(
            np.array(matrix, np.float64), [kernel[n] / ratio**n for n in range(1, power + 1)]
        )
        middle = kernel[0] - 2.0 * np.sum(sides)
        mixes.append([float(series[power - 1] * entry) for entry in [middle, *sides]])
    return float(ratio), half.tolist(), whole, mixes


RATIO, HALF_TABLE, WHOLE_TABLE, MIXES = recurrence_tables(12.0, chebyshev_weights)


def lower_half():
    return lax.broadcasted_iota(jnp.int32, (8, 256), 0) < 4


def swap(cells):
    return pltpu.roll(cells, 4, 0)


def below(cells):
    lanes = lax.broadcasted_iota(jnp.int32, (8, 128), 1)
    low, high = pltpu.roll(cells[:, :128], 1, 1), pltpu.roll(cells[:, 128:], 1, 1)
    return jnp.concatenate([jnp.where(lanes > 0, low, 0.0), jnp.where(lanes > 0, high, low)], axis=1)


def above(cells):
    lanes = lax.broadcasted_iota(jnp.int32, (8, 128), 1)
    low, high = pltpu.roll(cells[:, :128], 127, 1), pltpu.roll(cells[:, 128:], 127, 1)
    return jnp.concatenate([jnp.where(lanes < 127, low, high), jnp.where(lanes < 127, high, 0.0)], axis=1)


def either_side(cells):
    lanes = lax.broadcasted_iota(jnp.int32, (8, 128), 1)
    low, high = cells[:, :128], cells[:, 128:]
    low_up, high_up = pltpu.roll(low, 1, 1), pltpu.roll(high, 1, 1)
    low_down, high_down = pltpu.roll(low, 127, 1), pltpu.roll(high, 127, 1)
    first = jnp.where(lanes > 0, low_up, 0.0) + jnp.where(lanes < 127, low_down, high_down)
    second = jnp.where(lanes > 0, high_up, low_up) + jnp.where(lanes < 127, high_down, 0.0)
    return jnp.concatenate([first, second], axis=1)


def shift_of(index_ref):
    index = index_ref[0]
    value = jnp.float32(shift_table[0])
    for place in range(1, SHIFTS):
        value = jnp.where(index == place, jnp.float32(shift_table[place]), value)
    return value


def x_odd():
    return lax.rem(lax.axis_index("gx"), 2)


def z_even():
    return lax.rem(lax.axis_index("gz"), 2) == 0


def cascade(state, cells):
    grown = []
    for entry in state:
        cells = RATIO * entry + cells
        grown.append(cells)
    return tuple(grown)


def half_states(read):
    zero = jnp.zeros((8, 256), jnp.float32)

    def body(t, carry):
        forward, backward = carry
        return cascade(forward, read(t)), cascade(backward, read(HALF - 1 - t))

    return lax.fori_loop(0, HALF, body, ((zero,) * POISSON, (zero,) * POISSON), unroll=8)


def turned(table, states, row):
    total = None
    for column in range(row + 1):
        term = table[row][column] * states[column]
        total = term if total is None else total + term
    return total


FACTOR_AT = 24
PART = 152
CORNERS = [(c, dx, side, 0) for c in range(3) for dx in (1, 2) for side in (0, 1)]
CORNERS += [(2, 1, 0, 1), (2, 3, 0, 0)]


def pack_kernel(factor_hbm, base_ref, own_ref, a_ref, b1_ref, b2_ref, z1_ref, z2_ref, factor_ref, arrived):
    share = factor_ref.shape[0] // 3
    copies = []
    for component in range(3):
        rows = pl.ds(component * share, share)
        copies.append(
            pltpu.make_async_copy(factor_hbm.at[rows], factor_ref.at[rows], arrived.at[component])
        )
        copies[-1].start()
    odd = x_odd()
    even = 1 - odd
    low = lax.broadcasted_iota(jnp.int32, (8, 128), 0) < 4
    scale = -1.0 / viscosity
    for component in range(3):

        def load(m, _, component=component):
            for x in range(4):
                for tile in range(2):
                    row = (component * 64 + 2 * m) * 32 + tile * 4 + x
                    first = factor_ref[pl.ds(row, 8, stride=8), :] * scale
                    second = factor_ref[pl.ds(row + 1024, 8, stride=8), :] * scale
                    lanes = slice(tile * 128, tile * 128 + 128)
                    own_ref[component, x, 2 * m, :, lanes] = jnp.where(low, first, swap(second))
                    own_ref[component, x, 2 * m + 1, :, lanes] = jnp.where(low, swap(first), second)
            return 0

        copies[component].wait()
        lax.fori_loop(0, 16, load, 0, unroll=2)

    def edges(zz, _):
        for component in range(3):
            for layer in range(3):
                at = FACTOR_AT + (component * 3 + layer) * HALF
                a_ref[at + zz] = own_ref[component, layer + even, zz]
                cells = own_ref[component, layer + odd, zz]
                if at < PART:
                    b1_ref[at + zz] = cells
                else:
                    b2_ref[at - PART + zz] = cells
        return 0

    lax.fori_loop(0, HALF, edges, 0, unroll=2)
    for layer in range(3):
        for group in range(8):
            for tile in range(2):
                lanes = slice(tile * 128, tile * 128 + 128)
                row = group * 64 + tile * 4 + layer
                a_ref[layer * 8 + group, :, lanes] = base_ref[pl.ds(row + even, 8, stride=8), :]
                b1_ref[layer * 8 + group, :, lanes] = base_ref[pl.ds(row + odd, 8, stride=8), :]
    lower = lower_half()
    rightward = z_even()
    for component in range(3):
        for x in range(4):
            for pair in range(2):
                cells = lambda zz: own_ref[component, x, zz]
                up = jnp.where(lower, swap(cells(31 - 2 * pair)), cells(30 - 2 * pair))
                down = jnp.where(lower, cells(2 * pair), swap(cells(2 * pair + 1)))
                at = (component * 4 + x) * 2 + pair
                z1_ref[at] = jnp.where(rightward, up, down)
                z2_ref[at] = jnp.where(rightward, down, up)
    for k in range(4):
        for tile in range(2):
            lanes = slice(tile * 128, tile * 128 + 128)
            up = base_ref[(63 - k) * 8 + tile * 4 : (63 - k) * 8 + tile * 4 + 4, :]
            down = base_ref[k * 8 + tile * 4 : k * 8 + tile * 4 + 4, :]
            rows = slice((k % 2) * 4, (k % 2) * 4 + 4)
            z1_ref[24 + k // 2, rows, lanes] = jnp.where(rightward, up, down)
            z2_ref[24 + k // 2, rows, lanes] = jnp.where(rightward, down, up)


def corner_kernel(z1_ref, z2_ref, a_ref, b_ref):
    odd = x_odd()
    rightward = z_even()

    def fill(behind_ref, ahead_ref):
        for place, (component, dx, side, pair) in enumerate(CORNERS):
            source = (behind_ref, ahead_ref)[side]
            right_x = 4 - dx
            left_x = dx - 1
            a_x = jnp.where(odd == 1, left_x, right_x)
            b_x = jnp.where(odd == 1, right_x, left_x)
            a_ref[place] = source[(component * 4 + a_x) * 2 + pair]
            b_ref[place] = source[(component * 4 + b_x) * 2 + pair]
        for dx in (1, 2, 3):
            for k in range(4):
                for side, source in enumerate((behind_ref, ahead_ref)):
                    from_right = source[24 + k // 2, (k % 2) * 4 + 4 - dx, :]
                    from_left = source[24 + k // 2, (k % 2) * 4 + dx - 1, :]
                    at = len(CORNERS) + dx - 1
                    a_ref[at, side * 4 + k, :] = jnp.where(odd == 1, from_left, from_right)
                    b_ref[at, side * 4 + k, :] = jnp.where(odd == 1, from_right, from_left)

    @pl.when(rightward)
    def _():
        fill(z2_ref, z1_ref)

    @pl.when(jnp.logical_not(rightward))
    def _():
        fill(z1_ref, z2_ref)


def velocity_kernel(
    index_ref, own_ref, base_ref, a_ref, b1_ref, b3_ref, b2_ref, ca_ref, cb_ref, z1_ref, z2_ref,
    v_ref, bw_ref, s_ref, pa_ref, pb1_ref, pb2_ref,
    flow_ref, a1_ref, r_ref, v0_ref, va_ref, vb_ref,
):
    odd = x_odd()
    stream = lax.axis_index("gx")
    last = lax.axis_size("gx") - 1
    mask_left = jnp.where(stream > 0, 1.0, 0.0)
    mask_right = jnp.where(stream < last, 1.0, 0.0)
    relayed = jnp.logical_or(stream == 3, stream == 4)
    rightward = z_even()
    lower = lower_half()
    shift = shift_of(index_ref)

    def each_z(step):
        @pl.when(rightward)
        def _():
            step(z2_ref, z1_ref)

        @pl.when(jnp.logical_not(rightward))
        def _():
            step(z1_ref, z2_ref)

    def inside(at):
        return lambda zz: a_ref[at + zz]

    def outside(first_ref):
        def pick(at):
            if at < PART:
                return lambda zz: first_ref[at + zz]
            return lambda zz: b2_ref[at - PART + zz]

        return pick

    def each_x(step):
        @pl.when(jnp.logical_and(odd == 0, relayed))
        def _():
            step(outside(b3_ref), cb_ref, inside, ca_ref)

        @pl.when(jnp.logical_and(odd == 0, jnp.logical_not(relayed)))
        def _():
            step(outside(b1_ref), cb_ref, inside, ca_ref)

        @pl.when(jnp.logical_and(odd == 1, relayed))
        def _():
            step(inside, ca_ref, outside(b3_ref), cb_ref)

        @pl.when(jnp.logical_and(odd == 1, jnp.logical_not(relayed)))
        def _():
            step(inside, ca_ref, outside(b1_ref), cb_ref)

    for x in range(4):
        for group in range(8):
            for tile in range(2):
                lanes = slice(tile * 128, tile * 128 + 128)
                flow_ref[x + 3, 8 + 8 * group : 16 + 8 * group, lanes] = base_ref[
                    pl.ds(group * 64 + tile * 4 + x, 8, stride=8), :
                ]

    def flow_span(behind_ref, ahead_ref):
        for x in range(4):
            for k in range(4):
                at = 24 + k // 2
                row = (k % 2) * 4 + x
                flow_ref[x + 3, 7 - k, :] = behind_ref[at, row, :]
                flow_ref[x + 3, 72 + k, :] = ahead_ref[at, row, :]

    each_z(flow_span)

    def flow_stream(left, left_corner, right, right_corner):
        for dx in (1, 2, 3):
            for place, layer, read, corner in (
                (3 - dx, 3 - dx, left, left_corner),
                (6 + dx, dx - 1, right, right_corner),
            ):
                for group in range(8):
                    flow_ref[place, 8 + 8 * group : 16 + 8 * group, :] = read(layer * 8)(group)
                for k in range(4):
                    flow_ref[place, 7 - k, :] = corner[len(CORNERS) + dx - 1, k, :]
                    flow_ref[place, 72 + k, :] = corner[len(CORNERS) + dx - 1, 4 + k, :]

    each_x(flow_stream)

    def coefficients(zz, _):
        for x in range(10):
            first = jnp.broadcast_to(flow_ref[x, pl.ds(zz + 4, 1), :], (8, 256))
            second = jnp.broadcast_to(flow_ref[x, pl.ds(zz + 36, 1), :], (8, 256))
            flow = jnp.where(lower, first, second)
            scale = viscosity * (mask_left if x < 3 else mask_right if x > 6 else 1.0)
            a1_ref[x, zz] = scale / (shift + 6.0 * viscosity + flow)
            r_ref[x, zz] = 1.0 + flow * (1.0 / viscosity)
        return 0

    lax.fori_loop(0, 39, coefficients, 0, unroll=3)
    zero = jnp.zeros((8, 256), jnp.float32)
    for x in (0, 1, 2, 7, 8, 9):
        for zz in (0, 1, 2, 3, 36, 37, 38):
            v0_ref[x, zz] = zero

    def swept(source, zz, margin):
        layers = {x: source[x, zz] for x in range(2 - margin, 8 + margin)}
        result = {}
        for x in range(3 - margin, 7 + margin):
            centre = layers[x]
            total = layers[x + 1] + either_side(centre)
            total = total + (source[x, zz + 1] + source[x, zz - 1])
            result[x] = v0_ref[x, zz] + a1_ref[x, zz] * (total + r_ref[x, zz] * layers[x - 1])
        return result

    def sweep(source, target, margin):
        def body(zz, _):
            for x, cells in swept(source, zz, margin).items():
                target[x, zz] = cells
            return 0

        lax.fori_loop(3 - margin, 36 + margin, body, 0, unroll=6)

    for component in range(3):

        def interior(zz, _, component=component):
            for x in range(4):
                v0_ref[x + 3, zz + 4] = own_ref[component, x, zz] * a1_ref[x + 3, zz + 4]
            return 0

        lax.fori_loop(0, HALF, interior, 0, unroll=4)

        def before(cells, halo, k):
            if k % 2 == 0:
                return jnp.where(lower, halo, swap(cells))
            return swap(jnp.where(lower, cells, halo))

        def after(cells, halo, k):
            if k % 2 == 0:
                return swap(jnp.where(lower, halo, cells))
            return jnp.where(lower, swap(cells), halo)

        def span(behind_ref, ahead_ref, component=component):
            for x in range(4):
                at = (component * 4 + x) * 2
                for k in range(4):
                    cells = before(own_ref[component, x, 31 - k], behind_ref[at + k // 2], k)
                    v0_ref[x + 3, 3 - k] = cells * a1_ref[x + 3, 3 - k]
                for k in range(3):
                    cells = after(own_ref[component, x, k], ahead_ref[at + k // 2], k)
                    v0_ref[x + 3, 36 + k] = cells * a1_ref[x + 3, 36 + k]

        each_z(span)

        def sides(left, left_corner, right, right_corner, component=component):
            for dx in (1, 2, 3):
                for place, layer, pick, corner in (
                    (3 - dx, 3 - dx, left, left_corner),
                    (6 + dx, dx - 1, right, right_corner),
                ):
                    read = pick(FACTOR_AT + (component * 3 + layer) * HALF)

                    def body(zz, _, read=read, place=place):
                        v0_ref[place, zz + 4] = read(zz) * a1_ref[place, zz + 4]
                        return 0

                    lax.fori_loop(0, HALF, body, 0, unroll=4)
                    for entry, (c, away, side, pair) in enumerate(CORNERS):
                        if c != component or away != dx:
                            continue
                        for k in (2 * pair, 2 * pair + 1):
                            if side == 0:
                                cells = before(read(31 - k), corner[entry], k)
                                v0_ref[place, 3 - k] = cells * a1_ref[place, 3 - k]
                            else:
                                cells = after(read(k), corner[entry], k)
                                v0_ref[place, 36 + k] = cells * a1_ref[place, 36 + k]

        each_x(sides)
        sweep(v0_ref, va_ref, 2)
        sweep(va_ref, vb_ref, 1)

        def diverge(zz, before, component=component):
            cells = [swept(vb_ref, zz + 4, 0)[x + 3] for x in range(4)]
            for x in range(4):
                v_ref[component, x, zz] = cells[x]
                if component == 0:
                    bw_ref[x, zz] = -2.0 * (cells[x] if x == 0 else cells[x] - cells[x - 1])
                elif component == 1:
                    bw_ref[x, zz] = bw_ref[x, zz] - (cells[x] - below(cells[x]))
                else:
                    bw_ref[x, zz] = bw_ref[x, zz] - (cells[x] - before[x])
            if component == 0:
                bw_ref[4, zz] = cells[3]
            return tuple(cells) if component == 2 else 0

        start = 0
        if component == 2:
            start = tuple(swept(vb_ref, 3, 0)[x + 3] for x in range(4))
        lax.fori_loop(0, HALF, diverge, start, unroll=4)

    even = 1 - odd

    def edges(zz, _):
        for layer in range(4):
            pa_ref[layer, zz] = bw_ref[layer + even, zz]
            (pb1_ref if layer < 2 else pb2_ref)[layer % 2, zz] = bw_ref[layer + odd, zz]
        return 0

    lax.fori_loop(0, HALF, edges, 0, unroll=4)

    def states(layer, _):
        forward, backward = half_states(lambda t: bw_ref[layer, t])
        swapped_forward = [swap(entry) for entry in forward]
        swapped_backward = [swap(entry) for entry in backward]
        for i in range(POISSON):
            onward = forward[i] + turned(HALF_TABLE, swapped_forward, i)
            back = backward[i] + turned(HALF_TABLE, swapped_backward, i)
            s_ref[i, layer] = jnp.where(lower, back, onward)
        s_ref[POISSON, layer] = bw_ref[layer, 0]
        return 0

    lax.fori_loop(0, 5, states, 0)


def pressure_kernel(
    index_ref, cells_ref, v_ref, bw_ref, ba_ref, b1_ref, b3_ref, b2_ref, inc_ref, ia_ref, ib_ref, factor_ref,
    nf_hbm, solved_ref, sums_ref,
    f_ref, i_ref, u_ref, q_ref, t_ref, nf_ref, sent,
):
    odd = x_odd()
    stream = lax.axis_index("gx")
    span = lax.axis_index("gz")
    last = lax.axis_size("gx") - 1
    mask_left = jnp.where(stream > 0, 1.0, 0.0)
    mask_right = jnp.where(stream < last, 1.0, 0.0)
    lower = lower_half()
    shift = shift_of(index_ref)

    def gather(left, right, left_inc, right_inc):
        def body(zz, _):
            for x in range(3):
                f_ref[x, zz] = mask_left * left(x, zz)
                f_ref[x + 4, zz] = bw_ref[x + 1, zz]
                f_ref[x + 8, zz] = mask_right * right(x + 1, zz)
            f_ref[3, zz] = bw_ref[0, zz] + (2.0 * mask_left) * left(3, zz)
            f_ref[7, zz] = mask_right * (right(0, zz) + 2.0 * bw_ref[4, zz])
            return 0

        lax.fori_loop(0, HALF, body, 0, unroll=4)
        for i in range(POISSON + 1):
            for x in range(3):
                i_ref[i, x] = left_inc[i, x]
                i_ref[i, x + 4] = inc_ref[i, x + 1]
                i_ref[i, x + 8] = right_inc[i, x + 1]
            i_ref[i, 3] = inc_ref[i, 0] + 2.0 * left_inc[i, 3]
            i_ref[i, 7] = mask_right * (right_inc[i, 0] + 2.0 * inc_ref[i, 4])
        for x in range(11):
            f_ref[x, HALF] = swap(jnp.where(lower, i_ref[POISSON, x], f_ref[x, 0]))

    def inside(layer, zz):
        return ba_ref[layer, zz]

    def direct(layer, zz):
        return b1_ref[layer, zz] if layer < 2 else b2_ref[layer - 2, zz]

    def relayed(layer, zz):
        return b3_ref[layer, zz] if layer < 2 else b2_ref[layer - 2, zz]

    middle = jnp.logical_or(stream == 3, stream == 4)
    for parity in (0, 1):
        for through, outside in ((False, direct), (True, relayed)):

            @pl.when(jnp.logical_and(odd == parity, middle == through))
            def _(parity=parity, outside=outside):
                if parity == 0:
                    gather(outside, inside, ib_ref, ia_ref)
                else:
                    gather(inside, outside, ia_ref, ib_ref)

    def solve(x, _):
        forward, backward = half_states(lambda t: f_ref[x, t])
        arriving = [i_ref[i, x] for i in range(POISSON)]
        swapped = [swap(entry) for entry in arriving]
        onward = []
        back = []
        for i in range(POISSON):
            carried = turned(HALF_TABLE, swapped, i)
            onward.append(swap(jnp.where(lower, forward[i] + carried, arriving[i])))
            back.append(swap(jnp.where(lower, arriving[i], backward[i] + carried)))

        def ahead(zz, state):
            state = cascade(state, f_ref[x, zz])
            for i in range(POISSON):
                u_ref[i, zz] = state[i]
            return state

        lax.fori_loop(0, HALF, ahead, tuple(onward), unroll=8)
        end = cascade([u_ref[i, HALF - 1] for i in range(POISSON)], f_ref[x, HALF])
        for i in range(POISSON):
            u_ref[i, HALF] = end[i]

        def mix(zz, state):
            both = [f_ref[x, zz]] + [u_ref[i, zz] + state[i] for i in range(POISSON)]
            for power in range(POISSON):
                total = MIXES[power][0] * both[0]
                for i in range(1, power + 2):
                    total = total + MIXES[power][i] * both[i]
                q_ref[power, x, zz] = total

        mix(HALF, back)

        def behind(t, state):
            zz = HALF - 1 - t
            state = cascade(state, f_ref[x, zz])
            mix(zz, state)
            return state

        lax.fori_loop(0, HALF, behind, tuple(back), unroll=8)
        return 0

    lax.fori_loop(0, 11, solve, 0)
    for power in (2, 1, 0):

        def apply(zz, _, power=power):
            edge = 2 - power
            layers = {x: q_ref[power + 1, x, zz] for x in range(edge, 11 - edge)}
            for x in range(edge + 1, 10 - edge if power else 8):
                beside = 4.0 * (layers[x - 1] + layers[x + 1]) + either_side(layers[x])
                if x < 3:
                    beside = mask_left * beside
                if x > 6:
                    beside = mask_right * beside
                q_ref[power, x, zz] = q_ref[power, x, zz] + beside
            return 0

        lax.fori_loop(0, HALF + 1, apply, 0, unroll=3)

    def correct(m, _):
        for x in range(4):
            pair = []
            for zz in (2 * m, 2 * m + 1):
                centre = q_ref[0, x + 3, zz]
                pair.append(
                    (
                        v_ref[0, x, zz] - 2.0 * (q_ref[0, x + 4, zz] - centre),
                        v_ref[1, x, zz] - (above(centre) - centre),
                        v_ref[2, x, zz] - (q_ref[0, x + 3, zz + 1] - centre),
                    )
                )
            for component in range(3):
                first, second = pair[0][component], pair[1][component]
                early = jnp.where(lower, first, swap(second))
                late = jnp.where(lower, swap(first), second)
                for tile in range(2):
                    row = (component * 64 + 2 * m) * 32 + tile * 4 + x
                    lanes = slice(tile * 128, tile * 128 + 128)
                    solved_ref[pl.ds(row, 8, stride=8), :] = early[:, lanes]
                    solved_ref[pl.ds(row + 1024, 8, stride=8), :] = late[:, lanes]
        return 0

    lax.fori_loop(0, 16, correct, 0, unroll=2)
    couples = [(i, j) for i in range(4) for j in range(i, 4)]

    def update(block, sums):
        columns = []
        for i in range(4):
            rows = pl.ds(pl.multiple_of(block * 32 + 8 * i, 8), 8)
            cells = factor_ref[rows, :] + (2.0 * shift) * solved_ref[rows, :]
            nf_ref[rows, :] = cells
            columns.append(cells)
        return tuple(s + columns[i] * columns[j] for s, (i, j) in zip(sums, couples))

    sums = (jnp.zeros((8, 128), jnp.float32),) * len(couples)
    copies = []
    for part in range(4):
        sums = lax.fori_loop(part * 48, part * 48 + 48, update, sums, unroll=4)
        rows = pl.ds(part * 1536, 1536)
        copies.append(pltpu.make_async_copy(nf_ref.at[rows], nf_hbm.at[rows], sent.at[part]))
        copies[-1].start()
    t_ref[...] = jnp.zeros((32, 128), jnp.float32)
    for total, (i, j) in zip(sums, couples):
        t_ref[4 * i + j : 4 * i + j + 1, :] = jnp.sum(total, axis=0, keepdims=True)
    lanes = lax.broadcasted_iota(jnp.int32, (1, 128), 1)
    for sensor in range(4):
        component = cells_ref[sensor, 0]
        z = cells_ref[sensor, 1] - span * 64
        x = cells_ref[sensor, 2] - stream * 4
        y = cells_ref[sensor, 3]
        held = (z >= 0) & (z < 64) & (x >= 0) & (x < 4)
        z = jnp.clip(z, 0, 63)
        x = jnp.clip(x, 0, 3)
        tile = jnp.where(y >= 128, 1, 0)
        lane = jnp.where(held, y - 128 * tile, -1)
        for column in range(4):
            row = (component * 64 + z) * 32 + column * 8 + tile * 4 + x
            cells = solved_ref[pl.ds(row, 1), :]
            at = 16 + 4 * sensor + column
            t_ref[at : at + 1, :] = jnp.where(lanes == lane, cells, 0.0)
    totals = jnp.sum(t_ref[...], axis=1, keepdims=True)
    spread = lax.broadcasted_iota(jnp.int32, (32, 128), 1) == lax.broadcasted_iota(jnp.int32, (32, 128), 0)
    sums_ref[...] = jnp.sum(jnp.where(spread, totals, 0.0), axis=0, keepdims=True)
    for copy in copies:
        copy.wait()


def gain_kernel(index_ref, sums_ref, gain_ref, solved_ref, out_hbm, gram_ref, out_ref, sent):
    totals = jnp.sum(sums_ref[...], axis=0, keepdims=True)
    lanes = lax.broadcasted_iota(jnp.int32, (1, 128), 1)
    shift = shift_of(index_ref)

    def entry(at):
        return jnp.sum(jnp.where(lanes == at, totals, 0.0), axis=1, keepdims=True)

    table = [
        [jnp.broadcast_to(2.0 * shift * entry(16 + 4 * i + j), (8, 128)) for j in range(4)] for i in range(4)
    ]

    def body(block, _):
        rows = [pl.ds(pl.multiple_of(block * 32 + 8 * j, 8), 8) for j in range(4)]
        columns = [solved_ref[rows[j], :] for j in range(4)]
        for i in range(4):
            total = gain_ref[rows[i], :]
            for j in range(4):
                total = total + table[i][j] * columns[j]
            out_ref[rows[i], :] = total
        return 0

    copies = []
    for part in range(6):
        lax.fori_loop(part * 32, part * 32 + 32, body, 0, unroll=4)
        rows = pl.ds(part * 1024, 1024)
        copies.append(pltpu.make_async_copy(out_ref.at[rows], out_hbm.at[rows], sent.at[part]))
        copies[-1].start()
    row = lax.broadcasted_iota(jnp.int32, (4, 4), 0)
    column = lax.broadcasted_iota(jnp.int32, (4, 4), 1)
    gram = jnp.zeros((4, 4), jnp.float32)
    for i in range(4):
        for j in range(4):
            value = entry(4 * min(i, j) + max(i, j)) / 6291456.0
            gram = gram + jnp.where((row == i) & (column == j), value, 0.0)
    gram_ref[...] = gram
    for copy in copies:
        copy.wait()


def call(kernel, outputs, scratch, operands, smalls, flops, far_in=(), far_out=(), signals=(), least=0):
    arrays = [jax.ShapeDtypeStruct(shape, jnp.float32) for shape in outputs]
    places = [pl.BlockSpec(memory_space=pltpu.SMEM)] * smalls
    places += [pl.BlockSpec(memory_space=pltpu.VMEM)] * (len(operands) - smalls)
    results = [pl.BlockSpec(memory_space=pltpu.VMEM)] * len(outputs)
    for place in far_in:
        places[place] = pl.BlockSpec(memory_space=pltpu.HBM)
    for place in far_out:
        results[place] = pl.BlockSpec(memory_space=pltpu.HBM)
    room = sum(4 * math.prod(shape) for shape in scratch) + (2 << 20)
    moved = sum(4 * math.prod(shape) for shape in outputs) + sum(4 * math.prod(o.shape) for o in operands)
    return pl.pallas_call(
        kernel,
        out_shape=arrays,
        in_specs=places,
        out_specs=results,
        scratch_shapes=[pltpu.VMEM(shape, jnp.float32) for shape in scratch]
        + [pltpu.SemaphoreType.DMA((count,)) for count in signals],
        compiler_params=pltpu.CompilerParams(vmem_limit_bytes=26 << 20),
        cost_estimate=pl.CostEstimate(flops=flops, bytes_accessed=moved, transcendentals=0),
    )(*operands)


def to_rows(cells):
    head = cells.shape[:-2]
    order = tuple(range(len(head)))
    split = cells.reshape(*head, 4, 2, 128).transpose(*order, len(head) + 1, len(head), len(head) + 2)
    return split.reshape(-1, 128)


def from_rows(rows, head):
    order = tuple(range(len(head)))
    split = rows.reshape(*head, 2, 4, 128).transpose(*order, len(head) + 1, len(head), len(head) + 2)
    return split.reshape(*head, 4, 256)


def mixed(table, states):
    table = np.asarray(table).astype(np.float32)
    return jnp.stack(
        [sum(float(table[i, k]) * states[k] for k in range(i + 1)) for i in range(POISSON)]
    )


def ring_states(states, partner, own_even, far):
    upper = jnp.arange(8)[None, None, :, None] >= 4
    first = upper == own_even
    nearer = jnp.where(first, partner, states)
    farther = jnp.where(first, states, partner)
    joined = nearer[:POISSON] + mixed(WHOLE_TABLE, farther[:POISSON])
    other = lax.ppermute(jnp.concatenate([joined, states[POISSON:]]), "gz", far)
    square = WHOLE_TABLE @ WHOLE_TABLE
    cube = square @ WHOLE_TABLE
    around = np.linalg.inv(np.eye(POISSON) - square @ square)
    entering = jnp.where(
        first[0],
        other[:POISSON] + mixed(square, partner[:POISSON]),
        partner[:POISSON] + mixed(WHOLE_TABLE, other[:POISSON]),
    )
    entering = entering + mixed(cube, states[:POISSON])
    entering = mixed(around, entering)
    ahead = jnp.where(own_even, partner[POISSON:], other[POISSON:])
    return jnp.concatenate([entering, ahead])


def fast_shards(factor, gain, base_flow, shift_index, sensor_cells):
    swap_in = [(0, 1), (1, 0), (2, 3), (3, 2), (4, 5), (5, 4), (6, 7), (7, 6)]
    swap_out = [(1, 2), (2, 1), (3, 4), (4, 3), (5, 6), (6, 5)]
    send_round = [(1, 2), (2, 1), (5, 6), (6, 5), (3, 7), (4, 0)]
    forward_round = [(7, 4), (0, 3)]
    near = [(0, 1), (1, 0), (2, 3), (3, 2)]
    far = [(1, 2), (2, 1), (3, 0), (0, 3)]
    odd = lax.axis_index("gx") % 2
    own_even = lax.axis_index("gz") % 2 == 0
    factor_rows = to_rows(factor)
    base_rows = to_rows(base_flow)
    gain_rows = to_rows(gain)
    cell = (8, 256)
    own, a, b1, b2, z1, z2 = call(
        pack_kernel,
        [(3, 4, HALF, *cell), (312, *cell), (PART, *cell), (312 - PART, *cell), (26, *cell), (26, *cell)],
        [factor_rows.shape], [factor_rows, base_rows], 0, 10**6, far_in=(0,), signals=(3,),
    )
    b1_in = lax.ppermute(b1, "gx", send_round)
    z1 = lax.ppermute(z1, "gz", near)
    z2 = lax.ppermute(z2, "gz", far)
    b2_in = lax.ppermute(b2, "gx", swap_out)
    a_in = lax.ppermute(a, "gx", swap_in)
    corners = len(CORNERS) + 3
    ca, cb = call(corner_kernel, [(corners, *cell)] * 2, [], [z1, z2], 0, 10**5)
    ca = lax.ppermute(ca, "gx", swap_in)
    cb = lax.ppermute(cb, "gx", swap_out)
    b1_in, z1, z2 = lax.optimization_barrier((b1_in, z1, z2))
    b3_in = lax.ppermute(b1_in, "gx", forward_round)
    block = (10, 39, *cell)
    velocity, sides, states, pa, pb1, pb2 = call(
        velocity_kernel,
        [(3, 4, HALF, *cell), (5, HALF, *cell), (POISSON + 1, 5, *cell), (4, HALF, *cell)]
        + [(2, HALF, *cell)] * 2,
        [(10, 80, 256)] + [block] * 5,
        [shift_index, own, base_rows, a_in, b1_in, b3_in, b2_in, ca, cb, z1, z2], 1, 10**8,
    )
    pb1_in = lax.ppermute(pb1, "gx", send_round)
    pb2_in = lax.ppermute(pb2, "gx", swap_out)
    partner = lax.ppermute(states, "gz", near)
    pb1_in, partner = lax.optimization_barrier((pb1_in, partner))
    pa_in = lax.ppermute(pa, "gx", swap_in)
    pb3_in = lax.ppermute(pb1_in, "gx", forward_round)
    entering = ring_states(states, partner, own_even, far)
    enter_b = lax.ppermute(lax.dynamic_slice_in_dim(entering, odd, 4, axis=1), "gx", swap_out)
    enter_a = lax.ppermute(lax.dynamic_slice_in_dim(entering, 1 - odd, 4, axis=1), "gx", swap_in)
    block = (11, HALF + 1, *cell)
    new_rows, solved, sums = call(
        pressure_kernel,
        [factor_rows.shape, factor_rows.shape, (1, 128)],
        [block, (POISSON + 1, 11, *cell), (POISSON, HALF + 1, *cell), (POISSON, *block), (32, 128)]
        + [factor_rows.shape],
        [shift_index, sensor_cells, velocity, sides, pa_in, pb1_in, pb3_in, pb2_in]
        + [entering, enter_a, enter_b, factor_rows],
        2, 10**8, far_out=(0,), signals=(4,),
    )
    devices = lax.axis_size("gx") * lax.axis_size("gz")
    shared = lax.all_to_all(
        jnp.broadcast_to(sums[None], (devices, 1, 128)), ("gx", "gz"), split_axis=0, concat_axis=0, tiled=True
    )
    new_gain, gram = call(
        gain_kernel,
        [gain_rows.shape, (4, 4)],
        [gain_rows.shape], [shift_index, shared.reshape(devices, 128), gain_rows, solved], 1, 10**7,
        far_out=(0,), signals=(6,),
    )
    head = factor.shape[:3]
    return (from_rows(new_rows, head), from_rows(new_gain, head), gram)


def solution(mesh):
    placed = (
        P(None, "gz", None, "gx", None),
        P(None, "gz", None, "gx", None),
        P("gz", "gx", None),
        P(),
        P(),
    )
    fits = mesh.shape["gx"] == 8 and mesh.shape["gz"] == 4
    return jax.shard_map(
        fast_shards if fits else shards,
        mesh=mesh,
        in_specs=placed,
        out_specs=(P(None, "gz", None, "gx", None), P(None, "gz", None, "gx", None), P()),
        check_vma=False,
    )
```

```python
import math

import jax
import jax.numpy as jnp
import numpy as np
from jax import lax
from jax.experimental import pallas as pl
from jax.experimental.pallas import tpu as pltpu
from jax.sharding import PartitionSpec as P

SWEEPS = 3
POISSON = 4
SHIFTS = 8


viscosity = 0.4
shift_table = (0.6, 0.8, 1.0, 1.25, 1.6, 2.0, 2.5, 3.2)
chebyshev_weights = (1.0 / 1.9352976, 1.0 / 1.4752809, 1.0 / 0.8247191, 1.0 / 0.3647024)
highest = lax.Precision.HIGHEST


def padded_2(cells, sides, width, closed):
    for axis, dim in sides:
        count = lax.axis_size(axis)
        ends = count if closed else count - 1
        head = lax.slice_in_dim(cells, 0, width, axis=dim)
        tail = lax.slice_in_dim(cells, cells.shape[dim] - width, cells.shape[dim], axis=dim)
        cells = jnp.concatenate(
            [
                lax.ppermute(tail, axis, [(i, (i + 1) % count) for i in range(ends)]),
                cells,
                lax.ppermute(head, axis, [((i + 1) % count, i) for i in range(ends)]),
            ],
            axis=dim,
        )
    return cells


def around_sum(padded):
    summed = padded[:, 1:-1, :, 2:, 1:-1] + padded[:, 1:-1, :, :-2, 1:-1]
    summed = summed + padded[:, 1:-1, :, 1:-1, 2:] + padded[:, 1:-1, :, 1:-1, :-2]
    return summed + padded[:, 2:, :, 1:-1, 1:-1] + padded[:, :-2, :, 1:-1, 1:-1]


def shards(factor, gain, base_flow, shift_index, sensor_cells):
    components, span_cells, columns, stream_cells, normal_cells = factor.shape
    stream_start = lax.axis_index("gx") * stream_cells
    span_start = lax.axis_index("gz") * span_cells
    stream_total = stream_cells * lax.axis_size("gx")
    span_total = span_cells * lax.axis_size("gz")
    shift_values = jnp.asarray(shift_table, jnp.float32)
    shift_value = jnp.sum(jnp.where(jnp.arange(SHIFTS) == shift_index[0], shift_values, 0.0))
    base_field = base_flow[None, :, None, :, :]
    diagonal = shift_value + 6.0 * viscosity + base_field
    source = -factor

    def stream_inside(extent, margin):
        positions = stream_start - margin + jnp.arange(extent)
        return ((positions >= 0) & (positions < stream_total)).astype(jnp.float32)

    def extend(grid_field):
        padded = padded_2(grid_field, (("gx", 3), ("gz", 1)), 1, True)
        padded = padded * stream_inside(stream_cells + 2, 1)[None, None, None, :, None]
        return jnp.pad(padded, ((0, 0), (0, 0), (0, 0), (0, 0), (1, 1)))

    velocity = source / diagonal
    for sweep_index in range(SWEEPS):
        padded = extend(velocity)
        velocity = (
            source + viscosity * around_sum(padded) + base_field * padded[:, 1:-1, :, :-2, 1:-1]
        ) / diagonal
    padded = extend(velocity)
    divergence = 2.0 * (velocity[0] - padded[0, 1:-1, :, :-2, 1:-1])
    divergence = divergence + (velocity[1] - padded[1, 1:-1, :, 1:-1, :-2])
    divergence = divergence + (velocity[2] - padded[2, :-2, :, 1:-1, 1:-1])
    span_index = jnp.arange(span_total)
    products = span_index[:, None] * span_index[None, :] % span_total
    angles = 2.0 * math.pi * products.astype(jnp.float32) / span_total
    hartley_table = (jnp.cos(angles) + jnp.sin(angles)) / math.sqrt(span_total)

    def turn_modes(exchanged):
        turned = jnp.einsum("kz,zay->kay", hartley_table, exchanged, precision=highest)
        return lax.all_to_all(turned, "gz", split_axis=0, concat_axis=1, tiled=True)

    def transform(grid_field):
        flat = grid_field.reshape(span_cells, columns * stream_cells, normal_cells)
        result = turn_modes(lax.all_to_all(flat, "gz", split_axis=1, concat_axis=0, tiled=True))
        return result.reshape(span_cells, columns, stream_cells, normal_cells)

    modes_rhs = -transform(divergence)
    wave_index = span_start + jnp.arange(span_cells)
    wavenumber = 2.0 * math.pi * wave_index.astype(jnp.float32) / span_total
    mode_diagonal = (10.0 + (2.0 - 2.0 * jnp.cos(wavenumber)))[:, None, None, None]
    pressure = chebyshev_weights[0] * modes_rhs / mode_diagonal
    for sweep_level in range(1, POISSON):
        padded = padded_2(pressure, (("gx", 2),), 1, False)
        padded = jnp.pad(padded, ((0, 0), (0, 0), (0, 0), (1, 1)))
        beside_all = (
            4.0 * (padded[:, :, 2:, 1:-1] + padded[:, :, :-2, 1:-1])
            + padded[:, :, 1:-1, 2:]
            + padded[:, :, 1:-1, :-2]
        )
        pressure = (
            pressure
            + chebyshev_weights[sweep_level]
            * (modes_rhs - (mode_diagonal * pressure - beside_all))
            / mode_diagonal
        )
    pressure = transform(pressure)
    padded = extend(pressure[None])[0]
    gradient = jnp.stack(
        [
            2.0 * (padded[1:-1, :, 2:, 1:-1] - pressure),
            padded[1:-1, :, 1:-1, 2:] - pressure,
            padded[2:, :, 1:-1, 1:-1] - pressure,
        ]
    )
    solved = velocity - gradient
    span_ids = span_start + jnp.arange(span_cells)
    stream_ids = stream_start + jnp.arange(stream_cells)
    normal_ids = jnp.arange(normal_cells)
    located = span_ids[None, :, None, None] == sensor_cells[:, 1][:, None, None, None]
    located = located & (stream_ids[None, None, :, None] == sensor_cells[:, 2][:, None, None, None])
    located = located & (normal_ids[None, None, None, :] == sensor_cells[:, 3][:, None, None, None])
    picked = jnp.einsum("szxy,czjxy->scj", located.astype(jnp.float32), solved, precision=highest)
    chooser = (jnp.arange(3)[None, :] == sensor_cells[:, 0:1]).astype(jnp.float32)
    readout_local = jnp.sum(picked * chooser[:, :, None], axis=1)
    new_factor = factor + 2.0 * shift_value * solved
    gram_local = jnp.einsum("czixy,czjxy->ij", new_factor, new_factor, precision=highest)
    gram_total, readout = lax.psum((gram_local, readout_local), ("gx", "gz"))
    gram = gram_total / (3.0 * stream_total * normal_cells * span_total)
    new_gain = gain + 2.0 * shift_value * jnp.einsum(
        "czjxy,ij->czixy", solved, readout, precision=highest
    )
    return (new_factor, new_gain, gram)


HALF = 32
PAIRS = 8


def recurrence_tables(centre, weights):
    ratio = centre / 2.0 - math.sqrt(centre * centre / 4.0 - 1.0)
    order = len(weights)
    step = ratio * np.tril(np.ones((order, order)))
    half = np.linalg.matrix_power(step, HALF)
    whole = np.linalg.matrix_power(step, 2 * HALF)
    angles = 2.0 * np.pi * np.arange(4096) / 4096
    series = [weights[0]]
    for weight in weights[1:]:
        longer = [0.0] + [weight * entry for entry in series]
        for place, entry in enumerate(series):
            longer[place] += (1.0 - weight) * entry
        longer[0] += weight
        series = longer
    mixes = []
    for power in range(1, order + 1):
        symbol = 1.0 / (centre - 2.0 * np.cos(angles)) ** power
        kernel = [np.mean(symbol * np.cos(angles * n)) for n in range(order + 1)]
        matrix = [[math.comb(n + i - 1, i - 1) for i in range(1, power + 1)] for n in range(1, power + 1)]
        sides = np.linalg.solve(
            np.array(matrix, np.float64), [kernel[n] / ratio**n for n in range(1, power + 1)]
        )
        middle = kernel[0] - 2.0 * np.sum(sides)
        mixes.append([float(series[power - 1] * entry) for entry in [middle, *sides]])
    return float(ratio), half.tolist(), whole, mixes


RATIO, HALF_TABLE, WHOLE_TABLE, MIXES = recurrence_tables(12.0, chebyshev_weights)


def lower_half():
    return lax.broadcasted_iota(jnp.int32, (8, 256), 0) < 4


def swap(cells):
    return pltpu.roll(cells, 4, 0)


def below(cells):
    lanes = lax.broadcasted_iota(jnp.int32, (8, 128), 1)
    low, high = pltpu.roll(cells[:, :128], 1, 1), pltpu.roll(cells[:, 128:], 1, 1)
    return jnp.concatenate([jnp.where(lanes > 0, low, 0.0), jnp.where(lanes > 0, high, low)], axis=1)


def above(cells):
    lanes = lax.broadcasted_iota(jnp.int32, (8, 128), 1)
    low, high = pltpu.roll(cells[:, :128], 127, 1), pltpu.roll(cells[:, 128:], 127, 1)
    return jnp.concatenate([jnp.where(lanes < 127, low, high), jnp.where(lanes < 127, high, 0.0)], axis=1)


def either_side(cells):
    lanes = lax.broadcasted_iota(jnp.int32, (8, 128), 1)
    low, high = cells[:, :128], cells[:, 128:]
    low_up, high_up = pltpu.roll(low, 1, 1), pltpu.roll(high, 1, 1)
    low_down, high_down = pltpu.roll(low, 127, 1), pltpu.roll(high, 127, 1)
    first = jnp.where(lanes > 0, low_up, 0.0) + jnp.where(lanes < 127, low_down, high_down)
    second = jnp.where(lanes > 0, high_up, low_up) + jnp.where(lanes < 127, high_down, 0.0)
    return jnp.concatenate([first, second], axis=1)


def shift_of(index_ref):
    index = index_ref[0]
    value = jnp.float32(shift_table[0])
    for place in range(1, SHIFTS):
        value = jnp.where(index == place, jnp.float32(shift_table[place]), value)
    return value


def x_odd():
    return lax.rem(lax.axis_index("gx"), 2)


def z_even():
    return lax.rem(lax.axis_index("gz"), 2) == 0


def cascade(state, cells):
    grown = []
    for entry in state:
        cells = RATIO * entry + cells
        grown.append(cells)
    return tuple(grown)


def half_states(read):
    zero = jnp.zeros((8, 256), jnp.float32)

    def body(t, carry):
        forward, backward = carry
        return cascade(forward, read(t)), cascade(backward, read(HALF - 1 - t))

    return lax.fori_loop(0, HALF, body, ((zero,) * POISSON, (zero,) * POISSON), unroll=HALF)


def turned(table, states, row):
    total = None
    for column in range(row + 1):
        term = table[row][column] * states[column]
        total = term if total is None else total + term
    return total


FACTOR_AT = 24
PART = 152
CORNERS = [(c, dx, side, 0) for c in range(3) for dx in (1, 2) for side in (0, 1)]
CORNERS += [(2, 1, 0, 1), (2, 3, 0, 0)]


def pack_kernel(factor_hbm, base_ref, own_ref, a_ref, b1_ref, b2_ref, z1_ref, z2_ref, factor_ref, arrived):
    share = factor_ref.shape[0] // 3
    copies = []
    for component in range(3):
        rows = pl.ds(component * share, share)
        copies.append(
            pltpu.make_async_copy(factor_hbm.at[rows], factor_ref.at[rows], arrived.at[component])
        )
        copies[-1].start()
    odd = x_odd()
    even = 1 - odd
    low = lax.broadcasted_iota(jnp.int32, (8, 128), 0) < 4
    scale = -1.0 / viscosity
    for component in range(3):

        def load(m, _, component=component):
            for x in range(4):
                for tile in range(2):
                    row = (component * 64 + 2 * m) * 32 + tile * 4 + x
                    first = factor_ref[pl.ds(row, 8, stride=8), :] * scale
                    second = factor_ref[pl.ds(row + 1024, 8, stride=8), :] * scale
                    lanes = slice(tile * 128, tile * 128 + 128)
                    own_ref[component, x, 2 * m, :, lanes] = jnp.where(low, first, swap(second))
                    own_ref[component, x, 2 * m + 1, :, lanes] = jnp.where(low, swap(first), second)
            return 0

        copies[component].wait()
        lax.fori_loop(0, 16, load, 0, unroll=2)

    def edges(zz, _):
        for component in range(3):
            for layer in range(3):
                at = FACTOR_AT + (component * 3 + layer) * HALF
                a_ref[at + zz] = own_ref[component, layer + even, zz]
                cells = own_ref[component, layer + odd, zz]
                if at < PART:
                    b1_ref[at + zz] = cells
                else:
                    b2_ref[at - PART + zz] = cells
        return 0

    lax.fori_loop(0, HALF, edges, 0, unroll=2)
    for layer in range(3):
        for group in range(8):
            for tile in range(2):
                lanes = slice(tile * 128, tile * 128 + 128)
                row = group * 64 + tile * 4 + layer
                a_ref[layer * 8 + group, :, lanes] = base_ref[pl.ds(row + even, 8, stride=8), :]
                b1_ref[layer * 8 + group, :, lanes] = base_ref[pl.ds(row + odd, 8, stride=8), :]
    lower = lower_half()
    rightward = z_even()
    for component in range(3):
        for x in range(4):
            for pair in range(2):
                cells = lambda zz: own_ref[component, x, zz]
                up = jnp.where(lower, swap(cells(31 - 2 * pair)), cells(30 - 2 * pair))
                down = jnp.where(lower, cells(2 * pair), swap(cells(2 * pair + 1)))
                at = (component * 4 + x) * 2 + pair
                z1_ref[at] = jnp.where(rightward, up, down)
                z2_ref[at] = jnp.where(rightward, down, up)
    for k in range(4):
        for tile in range(2):
            lanes = slice(tile * 128, tile * 128 + 128)
            up = base_ref[(63 - k) * 8 + tile * 4 : (63 - k) * 8 + tile * 4 + 4, :]
            down = base_ref[k * 8 + tile * 4 : k * 8 + tile * 4 + 4, :]
            rows = slice((k % 2) * 4, (k % 2) * 4 + 4)
            z1_ref[24 + k // 2, rows, lanes] = jnp.where(rightward, up, down)
            z2_ref[24 + k // 2, rows, lanes] = jnp.where(rightward, down, up)


def corner_kernel(z1_ref, z2_ref, a_ref, b_ref):
    odd = x_odd()
    rightward = z_even()

    def fill(behind_ref, ahead_ref):
        for place, (component, dx, side, pair) in enumerate(CORNERS):
            source = (behind_ref, ahead_ref)[side]
            right_x = 4 - dx
            left_x = dx - 1
            a_x = jnp.where(odd == 1, left_x, right_x)
            b_x = jnp.where(odd == 1, right_x, left_x)
            a_ref[place] = source[(component * 4 + a_x) * 2 + pair]
            b_ref[place] = source[(component * 4 + b_x) * 2 + pair]
        for dx in (1, 2, 3):
            for k in range(4):
                for side, source in enumerate((behind_ref, ahead_ref)):
                    from_right = source[24 + k // 2, (k % 2) * 4 + 4 - dx, :]
                    from_left = source[24 + k // 2, (k % 2) * 4 + dx - 1, :]
                    at = len(CORNERS) + dx - 1
                    a_ref[at, side * 4 + k, :] = jnp.where(odd == 1, from_left, from_right)
                    b_ref[at, side * 4 + k, :] = jnp.where(odd == 1, from_right, from_left)

    @pl.when(rightward)
    def _():
        fill(z2_ref, z1_ref)

    @pl.when(jnp.logical_not(rightward))
    def _():
        fill(z1_ref, z2_ref)


def velocity_kernel(
    index_ref, own_ref, base_ref, a_ref, b1_ref, b3_ref, b2_ref, ca_ref, cb_ref, z1_ref, z2_ref,
    v_ref, bw_ref, s_ref, pa_ref, pb1_ref, pb2_ref,
    flow_ref, a1_ref, r_ref, v0_ref, va_ref, vb_ref,
):
    odd = x_odd()
    stream = lax.axis_index("gx")
    last = lax.axis_size("gx") - 1
    mask_left = jnp.where(stream > 0, 1.0, 0.0)
    mask_right = jnp.where(stream < last, 1.0, 0.0)
    relayed = jnp.logical_or(stream == 3, stream == 4)
    rightward = z_even()
    lower = lower_half()
    shift = shift_of(index_ref)

    def each_z(step):
        @pl.when(rightward)
        def _():
            step(z2_ref, z1_ref)

        @pl.when(jnp.logical_not(rightward))
        def _():
            step(z1_ref, z2_ref)

    def inside(at):
        return lambda zz: a_ref[at + zz]

    def outside(first_ref):
        def pick(at):
            if at < PART:
                return lambda zz: first_ref[at + zz]
            return lambda zz: b2_ref[at - PART + zz]

        return pick

    def each_x(step):
        @pl.when(jnp.logical_and(odd == 0, relayed))
        def _():
            step(outside(b3_ref), cb_ref, inside, ca_ref)

        @pl.when(jnp.logical_and(odd == 0, jnp.logical_not(relayed)))
        def _():
            step(outside(b1_ref), cb_ref, inside, ca_ref)

        @pl.when(jnp.logical_and(odd == 1, relayed))
        def _():
            step(inside, ca_ref, outside(b3_ref), cb_ref)

        @pl.when(jnp.logical_and(odd == 1, jnp.logical_not(relayed)))
        def _():
            step(inside, ca_ref, outside(b1_ref), cb_ref)

    for x in range(4):
        for group in range(8):
            for tile in range(2):
                lanes = slice(tile * 128, tile * 128 + 128)
                flow_ref[x + 3, 8 + 8 * group : 16 + 8 * group, lanes] = base_ref[
                    pl.ds(group * 64 + tile * 4 + x, 8, stride=8), :
                ]

    def flow_span(behind_ref, ahead_ref):
        for x in range(4):
            for k in range(4):
                at = 24 + k // 2
                row = (k % 2) * 4 + x
                flow_ref[x + 3, 7 - k, :] = behind_ref[at, row, :]
                flow_ref[x + 3, 72 + k, :] = ahead_ref[at, row, :]

    each_z(flow_span)

    def flow_stream(left, left_corner, right, right_corner):
        for dx in (1, 2, 3):
            for place, layer, read, corner in (
                (3 - dx, 3 - dx, left, left_corner),
                (6 + dx, dx - 1, right, right_corner),
            ):
                for group in range(8):
                    flow_ref[place, 8 + 8 * group : 16 + 8 * group, :] = read(layer * 8)(group)
                for k in range(4):
                    flow_ref[place, 7 - k, :] = corner[len(CORNERS) + dx - 1, k, :]
                    flow_ref[place, 72 + k, :] = corner[len(CORNERS) + dx - 1, 4 + k, :]

    each_x(flow_stream)

    def coefficients(zz, _):
        for x in range(10):
            first = jnp.broadcast_to(flow_ref[x, pl.ds(zz + 4, 1), :], (8, 256))
            second = jnp.broadcast_to(flow_ref[x, pl.ds(zz + 36, 1), :], (8, 256))
            flow = jnp.where(lower, first, second)
            scale = viscosity * (mask_left if x < 3 else mask_right if x > 6 else 1.0)
            a1_ref[x, zz] = scale / (shift + 6.0 * viscosity + flow)
            r_ref[x, zz] = 1.0 + flow * (1.0 / viscosity)
        return 0

    lax.fori_loop(0, 39, coefficients, 0, unroll=3)
    zero = jnp.zeros((8, 256), jnp.float32)
    for x in (0, 1, 2, 7, 8, 9):
        for zz in (0, 1, 2, 3, 36, 37, 38):
            v0_ref[x, zz] = zero

    def swept(source, zz, margin, depth):
        result = {}
        before = [source[2 - margin, zz + k] for k in range(depth)]
        here = [source[3 - margin, zz + k - 1] for k in range(depth + 2)]
        for x in range(3 - margin, 7 + margin):
            if x < 6 + margin:
                ahead = [source[x + 1, zz + k - 1] for k in range(depth + 2)]
            else:
                ahead = [None] + [source[x + 1, zz + k] for k in range(depth)]
            result[x] = []
            for k in range(depth):
                total = ahead[k + 1] + either_side(here[k + 1])
                total = total + (here[k] + here[k + 2])
                result[x].append(
                    v0_ref[x, zz + k] + a1_ref[x, zz + k] * (total + r_ref[x, zz + k] * before[k])
                )
            before, here = here[1 : depth + 1], ahead
        return result

    def sweep(source, target, margin):
        depth = 4
        first, extent = 3 - margin, 33 + 2 * margin

        def body(t, _):
            zz = first + jnp.minimum(t * depth, extent - depth)
            for x, column in swept(source, zz, margin, depth).items():
                for k, cells in enumerate(column):
                    target[x, zz + k] = cells
            return 0

        lax.fori_loop(0, -(-extent // depth), body, 0, unroll=2)

    for component in range(3):

        def interior(zz, _, component=component):
            for x in range(4):
                v0_ref[x + 3, zz + 4] = own_ref[component, x, zz] * a1_ref[x + 3, zz + 4]
            return 0

        lax.fori_loop(0, HALF, interior, 0, unroll=4)

        def before(cells, halo, k):
            if k % 2 == 0:
                return jnp.where(lower, halo, swap(cells))
            return swap(jnp.where(lower, cells, halo))

        def after(cells, halo, k):
            if k % 2 == 0:
                return swap(jnp.where(lower, halo, cells))
            return jnp.where(lower, swap(cells), halo)

        def span(behind_ref, ahead_ref, component=component):
            for x in range(4):
                at = (component * 4 + x) * 2
                for k in range(4):
                    cells = before(own_ref[component, x, 31 - k], behind_ref[at + k // 2], k)
                    v0_ref[x + 3, 3 - k] = cells * a1_ref[x + 3, 3 - k]
                for k in range(3):
                    cells = after(own_ref[component, x, k], ahead_ref[at + k // 2], k)
                    v0_ref[x + 3, 36 + k] = cells * a1_ref[x + 3, 36 + k]

        each_z(span)

        def sides(left, left_corner, right, right_corner, component=component):
            for dx in (1, 2, 3):
                for place, layer, pick, corner in (
                    (3 - dx, 3 - dx, left, left_corner),
                    (6 + dx, dx - 1, right, right_corner),
                ):
                    read = pick(FACTOR_AT + (component * 3 + layer) * HALF)

                    def body(zz, _, read=read, place=place):
                        v0_ref[place, zz + 4] = read(zz) * a1_ref[place, zz + 4]
                        return 0

                    lax.fori_loop(0, HALF, body, 0, unroll=4)
                    for entry, (c, away, side, pair) in enumerate(CORNERS):
                        if c != component or away != dx:
                            continue
                        for k in (2 * pair, 2 * pair + 1):
                            if side == 0:
                                cells = before(read(31 - k), corner[entry], k)
                                v0_ref[place, 3 - k] = cells * a1_ref[place, 3 - k]
                            else:
                                cells = after(read(k), corner[entry], k)
                                v0_ref[place, 36 + k] = cells * a1_ref[place, 36 + k]

        each_x(sides)
        sweep(v0_ref, va_ref, 2)
        sweep(va_ref, vb_ref, 1)

        def diverge(t, before, component=component):
            depth = 4
            swept_cells = swept(vb_ref, 4 + t * depth, 0, depth)
            for k in range(depth):
                zz = t * depth + k
                cells = [swept_cells[x + 3][k] for x in range(4)]
                for x in range(4):
                    v_ref[component, x, zz] = cells[x]
                    if component == 0:
                        bw_ref[x, zz] = -2.0 * (cells[x] if x == 0 else cells[x] - cells[x - 1])
                    elif component == 1:
                        bw_ref[x, zz] = bw_ref[x, zz] - (cells[x] - below(cells[x]))
                    else:
                        bw_ref[x, zz] = bw_ref[x, zz] - (cells[x] - before[x])
                if component == 0:
                    bw_ref[4, zz] = cells[3]
                before = tuple(cells) if component == 2 else 0
            return before

        start = 0
        if component == 2:
            start = tuple(swept(vb_ref, 3, 0, 1)[x + 3][0] for x in range(4))
        lax.fori_loop(0, HALF // 4, diverge, start, unroll=2)

    even = 1 - odd

    def edges(zz, _):
        for layer in range(4):
            pa_ref[layer, zz] = bw_ref[layer + even, zz]
            (pb1_ref if layer < 2 else pb2_ref)[layer % 2, zz] = bw_ref[layer + odd, zz]
        return 0

    lax.fori_loop(0, HALF, edges, 0, unroll=4)

    def states(layer, _):
        forward, backward = half_states(lambda t: bw_ref[layer, t])
        swapped_forward = [swap(entry) for entry in forward]
        swapped_backward = [swap(entry) for entry in backward]
        for i in range(POISSON):
            onward = forward[i] + turned(HALF_TABLE, swapped_forward, i)
            back = backward[i] + turned(HALF_TABLE, swapped_backward, i)
            s_ref[i, layer] = jnp.where(lower, back, onward)
        s_ref[POISSON, layer] = bw_ref[layer, 0]
        return 0

    lax.fori_loop(0, 5, states, 0)


def pressure_kernel(
    index_ref, cells_ref, v_ref, bw_ref, ba_ref, b1_ref, b3_ref, b2_ref, inc_ref, ia_ref, ib_ref, factor_ref,
    nf_hbm, solved_ref, sums_ref,
    f_ref, i_ref, u_ref, q_ref, t_ref, nf_ref, sent,
):
    odd = x_odd()
    stream = lax.axis_index("gx")
    span = lax.axis_index("gz")
    last = lax.axis_size("gx") - 1
    mask_left = jnp.where(stream > 0, 1.0, 0.0)
    mask_right = jnp.where(stream < last, 1.0, 0.0)
    lower = lower_half()
    shift = shift_of(index_ref)

    def gather(left, right, left_inc, right_inc):
        def body(zz, _):
            for x in range(3):
                f_ref[x, zz] = mask_left * left(x, zz)
                f_ref[x + 4, zz] = bw_ref[x + 1, zz]
                f_ref[x + 8, zz] = mask_right * right(x + 1, zz)
            f_ref[3, zz] = bw_ref[0, zz] + (2.0 * mask_left) * left(3, zz)
            f_ref[7, zz] = mask_right * (right(0, zz) + 2.0 * bw_ref[4, zz])
            return 0

        lax.fori_loop(0, HALF, body, 0, unroll=4)
        for i in range(POISSON + 1):
            for x in range(3):
                i_ref[i, x] = left_inc[i, x]
                i_ref[i, x + 4] = inc_ref[i, x + 1]
                i_ref[i, x + 8] = right_inc[i, x + 1]
            i_ref[i, 3] = inc_ref[i, 0] + 2.0 * left_inc[i, 3]
            i_ref[i, 7] = mask_right * (right_inc[i, 0] + 2.0 * inc_ref[i, 4])
        for x in range(11):
            f_ref[x, HALF] = swap(jnp.where(lower, i_ref[POISSON, x], f_ref[x, 0]))

    def inside(layer, zz):
        return ba_ref[layer, zz]

    def direct(layer, zz):
        return b1_ref[layer, zz] if layer < 2 else b2_ref[layer - 2, zz]

    def relayed(layer, zz):
        return b3_ref[layer, zz] if layer < 2 else b2_ref[layer - 2, zz]

    middle = jnp.logical_or(stream == 3, stream == 4)
    for parity in (0, 1):
        for through, outside in ((False, direct), (True, relayed)):

            @pl.when(jnp.logical_and(odd == parity, middle == through))
            def _(parity=parity, outside=outside):
                if parity == 0:
                    gather(outside, inside, ib_ref, ia_ref)
                else:
                    gather(inside, outside, ia_ref, ib_ref)

    def solve(x, _):
        forward, backward = half_states(lambda t: f_ref[x, t])
        arriving = [i_ref[i, x] for i in range(POISSON)]
        swapped = [swap(entry) for entry in arriving]
        onward = []
        back = []
        for i in range(POISSON):
            carried = turned(HALF_TABLE, swapped, i)
            onward.append(swap(jnp.where(lower, forward[i] + carried, arriving[i])))
            back.append(swap(jnp.where(lower, arriving[i], backward[i] + carried)))

        def ahead(zz, state):
            state = cascade(state, f_ref[x, zz])
            for i in range(POISSON):
                u_ref[i, zz] = state[i]
            return state

        lax.fori_loop(0, HALF, ahead, tuple(onward), unroll=8)
        end = cascade([u_ref[i, HALF - 1] for i in range(POISSON)], f_ref[x, HALF])
        for i in range(POISSON):
            u_ref[i, HALF] = end[i]

        def mix(zz, state):
            both = [f_ref[x, zz]] + [u_ref[i, zz] + state[i] for i in range(POISSON)]
            for power in range(POISSON):
                total = MIXES[power][0] * both[0]
                for i in range(1, power + 2):
                    total = total + MIXES[power][i] * both[i]
                q_ref[power, x, zz] = total

        mix(HALF, back)

        def behind(t, state):
            zz = HALF - 1 - t
            state = cascade(state, f_ref[x, zz])
            mix(zz, state)
            return state

        lax.fori_loop(0, HALF, behind, tuple(back), unroll=8)
        return 0

    lax.fori_loop(0, 11, solve, 0)
    for power in (2, 1, 0):

        def apply(zz, _, power=power):
            edge = 2 - power
            layers = {x: q_ref[power + 1, x, zz] for x in range(edge, 11 - edge)}
            for x in range(edge + 1, 10 - edge if power else 8):
                beside = 4.0 * (layers[x - 1] + layers[x + 1]) + either_side(layers[x])
                if x < 3:
                    beside = mask_left * beside
                if x > 6:
                    beside = mask_right * beside
                q_ref[power, x, zz] = q_ref[power, x, zz] + beside
            return 0

        lax.fori_loop(0, HALF + 1, apply, 0, unroll=11)

    def correct(m, _):
        for x in range(4):
            pair = []
            for zz in (2 * m, 2 * m + 1):
                centre = q_ref[0, x + 3, zz]
                pair.append(
                    (
                        v_ref[0, x, zz] - 2.0 * (q_ref[0, x + 4, zz] - centre),
                        v_ref[1, x, zz] - (above(centre) - centre),
                        v_ref[2, x, zz] - (q_ref[0, x + 3, zz + 1] - centre),
                    )
                )
            for component in range(3):
                first, second = pair[0][component], pair[1][component]
                early = jnp.where(lower, first, swap(second))
                late = jnp.where(lower, swap(first), second)
                for tile in range(2):
                    row = (component * 64 + 2 * m) * 32 + tile * 4 + x
                    lanes = slice(tile * 128, tile * 128 + 128)
                    solved_ref[pl.ds(row, 8, stride=8), :] = early[:, lanes]
                    solved_ref[pl.ds(row + 1024, 8, stride=8), :] = late[:, lanes]
        return 0

    lax.fori_loop(0, 16, correct, 0, unroll=2)
    couples = [(i, j) for i in range(4) for j in range(i, 4)]

    def update(block, sums):
        columns = []
        for i in range(4):
            rows = pl.ds(pl.multiple_of(block * 32 + 8 * i, 8), 8)
            cells = factor_ref[rows, :] + (2.0 * shift) * solved_ref[rows, :]
            nf_ref[rows, :] = cells
            columns.append(cells)
        return tuple(s + columns[i] * columns[j] for s, (i, j) in zip(sums, couples))

    sums = (jnp.zeros((8, 128), jnp.float32),) * len(couples)
    copies = []
    for part in range(4):
        sums = lax.fori_loop(part * 48, part * 48 + 48, update, sums, unroll=4)
        rows = pl.ds(part * 1536, 1536)
        copies.append(pltpu.make_async_copy(nf_ref.at[rows], nf_hbm.at[rows], sent.at[part]))
        copies[-1].start()
    t_ref[...] = jnp.zeros((32, 128), jnp.float32)
    for total, (i, j) in zip(sums, couples):
        t_ref[4 * i + j : 4 * i + j + 1, :] = jnp.sum(total, axis=0, keepdims=True)
    lanes = lax.broadcasted_iota(jnp.int32, (1, 128), 1)
    for sensor in range(4):
        component = cells_ref[sensor, 0]
        z = cells_ref[sensor, 1] - span * 64
        x = cells_ref[sensor, 2] - stream * 4
        y = cells_ref[sensor, 3]
        held = (z >= 0) & (z < 64) & (x >= 0) & (x < 4)
        z = jnp.clip(z, 0, 63)
        x = jnp.clip(x, 0, 3)
        tile = jnp.where(y >= 128, 1, 0)
        lane = jnp.where(held, y - 128 * tile, -1)
        for column in range(4):
            row = (component * 64 + z) * 32 + column * 8 + tile * 4 + x
            cells = solved_ref[pl.ds(row, 1), :]
            at = 16 + 4 * sensor + column
            t_ref[at : at + 1, :] = jnp.where(lanes == lane, cells, 0.0)
    totals = jnp.sum(t_ref[...], axis=1, keepdims=True)
    spread = lax.broadcasted_iota(jnp.int32, (32, 128), 1) == lax.broadcasted_iota(jnp.int32, (32, 128), 0)
    sums_ref[...] = jnp.sum(jnp.where(spread, totals, 0.0), axis=0, keepdims=True)
    for copy in copies:
        copy.wait()


def gain_kernel(index_ref, sums_ref, gain_ref, solved_ref, out_hbm, gram_ref, out_ref, sent):
    totals = jnp.sum(sums_ref[...], axis=0, keepdims=True)
    lanes = lax.broadcasted_iota(jnp.int32, (1, 128), 1)
    shift = shift_of(index_ref)

    def entry(at):
        return jnp.sum(jnp.where(lanes == at, totals, 0.0), axis=1, keepdims=True)

    table = [
        [jnp.broadcast_to(2.0 * shift * entry(16 + 4 * i + j), (8, 128)) for j in range(4)] for i in range(4)
    ]

    def body(block, _):
        rows = [pl.ds(pl.multiple_of(block * 32 + 8 * j, 8), 8) for j in range(4)]
        columns = [solved_ref[rows[j], :] for j in range(4)]
        for i in range(4):
            total = gain_ref[rows[i], :]
            for j in range(4):
                total = total + table[i][j] * columns[j]
            out_ref[rows[i], :] = total
        return 0

    copies = []
    for part in range(6):
        lax.fori_loop(part * 32, part * 32 + 32, body, 0, unroll=4)
        rows = pl.ds(part * 1024, 1024)
        copies.append(pltpu.make_async_copy(out_ref.at[rows], out_hbm.at[rows], sent.at[part]))
        copies[-1].start()
    row = lax.broadcasted_iota(jnp.int32, (4, 4), 0)
    column = lax.broadcasted_iota(jnp.int32, (4, 4), 1)
    gram = jnp.zeros((4, 4), jnp.float32)
    for i in range(4):
        for j in range(4):
            value = entry(4 * min(i, j) + max(i, j)) / 6291456.0
            gram = gram + jnp.where((row == i) & (column == j), value, 0.0)
    gram_ref[...] = gram
    for copy in copies:
        copy.wait()


def call(kernel, outputs, scratch, operands, smalls, flops, far_in=(), far_out=(), signals=(), least=0):
    arrays = [jax.ShapeDtypeStruct(shape, jnp.float32) for shape in outputs]
    places = [pl.BlockSpec(memory_space=pltpu.SMEM)] * smalls
    places += [pl.BlockSpec(memory_space=pltpu.VMEM)] * (len(operands) - smalls)
    results = [pl.BlockSpec(memory_space=pltpu.VMEM)] * len(outputs)
    for place in far_in:
        places[place] = pl.BlockSpec(memory_space=pltpu.HBM)
    for place in far_out:
        results[place] = pl.BlockSpec(memory_space=pltpu.HBM)
    room = sum(4 * math.prod(shape) for shape in scratch) + (2 << 20)
    moved = sum(4 * math.prod(shape) for shape in outputs) + sum(4 * math.prod(o.shape) for o in operands)
    return pl.pallas_call(
        kernel,
        out_shape=arrays,
        in_specs=places,
        out_specs=results,
        scratch_shapes=[pltpu.VMEM(shape, jnp.float32) for shape in scratch]
        + [pltpu.SemaphoreType.DMA((count,)) for count in signals],
        compiler_params=pltpu.CompilerParams(vmem_limit_bytes=26 << 20),
        cost_estimate=pl.CostEstimate(flops=flops, bytes_accessed=moved, transcendentals=0),
    )(*operands)


def to_rows(cells):
    head = cells.shape[:-2]
    order = tuple(range(len(head)))
    split = cells.reshape(*head, 4, 2, 128).transpose(*order, len(head) + 1, len(head), len(head) + 2)
    return split.reshape(-1, 128)


def from_rows(rows, head):
    order = tuple(range(len(head)))
    split = rows.reshape(*head, 2, 4, 128).transpose(*order, len(head) + 1, len(head), len(head) + 2)
    return split.reshape(*head, 4, 256)


def mixed(table, states):
    table = np.asarray(table).astype(np.float32)
    return jnp.stack(
        [sum(float(table[i, k]) * states[k] for k in range(i + 1)) for i in range(POISSON)]
    )


def ring_states(states, partner, own_even, far):
    upper = jnp.arange(8)[None, None, :, None] >= 4
    first = upper == own_even
    nearer = jnp.where(first, partner, states)
    farther = jnp.where(first, states, partner)
    joined = nearer[:POISSON] + mixed(WHOLE_TABLE, farther[:POISSON])
    other = lax.ppermute(jnp.concatenate([joined, states[POISSON:]]), "gz", far)
    square = WHOLE_TABLE @ WHOLE_TABLE
    cube = square @ WHOLE_TABLE
    around = np.linalg.inv(np.eye(POISSON) - square @ square)
    entering = jnp.where(
        first[0],
        other[:POISSON] + mixed(square, partner[:POISSON]),
        partner[:POISSON] + mixed(WHOLE_TABLE, other[:POISSON]),
    )
    entering = entering + mixed(cube, states[:POISSON])
    entering = mixed(around, entering)
    ahead = jnp.where(own_even, partner[POISSON:], other[POISSON:])
    return jnp.concatenate([entering, ahead])


def fast_shards(factor, gain, base_flow, shift_index, sensor_cells):
    swap_in = [(0, 1), (1, 0), (2, 3), (3, 2), (4, 5), (5, 4), (6, 7), (7, 6)]
    swap_out = [(1, 2), (2, 1), (3, 4), (4, 3), (5, 6), (6, 5)]
    send_round = [(1, 2), (2, 1), (5, 6), (6, 5), (3, 7), (4, 0)]
    forward_round = [(7, 4), (0, 3)]
    near = [(0, 1), (1, 0), (2, 3), (3, 2)]
    far = [(1, 2), (2, 1), (3, 0), (0, 3)]
    odd = lax.axis_index("gx") % 2
    own_even = lax.axis_index("gz") % 2 == 0
    factor_rows = to_rows(factor)
    base_rows = to_rows(base_flow)
    gain_rows = to_rows(gain)
    cell = (8, 256)
    own, a, b1, b2, z1, z2 = call(
        pack_kernel,
        [(3, 4, HALF, *cell), (312, *cell), (PART, *cell), (312 - PART, *cell), (26, *cell), (26, *cell)],
        [factor_rows.shape], [factor_rows, base_rows], 0, 10**6, far_in=(0,), signals=(3,),
    )
    b1_in = lax.ppermute(b1, "gx", send_round)
    z1 = lax.ppermute(z1, "gz", near)
    z2 = lax.ppermute(z2, "gz", far)
    b2_in = lax.ppermute(b2, "gx", swap_out)
    a_in = lax.ppermute(a, "gx", swap_in)
    corners = len(CORNERS) + 3
    ca, cb = call(corner_kernel, [(corners, *cell)] * 2, [], [z1, z2], 0, 10**5)
    ca = lax.ppermute(ca, "gx", swap_in)
    cb = lax.ppermute(cb, "gx", swap_out)
    b1_in, z1, z2 = lax.optimization_barrier((b1_in, z1, z2))
    b3_in = lax.ppermute(b1_in, "gx", forward_round)
    block = (10, 39, *cell)
    velocity, sides, states, pa, pb1, pb2 = call(
        velocity_kernel,
        [(3, 4, HALF, *cell), (5, HALF, *cell), (POISSON + 1, 5, *cell), (4, HALF, *cell)]
        + [(2, HALF, *cell)] * 2,
        [(10, 80, 256)] + [block] * 5,
        [shift_index, own, base_rows, a_in, b1_in, b3_in, b2_in, ca, cb, z1, z2], 1, 10**8,
    )
    pb1_in = lax.ppermute(pb1, "gx", send_round)
    pb2_in = lax.ppermute(pb2, "gx", swap_out)
    partner = lax.ppermute(states, "gz", near)
    pb1_in, partner = lax.optimization_barrier((pb1_in, partner))
    pa_in = lax.ppermute(pa, "gx", swap_in)
    pb3_in = lax.ppermute(pb1_in, "gx", forward_round)
    entering = ring_states(states, partner, own_even, far)
    enter_b = lax.ppermute(lax.dynamic_slice_in_dim(entering, odd, 4, axis=1), "gx", swap_out)
    enter_a = lax.ppermute(lax.dynamic_slice_in_dim(entering, 1 - odd, 4, axis=1), "gx", swap_in)
    block = (11, HALF + 1, *cell)
    new_rows, solved, sums = call(
        pressure_kernel,
        [factor_rows.shape, factor_rows.shape, (1, 128)],
        [block, (POISSON + 1, 11, *cell), (POISSON, HALF + 1, *cell), (POISSON, *block), (32, 128)]
        + [factor_rows.shape],
        [shift_index, sensor_cells, velocity, sides, pa_in, pb1_in, pb3_in, pb2_in]
        + [entering, enter_a, enter_b, factor_rows],
        2, 10**8, far_out=(0,), signals=(4,),
    )
    devices = lax.axis_size("gx") * lax.axis_size("gz")
    shared = lax.all_to_all(
        jnp.broadcast_to(sums[None], (devices, 1, 128)), ("gx", "gz"), split_axis=0, concat_axis=0, tiled=True
    )
    new_gain, gram = call(
        gain_kernel,
        [gain_rows.shape, (4, 4)],
        [gain_rows.shape], [shift_index, shared.reshape(devices, 128), gain_rows, solved], 1, 10**7,
        far_out=(0,), signals=(6,),
    )
    head = factor.shape[:3]
    return (from_rows(new_rows, head), from_rows(new_gain, head), gram)


def solution(mesh):
    placed = (
        P(None, "gz", None, "gx", None),
        P(None, "gz", None, "gx", None),
        P("gz", "gx", None),
        P(),
        P(),
    )
    fits = mesh.shape["gx"] == 8 and mesh.shape["gz"] == 4
    return jax.shard_map(
        fast_shards if fits else shards,
        mesh=mesh,
        in_specs=placed,
        out_specs=(P(None, "gz", None, "gx", None), P(None, "gz", None, "gx", None), P()),
        check_vma=False,
    )
```

```python
import functools
import math

import jax
import jax.numpy as jnp
import numpy as np
from jax import lax
from jax.experimental import pallas as pl
from jax.experimental.pallas import tpu as pltpu
from jax.sharding import PartitionSpec as P

SWEEPS = 3
POISSON = 4
SHIFTS = 8


viscosity = 0.4
shift_table = (0.6, 0.8, 1.0, 1.25, 1.6, 2.0, 2.5, 3.2)
chebyshev_weights = (1.0 / 1.9352976, 1.0 / 1.4752809, 1.0 / 0.8247191, 1.0 / 0.3647024)
highest = lax.Precision.HIGHEST


def padded_2(cells, sides, width, closed):
    for axis, dim in sides:
        count = lax.axis_size(axis)
        ends = count if closed else count - 1
        head = lax.slice_in_dim(cells, 0, width, axis=dim)
        tail = lax.slice_in_dim(cells, cells.shape[dim] - width, cells.shape[dim], axis=dim)
        cells = jnp.concatenate(
            [
                lax.ppermute(tail, axis, [(i, (i + 1) % count) for i in range(ends)]),
                cells,
                lax.ppermute(head, axis, [((i + 1) % count, i) for i in range(ends)]),
            ],
            axis=dim,
        )
    return cells


def around_sum(padded):
    summed = padded[:, 1:-1, :, 2:, 1:-1] + padded[:, 1:-1, :, :-2, 1:-1]
    summed = summed + padded[:, 1:-1, :, 1:-1, 2:] + padded[:, 1:-1, :, 1:-1, :-2]
    return summed + padded[:, 2:, :, 1:-1, 1:-1] + padded[:, :-2, :, 1:-1, 1:-1]


def shards(factor, gain, base_flow, shift_index, sensor_cells):
    components, span_cells, columns, stream_cells, normal_cells = factor.shape
    stream_start = lax.axis_index("gx") * stream_cells
    span_start = lax.axis_index("gz") * span_cells
    stream_total = stream_cells * lax.axis_size("gx")
    span_total = span_cells * lax.axis_size("gz")
    shift_values = jnp.asarray(shift_table, jnp.float32)
    shift_value = jnp.sum(jnp.where(jnp.arange(SHIFTS) == shift_index[0], shift_values, 0.0))
    base_field = base_flow[None, :, None, :, :]
    diagonal = shift_value + 6.0 * viscosity + base_field
    source = -factor

    def stream_inside(extent, margin):
        positions = stream_start - margin + jnp.arange(extent)
        return ((positions >= 0) & (positions < stream_total)).astype(jnp.float32)

    def extend(grid_field):
        padded = padded_2(grid_field, (("gx", 3), ("gz", 1)), 1, True)
        padded = padded * stream_inside(stream_cells + 2, 1)[None, None, None, :, None]
        return jnp.pad(padded, ((0, 0), (0, 0), (0, 0), (0, 0), (1, 1)))

    velocity = source / diagonal
    for sweep_index in range(SWEEPS):
        padded = extend(velocity)
        velocity = (
            source + viscosity * around_sum(padded) + base_field * padded[:, 1:-1, :, :-2, 1:-1]
        ) / diagonal
    padded = extend(velocity)
    divergence = 2.0 * (velocity[0] - padded[0, 1:-1, :, :-2, 1:-1])
    divergence = divergence + (velocity[1] - padded[1, 1:-1, :, 1:-1, :-2])
    divergence = divergence + (velocity[2] - padded[2, :-2, :, 1:-1, 1:-1])
    span_index = jnp.arange(span_total)
    products = span_index[:, None] * span_index[None, :] % span_total
    angles = 2.0 * math.pi * products.astype(jnp.float32) / span_total
    hartley_table = (jnp.cos(angles) + jnp.sin(angles)) / math.sqrt(span_total)

    def turn_modes(exchanged):
        turned = jnp.einsum("kz,zay->kay", hartley_table, exchanged, precision=highest)
        return lax.all_to_all(turned, "gz", split_axis=0, concat_axis=1, tiled=True)

    def transform(grid_field):
        flat = grid_field.reshape(span_cells, columns * stream_cells, normal_cells)
        result = turn_modes(lax.all_to_all(flat, "gz", split_axis=1, concat_axis=0, tiled=True))
        return result.reshape(span_cells, columns, stream_cells, normal_cells)

    modes_rhs = -transform(divergence)
    wave_index = span_start + jnp.arange(span_cells)
    wavenumber = 2.0 * math.pi * wave_index.astype(jnp.float32) / span_total
    mode_diagonal = (10.0 + (2.0 - 2.0 * jnp.cos(wavenumber)))[:, None, None, None]
    pressure = chebyshev_weights[0] * modes_rhs / mode_diagonal
    for sweep_level in range(1, POISSON):
        padded = padded_2(pressure, (("gx", 2),), 1, False)
        padded = jnp.pad(padded, ((0, 0), (0, 0), (0, 0), (1, 1)))
        beside_all = (
            4.0 * (padded[:, :, 2:, 1:-1] + padded[:, :, :-2, 1:-1])
            + padded[:, :, 1:-1, 2:]
            + padded[:, :, 1:-1, :-2]
        )
        pressure = (
            pressure
            + chebyshev_weights[sweep_level]
            * (modes_rhs - (mode_diagonal * pressure - beside_all))
            / mode_diagonal
        )
    pressure = transform(pressure)
    padded = extend(pressure[None])[0]
    gradient = jnp.stack(
        [
            2.0 * (padded[1:-1, :, 2:, 1:-1] - pressure),
            padded[1:-1, :, 1:-1, 2:] - pressure,
            padded[2:, :, 1:-1, 1:-1] - pressure,
        ]
    )
    solved = velocity - gradient
    span_ids = span_start + jnp.arange(span_cells)
    stream_ids = stream_start + jnp.arange(stream_cells)
    normal_ids = jnp.arange(normal_cells)
    located = span_ids[None, :, None, None] == sensor_cells[:, 1][:, None, None, None]
    located = located & (stream_ids[None, None, :, None] == sensor_cells[:, 2][:, None, None, None])
    located = located & (normal_ids[None, None, None, :] == sensor_cells[:, 3][:, None, None, None])
    picked = jnp.einsum("szxy,czjxy->scj", located.astype(jnp.float32), solved, precision=highest)
    chooser = (jnp.arange(3)[None, :] == sensor_cells[:, 0:1]).astype(jnp.float32)
    readout_local = jnp.sum(picked * chooser[:, :, None], axis=1)
    new_factor = factor + 2.0 * shift_value * solved
    gram_local = jnp.einsum("czixy,czjxy->ij", new_factor, new_factor, precision=highest)
    gram_total, readout = lax.psum((gram_local, readout_local), ("gx", "gz"))
    gram = gram_total / (3.0 * stream_total * normal_cells * span_total)
    new_gain = gain + 2.0 * shift_value * jnp.einsum(
        "czjxy,ij->czixy", solved, readout, precision=highest
    )
    return (new_factor, new_gain, gram)


HALF = 32
PAIRS = 8


def recurrence_tables(centre, weights):
    ratio = centre / 2.0 - math.sqrt(centre * centre / 4.0 - 1.0)
    order = len(weights)
    step = ratio * np.tril(np.ones((order, order)))
    half = np.linalg.matrix_power(step, HALF)
    whole = np.linalg.matrix_power(step, 2 * HALF)
    angles = 2.0 * np.pi * np.arange(4096) / 4096
    series = [weights[0]]
    for weight in weights[1:]:
        longer = [0.0] + [weight * entry for entry in series]
        for place, entry in enumerate(series):
            longer[place] += (1.0 - weight) * entry
        longer[0] += weight
        series = longer
    mixes = []
    for power in range(1, order + 1):
        symbol = 1.0 / (centre - 2.0 * np.cos(angles)) ** power
        kernel = [np.mean(symbol * np.cos(angles * n)) for n in range(order + 1)]
        matrix = [[math.comb(n + i - 1, i - 1) for i in range(1, power + 1)] for n in range(1, power + 1)]
        sides = np.linalg.solve(
            np.array(matrix, np.float64), [kernel[n] / ratio**n for n in range(1, power + 1)]
        )
        middle = kernel[0] - 2.0 * np.sum(sides)
        mixes.append([float(series[power - 1] * entry) for entry in [middle, *sides]])
    return float(ratio), half.tolist(), whole, mixes


RATIO, HALF_TABLE, WHOLE_TABLE, MIXES = recurrence_tables(12.0, chebyshev_weights)


def lower_half():
    return lax.broadcasted_iota(jnp.int32, (8, 256), 0) < 4


def swap(cells):
    return pltpu.roll(cells, 4, 0)


def below(cells):
    lanes = lax.broadcasted_iota(jnp.int32, (8, 128), 1)
    low, high = pltpu.roll(cells[:, :128], 1, 1), pltpu.roll(cells[:, 128:], 1, 1)
    return jnp.concatenate([jnp.where(lanes > 0, low, 0.0), jnp.where(lanes > 0, high, low)], axis=1)


def above(cells):
    lanes = lax.broadcasted_iota(jnp.int32, (8, 128), 1)
    low, high = pltpu.roll(cells[:, :128], 127, 1), pltpu.roll(cells[:, 128:], 127, 1)
    return jnp.concatenate([jnp.where(lanes < 127, low, high), jnp.where(lanes < 127, high, 0.0)], axis=1)


def either_side(cells):
    lanes = lax.broadcasted_iota(jnp.int32, (8, 128), 1)
    low, high = cells[:, :128], cells[:, 128:]
    low_up, high_up = pltpu.roll(low, 1, 1), pltpu.roll(high, 1, 1)
    low_down, high_down = pltpu.roll(low, 127, 1), pltpu.roll(high, 127, 1)
    first = jnp.where(lanes > 0, low_up, 0.0) + jnp.where(lanes < 127, low_down, high_down)
    second = jnp.where(lanes > 0, high_up, low_up) + jnp.where(lanes < 127, high_down, 0.0)
    return jnp.concatenate([first, second], axis=1)


def shift_of(index_ref):
    index = index_ref[0]
    value = jnp.float32(shift_table[0])
    for place in range(1, SHIFTS):
        value = jnp.where(index == place, jnp.float32(shift_table[place]), value)
    return value


def x_odd():
    return lax.rem(lax.axis_index("gx"), 2)


def z_even():
    return lax.rem(lax.axis_index("gz"), 2) == 0


def cascade(state, cells):
    grown = []
    for entry in state:
        cells = RATIO * entry + cells
        grown.append(cells)
    return tuple(grown)


def half_states(read):
    zero = jnp.zeros((8, 256), jnp.float32)

    def body(t, carry):
        forward, backward = carry
        return cascade(forward, read(t)), cascade(backward, read(HALF - 1 - t))

    return lax.fori_loop(0, HALF, body, ((zero,) * POISSON, (zero,) * POISSON), unroll=HALF)


def turned(table, states, row):
    total = None
    for column in range(row + 1):
        term = table[row][column] * states[column]
        total = term if total is None else total + term
    return total


FACTOR_AT = 24
PART = 152
CORNERS = [(c, dx, side, 0) for c in range(3) for dx in (1, 2) for side in (0, 1)]
CORNERS += [(2, 1, 0, 1), (2, 3, 0, 0)]


def pack_kernel(factor_hbm, base_ref, own_ref, a_ref, b1_ref, b2_ref, z1_ref, z2_ref, factor_ref, arrived):
    share = factor_ref.shape[0] // 3
    copies = []
    for component in range(3):
        rows = pl.ds(component * share, share)
        copies.append(
            pltpu.make_async_copy(factor_hbm.at[rows], factor_ref.at[rows], arrived.at[component])
        )
        copies[-1].start()
    odd = x_odd()
    even = 1 - odd
    low = lax.broadcasted_iota(jnp.int32, (8, 128), 0) < 4
    scale = -1.0 / viscosity
    for component in range(3):

        def load(m, _, component=component):
            for x in range(4):
                for tile in range(2):
                    row = (component * 64 + 2 * m) * 32 + tile * 4 + x
                    first = factor_ref[pl.ds(row, 8, stride=8), :] * scale
                    second = factor_ref[pl.ds(row + 1024, 8, stride=8), :] * scale
                    lanes = slice(tile * 128, tile * 128 + 128)
                    own_ref[component, x, 2 * m, :, lanes] = jnp.where(low, first, swap(second))
                    own_ref[component, x, 2 * m + 1, :, lanes] = jnp.where(low, swap(first), second)
            return 0

        copies[component].wait()
        lax.fori_loop(0, 16, load, 0, unroll=2)

    def edges(zz, _):
        for component in range(3):
            for layer in range(3):
                at = FACTOR_AT + (component * 3 + layer) * HALF
                a_ref[at + zz] = own_ref[component, layer + even, zz]
                cells = own_ref[component, layer + odd, zz]
                if at < PART:
                    b1_ref[at + zz] = cells
                else:
                    b2_ref[at - PART + zz] = cells
        return 0

    lax.fori_loop(0, HALF, edges, 0, unroll=2)
    for layer in range(3):
        for group in range(8):
            for tile in range(2):
                lanes = slice(tile * 128, tile * 128 + 128)
                row = group * 64 + tile * 4 + layer
                a_ref[layer * 8 + group, :, lanes] = base_ref[pl.ds(row + even, 8, stride=8), :]
                b1_ref[layer * 8 + group, :, lanes] = base_ref[pl.ds(row + odd, 8, stride=8), :]
    lower = lower_half()
    rightward = z_even()
    for component in range(3):
        for x in range(4):
            for pair in range(2):
                cells = lambda zz: own_ref[component, x, zz]
                up = jnp.where(lower, swap(cells(31 - 2 * pair)), cells(30 - 2 * pair))
                down = jnp.where(lower, cells(2 * pair), swap(cells(2 * pair + 1)))
                at = (component * 4 + x) * 2 + pair
                z1_ref[at] = jnp.where(rightward, up, down)
                z2_ref[at] = jnp.where(rightward, down, up)
    for k in range(4):
        for tile in range(2):
            lanes = slice(tile * 128, tile * 128 + 128)
            up = base_ref[(63 - k) * 8 + tile * 4 : (63 - k) * 8 + tile * 4 + 4, :]
            down = base_ref[k * 8 + tile * 4 : k * 8 + tile * 4 + 4, :]
            rows = slice((k % 2) * 4, (k % 2) * 4 + 4)
            z1_ref[24 + k // 2, rows, lanes] = jnp.where(rightward, up, down)
            z2_ref[24 + k // 2, rows, lanes] = jnp.where(rightward, down, up)


def corner_kernel(z1_ref, z2_ref, a_ref, b_ref):
    odd = x_odd()
    rightward = z_even()

    def fill(behind_ref, ahead_ref):
        for place, (component, dx, side, pair) in enumerate(CORNERS):
            source = (behind_ref, ahead_ref)[side]
            right_x = 4 - dx
            left_x = dx - 1
            a_x = jnp.where(odd == 1, left_x, right_x)
            b_x = jnp.where(odd == 1, right_x, left_x)
            a_ref[place] = source[(component * 4 + a_x) * 2 + pair]
            b_ref[place] = source[(component * 4 + b_x) * 2 + pair]
        for dx in (1, 2, 3):
            for k in range(4):
                for side, source in enumerate((behind_ref, ahead_ref)):
                    from_right = source[24 + k // 2, (k % 2) * 4 + 4 - dx, :]
                    from_left = source[24 + k // 2, (k % 2) * 4 + dx - 1, :]
                    at = len(CORNERS) + dx - 1
                    a_ref[at, side * 4 + k, :] = jnp.where(odd == 1, from_left, from_right)
                    b_ref[at, side * 4 + k, :] = jnp.where(odd == 1, from_right, from_left)

    @pl.when(rightward)
    def _():
        fill(z2_ref, z1_ref)

    @pl.when(jnp.logical_not(rightward))
    def _():
        fill(z1_ref, z2_ref)


KNOWN = {("early", 0): (3, 9), ("early", 1): (0, 6), ("late", 0): (0, 5), ("late", 1): (4, 9)}
SWEPT = {
    ("early", 0): ((4, 8), (5, 7), (6, 6)),
    ("early", 1): ((1, 5), (2, 4), (3, 3)),
    ("late", 0): ((1, 3), (2, 4), (3, 5)),
    ("late", 1): ((6, 8), (5, 7), (4, 6)),
}
HANDED = (((4, 5), (5, 6), 6), ((4, 5), (3, 4), 3))


def velocity_kernel(stage, *refs):
    early = stage == "early"
    if early:
        index_ref, own_ref, base_ref, a_ref, c_ref, z1_ref, z2_ref, *refs = refs
        h1_ref, h2_ref, h3_ref, *refs = refs
    else:
        index_ref, own_ref, base_ref, b1_ref, b3_ref, b2_ref, c_ref, z1_ref, z2_ref, *refs = refs
        h1_ref, h2_ref, h3_ref, v_ref, bw_ref, s_ref, pa_ref, pb1_ref, pb2_ref, *refs = refs
    flow_ref, a1_ref, r_ref, v0_ref, va_ref, vb_ref = refs
    odd = x_odd()
    stream = lax.axis_index("gx")
    last = lax.axis_size("gx") - 1
    mask_left = jnp.where(stream > 0, 1.0, 0.0)
    mask_right = jnp.where(stream < last, 1.0, 0.0)
    relayed = jnp.logical_or(stream == 3, stream == 4)
    rightward = z_even()
    lower = lower_half()
    shift = shift_of(index_ref)
    zero = jnp.zeros((8, 256), jnp.float32)

    def each_z(step):
        @pl.when(rightward)
        def _():
            step(z2_ref, z1_ref)

        @pl.when(jnp.logical_not(rightward))
        def _():
            step(z1_ref, z2_ref)

    def inside(at):
        return lambda zz: a_ref[at + zz]

    def outside(first_ref):
        def pick(at):
            if at < PART:
                return lambda zz: first_ref[at + zz]
            return lambda zz: b2_ref[at - PART + zz]

        return pick

    def each_x(step):
        if early:
            step(inside)
            return

        @pl.when(relayed)
        def _():
            step(outside(b3_ref))

        @pl.when(jnp.logical_not(relayed))
        def _():
            step(outside(b1_ref))

    def before(cells, halo, k):
        if k % 2 == 0:
            return jnp.where(lower, halo, swap(cells))
        return swap(jnp.where(lower, cells, halo))

    def after(cells, halo, k):
        if k % 2 == 0:
            return swap(jnp.where(lower, halo, cells))
        return jnp.where(lower, swap(cells), halo)

    def run(parity):
        low, high = KNOWN[stage, parity]
        own_layers = [x for x in range(4) if low <= x + 3 <= high]
        if low < 3:
            halo = [(dx, 3 - dx, 3 - dx) for dx in (1, 2, 3)]
        else:
            halo = [(dx, 6 + dx, dx - 1) for dx in (1, 2, 3)]

        for x in own_layers:
            for group in range(8):
                for tile in range(2):
                    lanes = slice(tile * 128, tile * 128 + 128)
                    flow_ref[x + 3, 8 + 8 * group : 16 + 8 * group, lanes] = base_ref[
                        pl.ds(group * 64 + tile * 4 + x, 8, stride=8), :
                    ]

        def flow_span(behind_ref, ahead_ref):
            for x in own_layers:
                for k in range(4):
                    at = 24 + k // 2
                    row = (k % 2) * 4 + x
                    flow_ref[x + 3, 7 - k, :] = behind_ref[at, row, :]
                    flow_ref[x + 3, 72 + k, :] = ahead_ref[at, row, :]

        each_z(flow_span)

        def flow_stream(pick):
            for dx, place, layer in halo:
                for group in range(8):
                    flow_ref[place, 8 + 8 * group : 16 + 8 * group, :] = pick(layer * 8)(group)
                for k in range(4):
                    flow_ref[place, 7 - k, :] = c_ref[len(CORNERS) + dx - 1, k, :]
                    flow_ref[place, 72 + k, :] = c_ref[len(CORNERS) + dx - 1, 4 + k, :]

        each_x(flow_stream)

        def coefficients(zz, _):
            for x in range(low, high + 1):
                first = jnp.broadcast_to(flow_ref[x, pl.ds(zz + 4, 1), :], (8, 256))
                second = jnp.broadcast_to(flow_ref[x, pl.ds(zz + 36, 1), :], (8, 256))
                flow = jnp.where(lower, first, second)
                scale = viscosity * (mask_left if x < 3 else mask_right if x > 6 else 1.0)
                a1_ref[x, zz] = scale / (shift + 6.0 * viscosity + flow)
                r_ref[x, zz] = 1.0 + flow * (1.0 / viscosity)
            return 0

        lax.fori_loop(0, 39, coefficients, 0, unroll=3)
        for _, place, _ in halo:
            for zz in (0, 1, 2, 3, 36, 37, 38):
                v0_ref[place, zz] = zero

        def swept(source, span, zz, depth):
            result = {}
            first, final = span
            behind = [source(first - 1, zz + k) for k in range(depth)]
            here = [source(first, zz + k - 1) for k in range(depth + 2)]
            for x in range(first, final + 1):
                if x < final:
                    ahead = [source(x + 1, zz + k - 1) for k in range(depth + 2)]
                else:
                    ahead = [None] + [source(x + 1, zz + k) for k in range(depth)]
                result[x] = []
                for k in range(depth):
                    total = ahead[k + 1] + either_side(here[k + 1])
                    total = total + (here[k] + here[k + 2])
                    total = total + r_ref[x, zz + k] * behind[k]
                    result[x].append(v0_ref[x, zz + k] + a1_ref[x, zz + k] * total)
                behind, here = here[1 : depth + 1], ahead
            return result

        def sweep(source, target, level, margin, hand):
            depth = 4
            first, extent = 3 - margin, 33 + 2 * margin

            def body(t, _):
                zz = first + jnp.minimum(t * depth, extent - depth)
                for x, column in swept(source, SWEPT[stage, parity][level], zz, depth).items():
                    for k, cells in enumerate(column):
                        if target is not None:
                            target[x, zz + k] = cells
                        hand(x, zz + k, cells)
                return 0

            lax.fori_loop(0, -(-extent // depth), body, 0, unroll=2)

        handed_first, handed_second, handed_third = HANDED[parity]
        for component in range(3):

            def interior(zz, _, component=component):
                for x in own_layers:
                    v0_ref[x + 3, zz + 4] = own_ref[component, x, zz] * a1_ref[x + 3, zz + 4]
                return 0

            lax.fori_loop(0, HALF, interior, 0, unroll=4)

            def span(behind_ref, ahead_ref, component=component):
                for x in own_layers:
                    at = (component * 4 + x) * 2
                    for k in range(4):
                        cells = before(own_ref[component, x, 31 - k], behind_ref[at + k // 2], k)
                        v0_ref[x + 3, 3 - k] = cells * a1_ref[x + 3, 3 - k]
                    for k in range(3):
                        cells = after(own_ref[component, x, k], ahead_ref[at + k // 2], k)
                        v0_ref[x + 3, 36 + k] = cells * a1_ref[x + 3, 36 + k]

            each_z(span)

            def sides(pick, component=component):
                for dx, place, layer in halo:
                    read = pick(FACTOR_AT + (component * 3 + layer) * HALF)

                    def body(zz, _, read=read, place=place):
                        v0_ref[place, zz + 4] = read(zz) * a1_ref[place, zz + 4]
                        return 0

                    lax.fori_loop(0, HALF, body, 0, unroll=4)
                    for entry, (c, away, side, pair) in enumerate(CORNERS):
                        if c != component or away != dx:
                            continue
                        for k in (2 * pair, 2 * pair + 1):
                            if side == 0:
                                cells = before(read(31 - k), c_ref[entry], k)
                                v0_ref[place, 3 - k] = cells * a1_ref[place, 3 - k]
                            else:
                                cells = after(read(k), c_ref[entry], k)
                                v0_ref[place, 36 + k] = cells * a1_ref[place, 36 + k]

            each_x(sides)

            def hand_first(x, zz, cells, component=component):
                if early and x in handed_first:
                    h1_ref[component, handed_first.index(x), zz] = cells

            def hand_second(x, zz, cells, component=component):
                if early and x in handed_second:
                    h2_ref[component, handed_second.index(x), zz] = cells

            def hand_third(x, zz, cells, component=component):
                h3_ref[component, zz - 3] = cells

            def from_first(x, zz, component=component):
                if not early and x in handed_first:
                    return h1_ref[component, handed_first.index(x), zz]
                return va_ref[x, zz]

            def from_second(x, zz, component=component):
                if not early and x in handed_second:
                    return h2_ref[component, handed_second.index(x), zz]
                return vb_ref[x, zz]

            sweep(lambda x, zz: v0_ref[x, zz], va_ref, 0, 2, hand_first)
            sweep(from_first, vb_ref, 1, 1, hand_second)
            if early:
                sweep(from_second, None, 2, 0, hand_third)
                continue

            def finished(zz, depth, component=component):
                found = swept(from_second, SWEPT[stage, parity][2], zz + 4, depth)
                found[handed_third] = [h3_ref[component, zz + 1 + k] for k in range(depth)]
                return [[found[x + 3][k] for x in range(4)] for k in range(depth)]

            def diverge(t, past, component=component):
                for k, cells in enumerate(finished(4 * t, 4)):
                    zz = 4 * t + k
                    for x in range(4):
                        v_ref[component, x, zz] = cells[x]
                        if component == 0:
                            bw_ref[x, zz] = -2.0 * (cells[x] if x == 0 else cells[x] - cells[x - 1])
                        elif component == 1:
                            bw_ref[x, zz] = bw_ref[x, zz] - (cells[x] - below(cells[x]))
                        else:
                            bw_ref[x, zz] = bw_ref[x, zz] - (cells[x] - past[x])
                    if component == 0:
                        bw_ref[4, zz] = cells[3]
                    past = tuple(cells) if component == 2 else 0
                return past

            start = tuple(finished(-1, 1)[0]) if component == 2 else 0
            lax.fori_loop(0, HALF // 4, diverge, start, unroll=2)

    for parity in (0, 1):

        @pl.when(odd == parity)
        def _(parity=parity):
            run(parity)

    if early:
        return
    even = 1 - odd

    def edges(zz, _):
        for layer in range(4):
            pa_ref[layer, zz] = bw_ref[layer + even, zz]
            (pb1_ref if layer < 2 else pb2_ref)[layer % 2, zz] = bw_ref[layer + odd, zz]
        return 0

    lax.fori_loop(0, HALF, edges, 0, unroll=4)

    def states(layer, _):
        forward, backward = half_states(lambda t: bw_ref[layer, t])
        swapped_forward = [swap(entry) for entry in forward]
        swapped_backward = [swap(entry) for entry in backward]
        for i in range(POISSON):
            onward = forward[i] + turned(HALF_TABLE, swapped_forward, i)
            back = backward[i] + turned(HALF_TABLE, swapped_backward, i)
            s_ref[i, layer] = jnp.where(lower, back, onward)
        s_ref[POISSON, layer] = bw_ref[layer, 0]
        return 0

    lax.fori_loop(0, 5, states, 0)


def pressure_kernel(
    index_ref, cells_ref, v_ref, bw_ref, ba_ref, b1_ref, b3_ref, b2_ref, inc_ref, ia_ref, ib_ref, factor_ref,
    nf_hbm, solved_ref, sums_ref,
    f_ref, i_ref, u_ref, q_ref, t_ref, nf_ref, sent,
):
    odd = x_odd()
    stream = lax.axis_index("gx")
    span = lax.axis_index("gz")
    last = lax.axis_size("gx") - 1
    mask_left = jnp.where(stream > 0, 1.0, 0.0)
    mask_right = jnp.where(stream < last, 1.0, 0.0)
    lower = lower_half()
    shift = shift_of(index_ref)

    def gather(left, right, left_inc, right_inc):
        def body(zz, _):
            for x in range(3):
                f_ref[x, zz] = mask_left * left(x, zz)
                f_ref[x + 4, zz] = bw_ref[x + 1, zz]
                f_ref[x + 8, zz] = mask_right * right(x + 1, zz)
            f_ref[3, zz] = bw_ref[0, zz] + (2.0 * mask_left) * left(3, zz)
            f_ref[7, zz] = mask_right * (right(0, zz) + 2.0 * bw_ref[4, zz])
            return 0

        lax.fori_loop(0, HALF, body, 0, unroll=4)
        for i in range(POISSON + 1):
            for x in range(3):
                i_ref[i, x] = left_inc[i, x]
                i_ref[i, x + 4] = inc_ref[i, x + 1]
                i_ref[i, x + 8] = right_inc[i, x + 1]
            i_ref[i, 3] = inc_ref[i, 0] + 2.0 * left_inc[i, 3]
            i_ref[i, 7] = mask_right * (right_inc[i, 0] + 2.0 * inc_ref[i, 4])
        for x in range(11):
            f_ref[x, HALF] = swap(jnp.where(lower, i_ref[POISSON, x], f_ref[x, 0]))

    def inside(layer, zz):
        return ba_ref[layer, zz]

    def direct(layer, zz):
        return b1_ref[layer, zz] if layer < 2 else b2_ref[layer - 2, zz]

    def relayed(layer, zz):
        return b3_ref[layer, zz] if layer < 2 else b2_ref[layer - 2, zz]

    middle = jnp.logical_or(stream == 3, stream == 4)
    for parity in (0, 1):
        for through, outside in ((False, direct), (True, relayed)):

            @pl.when(jnp.logical_and(odd == parity, middle == through))
            def _(parity=parity, outside=outside):
                if parity == 0:
                    gather(outside, inside, ib_ref, ia_ref)
                else:
                    gather(inside, outside, ia_ref, ib_ref)

    def solve(x, _):
        forward, backward = half_states(lambda t: f_ref[x, t])
        arriving = [i_ref[i, x] for i in range(POISSON)]
        swapped = [swap(entry) for entry in arriving]
        onward = []
        back = []
        for i in range(POISSON):
            carried = turned(HALF_TABLE, swapped, i)
            onward.append(swap(jnp.where(lower, forward[i] + carried, arriving[i])))
            back.append(swap(jnp.where(lower, arriving[i], backward[i] + carried)))

        def ahead(zz, state):
            state = cascade(state, f_ref[x, zz])
            for i in range(POISSON):
                u_ref[i, zz] = state[i]
            return state

        lax.fori_loop(0, HALF, ahead, tuple(onward), unroll=8)
        end = cascade([u_ref[i, HALF - 1] for i in range(POISSON)], f_ref[x, HALF])
        for i in range(POISSON):
            u_ref[i, HALF] = end[i]

        def mix(zz, state):
            both = [f_ref[x, zz]] + [u_ref[i, zz] + state[i] for i in range(POISSON)]
            for power in range(POISSON):
                total = MIXES[power][0] * both[0]
                for i in range(1, power + 2):
                    total = total + MIXES[power][i] * both[i]
                q_ref[power, x, zz] = total

        mix(HALF, back)

        def behind(t, state):
            zz = HALF - 1 - t
            state = cascade(state, f_ref[x, zz])
            mix(zz, state)
            return state

        lax.fori_loop(0, HALF, behind, tuple(back), unroll=8)
        return 0

    lax.fori_loop(0, 11, solve, 0)
    for power in (2, 1, 0):

        def apply(zz, _, power=power):
            edge = 2 - power
            layers = {x: q_ref[power + 1, x, zz] for x in range(edge, 11 - edge)}
            for x in range(edge + 1, 10 - edge if power else 8):
                beside = 4.0 * (layers[x - 1] + layers[x + 1]) + either_side(layers[x])
                if x < 3:
                    beside = mask_left * beside
                if x > 6:
                    beside = mask_right * beside
                q_ref[power, x, zz] = q_ref[power, x, zz] + beside
            return 0

        lax.fori_loop(0, HALF + 1, apply, 0, unroll=11)

    def correct(m, _):
        for x in range(4):
            pair = []
            for zz in (2 * m, 2 * m + 1):
                centre = q_ref[0, x + 3, zz]
                pair.append(
                    (
                        v_ref[0, x, zz] - 2.0 * (q_ref[0, x + 4, zz] - centre),
                        v_ref[1, x, zz] - (above(centre) - centre),
                        v_ref[2, x, zz] - (q_ref[0, x + 3, zz + 1] - centre),
                    )
                )
            for component in range(3):
                first, second = pair[0][component], pair[1][component]
                early = jnp.where(lower, first, swap(second))
                late = jnp.where(lower, swap(first), second)
                for tile in range(2):
                    row = (component * 64 + 2 * m) * 32 + tile * 4 + x
                    lanes = slice(tile * 128, tile * 128 + 128)
                    solved_ref[pl.ds(row, 8, stride=8), :] = early[:, lanes]
                    solved_ref[pl.ds(row + 1024, 8, stride=8), :] = late[:, lanes]
        return 0

    lax.fori_loop(0, 16, correct, 0, unroll=2)
    couples = [(i, j) for i in range(4) for j in range(i, 4)]

    def update(block, sums):
        columns = []
        for i in range(4):
            rows = pl.ds(pl.multiple_of(block * 32 + 8 * i, 8), 8)
            cells = factor_ref[rows, :] + (2.0 * shift) * solved_ref[rows, :]
            nf_ref[rows, :] = cells
            columns.append(cells)
        return tuple(s + columns[i] * columns[j] for s, (i, j) in zip(sums, couples))

    sums = (jnp.zeros((8, 128), jnp.float32),) * len(couples)
    copies = []
    for part in range(4):
        sums = lax.fori_loop(part * 48, part * 48 + 48, update, sums, unroll=4)
        rows = pl.ds(part * 1536, 1536)
        copies.append(pltpu.make_async_copy(nf_ref.at[rows], nf_hbm.at[rows], sent.at[part]))
        copies[-1].start()
    t_ref[...] = jnp.zeros((32, 128), jnp.float32)
    for total, (i, j) in zip(sums, couples):
        t_ref[4 * i + j : 4 * i + j + 1, :] = jnp.sum(total, axis=0, keepdims=True)
    lanes = lax.broadcasted_iota(jnp.int32, (1, 128), 1)
    for sensor in range(4):
        component = cells_ref[sensor, 0]
        z = cells_ref[sensor, 1] - span * 64
        x = cells_ref[sensor, 2] - stream * 4
        y = cells_ref[sensor, 3]
        held = (z >= 0) & (z < 64) & (x >= 0) & (x < 4)
        z = jnp.clip(z, 0, 63)
        x = jnp.clip(x, 0, 3)
        tile = jnp.where(y >= 128, 1, 0)
        lane = jnp.where(held, y - 128 * tile, -1)
        for column in range(4):
            row = (component * 64 + z) * 32 + column * 8 + tile * 4 + x
            cells = solved_ref[pl.ds(row, 1), :]
            at = 16 + 4 * sensor + column
            t_ref[at : at + 1, :] = jnp.where(lanes == lane, cells, 0.0)
    totals = jnp.sum(t_ref[...], axis=1, keepdims=True)
    spread = lax.broadcasted_iota(jnp.int32, (32, 128), 1) == lax.broadcasted_iota(jnp.int32, (32, 128), 0)
    sums_ref[...] = jnp.sum(jnp.where(spread, totals, 0.0), axis=0, keepdims=True)
    for copy in copies:
        copy.wait()


def gain_kernel(index_ref, sums_ref, gain_ref, solved_ref, out_hbm, gram_ref, out_ref, sent):
    totals = jnp.sum(sums_ref[...], axis=0, keepdims=True)
    lanes = lax.broadcasted_iota(jnp.int32, (1, 128), 1)
    shift = shift_of(index_ref)

    def entry(at):
        return jnp.sum(jnp.where(lanes == at, totals, 0.0), axis=1, keepdims=True)

    table = [
        [jnp.broadcast_to(2.0 * shift * entry(16 + 4 * i + j), (8, 128)) for j in range(4)] for i in range(4)
    ]

    def body(block, _):
        rows = [pl.ds(pl.multiple_of(block * 32 + 8 * j, 8), 8) for j in range(4)]
        columns = [solved_ref[rows[j], :] for j in range(4)]
        for i in range(4):
            total = gain_ref[rows[i], :]
            for j in range(4):
                total = total + table[i][j] * columns[j]
            out_ref[rows[i], :] = total
        return 0

    copies = []
    for part in range(6):
        lax.fori_loop(part * 32, part * 32 + 32, body, 0, unroll=4)
        rows = pl.ds(part * 1024, 1024)
        copies.append(pltpu.make_async_copy(out_ref.at[rows], out_hbm.at[rows], sent.at[part]))
        copies[-1].start()
    row = lax.broadcasted_iota(jnp.int32, (4, 4), 0)
    column = lax.broadcasted_iota(jnp.int32, (4, 4), 1)
    gram = jnp.zeros((4, 4), jnp.float32)
    for i in range(4):
        for j in range(4):
            value = entry(4 * min(i, j) + max(i, j)) / 6291456.0
            gram = gram + jnp.where((row == i) & (column == j), value, 0.0)
    gram_ref[...] = gram
    for copy in copies:
        copy.wait()


def call(kernel, outputs, scratch, operands, smalls, flops, far_in=(), far_out=(), signals=(), least=0):
    arrays = [jax.ShapeDtypeStruct(shape, jnp.float32) for shape in outputs]
    places = [pl.BlockSpec(memory_space=pltpu.SMEM)] * smalls
    places += [pl.BlockSpec(memory_space=pltpu.VMEM)] * (len(operands) - smalls)
    results = [pl.BlockSpec(memory_space=pltpu.VMEM)] * len(outputs)
    for place in far_in:
        places[place] = pl.BlockSpec(memory_space=pltpu.HBM)
    for place in far_out:
        results[place] = pl.BlockSpec(memory_space=pltpu.HBM)
    room = sum(4 * math.prod(shape) for shape in scratch) + (2 << 20)
    moved = sum(4 * math.prod(shape) for shape in outputs) + sum(4 * math.prod(o.shape) for o in operands)
    return pl.pallas_call(
        kernel,
        out_shape=arrays,
        in_specs=places,
        out_specs=results,
        scratch_shapes=[pltpu.VMEM(shape, jnp.float32) for shape in scratch]
        + [pltpu.SemaphoreType.DMA((count,)) for count in signals],
        compiler_params=pltpu.CompilerParams(vmem_limit_bytes=(24 if len(scratch) > 1 else 12 if scratch else 4) << 20),
        cost_estimate=pl.CostEstimate(flops=flops, bytes_accessed=moved, transcendentals=0),
    )(*operands)


def to_rows(cells):
    head = cells.shape[:-2]
    order = tuple(range(len(head)))
    split = cells.reshape(*head, 4, 2, 128).transpose(*order, len(head) + 1, len(head), len(head) + 2)
    return split.reshape(-1, 128)


def from_rows(rows, head):
    order = tuple(range(len(head)))
    split = rows.reshape(*head, 2, 4, 128).transpose(*order, len(head) + 1, len(head), len(head) + 2)
    return split.reshape(*head, 4, 256)


def mixed(table, states):
    table = np.asarray(table).astype(np.float32)
    return jnp.stack(
        [sum(float(table[i, k]) * states[k] for k in range(i + 1)) for i in range(POISSON)]
    )


def ring_states(states, partner, own_even, far):
    upper = jnp.arange(8)[None, None, :, None] >= 4
    first = upper == own_even
    nearer = jnp.where(first, partner, states)
    farther = jnp.where(first, states, partner)
    joined = nearer[:POISSON] + mixed(WHOLE_TABLE, farther[:POISSON])
    other = lax.ppermute(jnp.concatenate([joined, states[POISSON:]]), "gz", far)
    square = WHOLE_TABLE @ WHOLE_TABLE
    cube = square @ WHOLE_TABLE
    around = np.linalg.inv(np.eye(POISSON) - square @ square)
    entering = jnp.where(
        first[0],
        other[:POISSON] + mixed(square, partner[:POISSON]),
        partner[:POISSON] + mixed(WHOLE_TABLE, other[:POISSON]),
    )
    entering = entering + mixed(cube, states[:POISSON])
    entering = mixed(around, entering)
    ahead = jnp.where(own_even, partner[POISSON:], other[POISSON:])
    return jnp.concatenate([entering, ahead])


def fast_shards(factor, gain, base_flow, shift_index, sensor_cells):
    swap_in = [(0, 1), (1, 0), (2, 3), (3, 2), (4, 5), (5, 4), (6, 7), (7, 6)]
    swap_out = [(1, 2), (2, 1), (3, 4), (4, 3), (5, 6), (6, 5)]
    send_round = [(1, 2), (2, 1), (5, 6), (6, 5), (3, 7), (4, 0)]
    forward_round = [(7, 4), (0, 3)]
    near = [(0, 1), (1, 0), (2, 3), (3, 2)]
    far = [(1, 2), (2, 1), (3, 0), (0, 3)]
    odd = lax.axis_index("gx") % 2
    own_even = lax.axis_index("gz") % 2 == 0
    factor_rows = to_rows(factor)
    base_rows = to_rows(base_flow)
    gain_rows = to_rows(gain)
    cell = (8, 256)
    own, a, b1, b2, z1, z2 = call(
        pack_kernel,
        [(3, 4, HALF, *cell), (312, *cell), (PART, *cell), (312 - PART, *cell), (26, *cell), (26, *cell)],
        [factor_rows.shape], [factor_rows, base_rows], 0, 10**6, far_in=(0,), signals=(3,),
    )
    b1_in = lax.ppermute(b1, "gx", send_round)
    z1 = lax.ppermute(z1, "gz", near)
    z2 = lax.ppermute(z2, "gz", far)
    b2_in = lax.ppermute(b2, "gx", swap_out)
    a_in = lax.ppermute(a, "gx", swap_in)
    corners = len(CORNERS) + 3
    ca, cb = call(corner_kernel, [(corners, *cell)] * 2, [], [z1, z2], 0, 10**5)
    ca = lax.ppermute(ca, "gx", swap_in)
    cb = lax.ppermute(cb, "gx", swap_out)
    b1_in, z1, z2 = lax.optimization_barrier((b1_in, z1, z2))
    b3_in = lax.ppermute(b1_in, "gx", forward_round)
    block = (10, 39, *cell)
    scratch = [(10, 80, 256)] + [block] * 5
    handed = call(
        functools.partial(velocity_kernel, "early"),
        [(3, 2, 39, *cell), (3, 2, 39, *cell), (3, HALF + 1, *cell)],
        scratch, [shift_index, own, base_rows, a_in, ca, z1, z2], 1, 10**8,
    )
    velocity, sides, states, pa, pb1, pb2 = call(
        functools.partial(velocity_kernel, "late"),
        [(3, 4, HALF, *cell), (5, HALF, *cell), (POISSON + 1, 5, *cell), (4, HALF, *cell)]
        + [(2, HALF, *cell)] * 2,
        scratch,
        [shift_index, own, base_rows, b1_in, b3_in, b2_in, cb, z1, z2, *handed], 1, 10**8,
    )
    pb1_in = lax.ppermute(pb1, "gx", send_round)
    pb2_in = lax.ppermute(pb2, "gx", swap_out)
    partner = lax.ppermute(states, "gz", near)
    pb1_in, partner = lax.optimization_barrier((pb1_in, partner))
    pa_in = lax.ppermute(pa, "gx", swap_in)
    pb3_in = lax.ppermute(pb1_in, "gx", forward_round)
    entering = ring_states(states, partner, own_even, far)
    enter_b = lax.ppermute(lax.dynamic_slice_in_dim(entering, odd, 4, axis=1), "gx", swap_out)
    enter_a = lax.ppermute(lax.dynamic_slice_in_dim(entering, 1 - odd, 4, axis=1), "gx", swap_in)
    block = (11, HALF + 1, *cell)
    new_rows, solved, sums = call(
        pressure_kernel,
        [factor_rows.shape, factor_rows.shape, (1, 128)],
        [block, (POISSON + 1, 11, *cell), (POISSON, HALF + 1, *cell), (POISSON, *block), (32, 128)]
        + [factor_rows.shape],
        [shift_index, sensor_cells, velocity, sides, pa_in, pb1_in, pb3_in, pb2_in]
        + [entering, enter_a, enter_b, factor_rows],
        2, 10**8, far_out=(0,), signals=(4,),
    )
    devices = lax.axis_size("gx") * lax.axis_size("gz")
    shared = lax.all_to_all(
        jnp.broadcast_to(sums[None], (devices, 1, 128)), ("gx", "gz"), split_axis=0, concat_axis=0, tiled=True
    )
    new_gain, gram = call(
        gain_kernel,
        [gain_rows.shape, (4, 4)],
        [gain_rows.shape], [shift_index, shared.reshape(devices, 128), gain_rows, solved], 1, 10**7,
        far_out=(0,), signals=(6,),
    )
    head = factor.shape[:3]
    return (from_rows(new_rows, head), from_rows(new_gain, head), gram)


def solution(mesh):
    placed = (
        P(None, "gz", None, "gx", None),
        P(None, "gz", None, "gx", None),
        P("gz", "gx", None),
        P(),
        P(),
    )
    fits = mesh.shape["gx"] == 8 and mesh.shape["gz"] == 4
    return jax.shard_map(
        fast_shards if fits else shards,
        mesh=mesh,
        in_specs=placed,
        out_specs=(P(None, "gz", None, "gx", None), P(None, "gz", None, "gx", None), P()),
        check_vma=False,
    )
```

```python
import functools
import math

import jax
import jax.numpy as jnp
import numpy as np
from jax import lax
from jax.experimental import pallas as pl
from jax.experimental.pallas import tpu as pltpu
from jax.sharding import PartitionSpec as P

SWEEPS = 3
POISSON = 4
SHIFTS = 8


viscosity = 0.4
shift_table = (0.6, 0.8, 1.0, 1.25, 1.6, 2.0, 2.5, 3.2)
chebyshev_weights = (1.0 / 1.9352976, 1.0 / 1.4752809, 1.0 / 0.8247191, 1.0 / 0.3647024)
highest = lax.Precision.HIGHEST


def padded_2(cells, sides, width, closed):
    for axis, dim in sides:
        count = lax.axis_size(axis)
        ends = count if closed else count - 1
        head = lax.slice_in_dim(cells, 0, width, axis=dim)
        tail = lax.slice_in_dim(cells, cells.shape[dim] - width, cells.shape[dim], axis=dim)
        cells = jnp.concatenate(
            [
                lax.ppermute(tail, axis, [(i, (i + 1) % count) for i in range(ends)]),
                cells,
                lax.ppermute(head, axis, [((i + 1) % count, i) for i in range(ends)]),
            ],
            axis=dim,
        )
    return cells


def around_sum(padded):
    summed = padded[:, 1:-1, :, 2:, 1:-1] + padded[:, 1:-1, :, :-2, 1:-1]
    summed = summed + padded[:, 1:-1, :, 1:-1, 2:] + padded[:, 1:-1, :, 1:-1, :-2]
    return summed + padded[:, 2:, :, 1:-1, 1:-1] + padded[:, :-2, :, 1:-1, 1:-1]


def shards(factor, gain, base_flow, shift_index, sensor_cells):
    components, span_cells, columns, stream_cells, normal_cells = factor.shape
    stream_start = lax.axis_index("gx") * stream_cells
    span_start = lax.axis_index("gz") * span_cells
    stream_total = stream_cells * lax.axis_size("gx")
    span_total = span_cells * lax.axis_size("gz")
    shift_values = jnp.asarray(shift_table, jnp.float32)
    shift_value = jnp.sum(jnp.where(jnp.arange(SHIFTS) == shift_index[0], shift_values, 0.0))
    base_field = base_flow[None, :, None, :, :]
    diagonal = shift_value + 6.0 * viscosity + base_field
    source = -factor

    def stream_inside(extent, margin):
        positions = stream_start - margin + jnp.arange(extent)
        return ((positions >= 0) & (positions < stream_total)).astype(jnp.float32)

    def extend(grid_field):
        padded = padded_2(grid_field, (("gx", 3), ("gz", 1)), 1, True)
        padded = padded * stream_inside(stream_cells + 2, 1)[None, None, None, :, None]
        return jnp.pad(padded, ((0, 0), (0, 0), (0, 0), (0, 0), (1, 1)))

    velocity = source / diagonal
    for sweep_index in range(SWEEPS):
        padded = extend(velocity)
        velocity = (
            source + viscosity * around_sum(padded) + base_field * padded[:, 1:-1, :, :-2, 1:-1]
        ) / diagonal
    padded = extend(velocity)
    divergence = 2.0 * (velocity[0] - padded[0, 1:-1, :, :-2, 1:-1])
    divergence = divergence + (velocity[1] - padded[1, 1:-1, :, 1:-1, :-2])
    divergence = divergence + (velocity[2] - padded[2, :-2, :, 1:-1, 1:-1])
    span_index = jnp.arange(span_total)
    products = span_index[:, None] * span_index[None, :] % span_total
    angles = 2.0 * math.pi * products.astype(jnp.float32) / span_total
    hartley_table = (jnp.cos(angles) + jnp.sin(angles)) / math.sqrt(span_total)

    def turn_modes(exchanged):
        turned = jnp.einsum("kz,zay->kay", hartley_table, exchanged, precision=highest)
        return lax.all_to_all(turned, "gz", split_axis=0, concat_axis=1, tiled=True)

    def transform(grid_field):
        flat = grid_field.reshape(span_cells, columns * stream_cells, normal_cells)
        result = turn_modes(lax.all_to_all(flat, "gz", split_axis=1, concat_axis=0, tiled=True))
        return result.reshape(span_cells, columns, stream_cells, normal_cells)

    modes_rhs = -transform(divergence)
    wave_index = span_start + jnp.arange(span_cells)
    wavenumber = 2.0 * math.pi * wave_index.astype(jnp.float32) / span_total
    mode_diagonal = (10.0 + (2.0 - 2.0 * jnp.cos(wavenumber)))[:, None, None, None]
    pressure = chebyshev_weights[0] * modes_rhs / mode_diagonal
    for sweep_level in range(1, POISSON):
        padded = padded_2(pressure, (("gx", 2),), 1, False)
        padded = jnp.pad(padded, ((0, 0), (0, 0), (0, 0), (1, 1)))
        beside_all = (
            4.0 * (padded[:, :, 2:, 1:-1] + padded[:, :, :-2, 1:-1])
            + padded[:, :, 1:-1, 2:]
            + padded[:, :, 1:-1, :-2]
        )
        pressure = (
            pressure
            + chebyshev_weights[sweep_level]
            * (modes_rhs - (mode_diagonal * pressure - beside_all))
            / mode_diagonal
        )
    pressure = transform(pressure)
    padded = extend(pressure[None])[0]
    gradient = jnp.stack(
        [
            2.0 * (padded[1:-1, :, 2:, 1:-1] - pressure),
            padded[1:-1, :, 1:-1, 2:] - pressure,
            padded[2:, :, 1:-1, 1:-1] - pressure,
        ]
    )
    solved = velocity - gradient
    span_ids = span_start + jnp.arange(span_cells)
    stream_ids = stream_start + jnp.arange(stream_cells)
    normal_ids = jnp.arange(normal_cells)
    located = span_ids[None, :, None, None] == sensor_cells[:, 1][:, None, None, None]
    located = located & (stream_ids[None, None, :, None] == sensor_cells[:, 2][:, None, None, None])
    located = located & (normal_ids[None, None, None, :] == sensor_cells[:, 3][:, None, None, None])
    picked = jnp.einsum("szxy,czjxy->scj", located.astype(jnp.float32), solved, precision=highest)
    chooser = (jnp.arange(3)[None, :] == sensor_cells[:, 0:1]).astype(jnp.float32)
    readout_local = jnp.sum(picked * chooser[:, :, None], axis=1)
    new_factor = factor + 2.0 * shift_value * solved
    gram_local = jnp.einsum("czixy,czjxy->ij", new_factor, new_factor, precision=highest)
    gram_total, readout = lax.psum((gram_local, readout_local), ("gx", "gz"))
    gram = gram_total / (3.0 * stream_total * normal_cells * span_total)
    new_gain = gain + 2.0 * shift_value * jnp.einsum(
        "czjxy,ij->czixy", solved, readout, precision=highest
    )
    return (new_factor, new_gain, gram)


HALF = 32
PAIRS = 8


def recurrence_tables(centre, weights):
    ratio = centre / 2.0 - math.sqrt(centre * centre / 4.0 - 1.0)
    order = len(weights)
    step = ratio * np.tril(np.ones((order, order)))
    half = np.linalg.matrix_power(step, HALF)
    whole = np.linalg.matrix_power(step, 2 * HALF)
    angles = 2.0 * np.pi * np.arange(4096) / 4096
    series = [weights[0]]
    for weight in weights[1:]:
        longer = [0.0] + [weight * entry for entry in series]
        for place, entry in enumerate(series):
            longer[place] += (1.0 - weight) * entry
        longer[0] += weight
        series = longer
    mixes = []
    for power in range(1, order + 1):
        symbol = 1.0 / (centre - 2.0 * np.cos(angles)) ** power
        kernel = [np.mean(symbol * np.cos(angles * n)) for n in range(order + 1)]
        matrix = [[math.comb(n + i - 1, i - 1) for i in range(1, power + 1)] for n in range(1, power + 1)]
        sides = np.linalg.solve(
            np.array(matrix, np.float64), [kernel[n] / ratio**n for n in range(1, power + 1)]
        )
        middle = kernel[0] - 2.0 * np.sum(sides)
        mixes.append([float(series[power - 1] * entry) for entry in [middle, *sides]])
    square = whole @ whole
    around = np.linalg.inv(np.eye(order) - square @ square)
    wholes = [table.tolist() for table in (whole, square, square @ whole, around)]
    return float(ratio), half.tolist(), wholes, mixes


RATIO, HALF_TABLE, WHOLE_TABLES, MIXES = recurrence_tables(12.0, chebyshev_weights)


def lower_half():
    return lax.broadcasted_iota(jnp.int32, (8, 256), 0) < 4


def swap(cells):
    return pltpu.roll(cells, 4, 0)


def below(cells):
    lanes = lax.broadcasted_iota(jnp.int32, (8, 128), 1)
    low, high = pltpu.roll(cells[:, :128], 1, 1), pltpu.roll(cells[:, 128:], 1, 1)
    return jnp.concatenate([jnp.where(lanes > 0, low, 0.0), jnp.where(lanes > 0, high, low)], axis=1)


def above(cells):
    lanes = lax.broadcasted_iota(jnp.int32, (8, 128), 1)
    low, high = pltpu.roll(cells[:, :128], 127, 1), pltpu.roll(cells[:, 128:], 127, 1)
    return jnp.concatenate([jnp.where(lanes < 127, low, high), jnp.where(lanes < 127, high, 0.0)], axis=1)


def either_side(cells):
    lanes = lax.broadcasted_iota(jnp.int32, (8, 128), 1)
    low, high = cells[:, :128], cells[:, 128:]
    low_up, high_up = pltpu.roll(low, 1, 1), pltpu.roll(high, 1, 1)
    low_down, high_down = pltpu.roll(low, 127, 1), pltpu.roll(high, 127, 1)
    first = jnp.where(lanes > 0, low_up, 0.0) + jnp.where(lanes < 127, low_down, high_down)
    second = jnp.where(lanes > 0, high_up, low_up) + jnp.where(lanes < 127, high_down, 0.0)
    return jnp.concatenate([first, second], axis=1)


def shift_of(index_ref):
    index = index_ref[0]
    value = jnp.float32(shift_table[0])
    for place in range(1, SHIFTS):
        value = jnp.where(index == place, jnp.float32(shift_table[place]), value)
    return value


def x_odd():
    return lax.rem(lax.axis_index("gx"), 2)


def z_even():
    return lax.rem(lax.axis_index("gz"), 2) == 0


def cascade(state, cells):
    grown = []
    for entry in state:
        cells = RATIO * entry + cells
        grown.append(cells)
    return tuple(grown)


def half_states(read):
    zero = jnp.zeros((8, 256), jnp.float32)

    def body(t, carry):
        forward, backward = carry
        return cascade(forward, read(t)), cascade(backward, read(HALF - 1 - t))

    return lax.fori_loop(0, HALF, body, ((zero,) * POISSON, (zero,) * POISSON), unroll=HALF)


def turned(table, states, row):
    total = None
    for column in range(row + 1):
        term = table[row][column] * states[column]
        total = term if total is None else total + term
    return total


FACTOR_AT = 24
PART = 152
CORNERS = [(c, dx, side, 0) for c in range(3) for dx in (1, 2) for side in (0, 1)]
CORNERS += [(2, 1, 0, 1), (2, 3, 0, 0)]


def pack_kernel(factor_hbm, base_ref, own_ref, a_ref, b1_ref, b2_ref, z1_ref, z2_ref, factor_ref, arrived):
    share = factor_ref.shape[0] // 3
    copies = []
    for component in range(3):
        rows = pl.ds(component * share, share)
        copies.append(
            pltpu.make_async_copy(factor_hbm.at[rows], factor_ref.at[rows], arrived.at[component])
        )
        copies[-1].start()
    odd = x_odd()
    even = 1 - odd
    low = lax.broadcasted_iota(jnp.int32, (8, 128), 0) < 4
    scale = -1.0 / viscosity
    for component in range(3):

        def load(m, _, component=component):
            for x in range(4):
                for tile in range(2):
                    row = (component * 64 + 2 * m) * 32 + tile * 4 + x
                    first = factor_ref[pl.ds(row, 8, stride=8), :] * scale
                    second = factor_ref[pl.ds(row + 1024, 8, stride=8), :] * scale
                    lanes = slice(tile * 128, tile * 128 + 128)
                    own_ref[component, x, 2 * m, :, lanes] = jnp.where(low, first, swap(second))
                    own_ref[component, x, 2 * m + 1, :, lanes] = jnp.where(low, swap(first), second)
            return 0

        copies[component].wait()
        lax.fori_loop(0, 16, load, 0, unroll=2)

    def edges(zz, _):
        for component in range(3):
            for layer in range(3):
                at = FACTOR_AT + (component * 3 + layer) * HALF
                a_ref[at + zz] = own_ref[component, layer + even, zz]
                cells = own_ref[component, layer + odd, zz]
                if at < PART:
                    b1_ref[at + zz] = cells
                else:
                    b2_ref[at - PART + zz] = cells
        return 0

    lax.fori_loop(0, HALF, edges, 0, unroll=2)
    for layer in range(3):
        for group in range(8):
            for tile in range(2):
                lanes = slice(tile * 128, tile * 128 + 128)
                row = group * 64 + tile * 4 + layer
                a_ref[layer * 8 + group, :, lanes] = base_ref[pl.ds(row + even, 8, stride=8), :]
                b1_ref[layer * 8 + group, :, lanes] = base_ref[pl.ds(row + odd, 8, stride=8), :]
    lower = lower_half()
    rightward = z_even()
    for component in range(3):
        for x in range(4):
            for pair in range(2):
                cells = lambda zz: own_ref[component, x, zz]
                up = jnp.where(lower, swap(cells(31 - 2 * pair)), cells(30 - 2 * pair))
                down = jnp.where(lower, cells(2 * pair), swap(cells(2 * pair + 1)))
                at = (component * 4 + x) * 2 + pair
                z1_ref[at] = jnp.where(rightward, up, down)
                z2_ref[at] = jnp.where(rightward, down, up)
    for k in range(4):
        for tile in range(2):
            lanes = slice(tile * 128, tile * 128 + 128)
            up = base_ref[(63 - k) * 8 + tile * 4 : (63 - k) * 8 + tile * 4 + 4, :]
            down = base_ref[k * 8 + tile * 4 : k * 8 + tile * 4 + 4, :]
            rows = slice((k % 2) * 4, (k % 2) * 4 + 4)
            z1_ref[24 + k // 2, rows, lanes] = jnp.where(rightward, up, down)
            z2_ref[24 + k // 2, rows, lanes] = jnp.where(rightward, down, up)


def corner_kernel(z1_ref, z2_ref, a_ref, b_ref):
    odd = x_odd()
    rightward = z_even()

    def fill(behind_ref, ahead_ref):
        for place, (component, dx, side, pair) in enumerate(CORNERS):
            source = (behind_ref, ahead_ref)[side]
            right_x = 4 - dx
            left_x = dx - 1
            a_x = jnp.where(odd == 1, left_x, right_x)
            b_x = jnp.where(odd == 1, right_x, left_x)
            a_ref[place] = source[(component * 4 + a_x) * 2 + pair]
            b_ref[place] = source[(component * 4 + b_x) * 2 + pair]
        for dx in (1, 2, 3):
            for k in range(4):
                for side, source in enumerate((behind_ref, ahead_ref)):
                    from_right = source[24 + k // 2, (k % 2) * 4 + 4 - dx, :]
                    from_left = source[24 + k // 2, (k % 2) * 4 + dx - 1, :]
                    at = len(CORNERS) + dx - 1
                    a_ref[at, side * 4 + k, :] = jnp.where(odd == 1, from_left, from_right)
                    b_ref[at, side * 4 + k, :] = jnp.where(odd == 1, from_right, from_left)

    @pl.when(rightward)
    def _():
        fill(z2_ref, z1_ref)

    @pl.when(jnp.logical_not(rightward))
    def _():
        fill(z1_ref, z2_ref)


KNOWN = {("early", 0): (3, 9), ("early", 1): (0, 6), ("late", 0): (0, 5), ("late", 1): (4, 9)}
SWEPT = {
    ("early", 0): ((4, 8), (5, 7), (6, 6)),
    ("early", 1): ((1, 5), (2, 4), (3, 3)),
    ("late", 0): ((1, 3), (2, 4), (3, 5)),
    ("late", 1): ((6, 8), (5, 7), (4, 6)),
}
HANDED = (((4, 5), (5, 6), 6), ((4, 5), (3, 4), 3))


def velocity_kernel(stage, *refs):
    early = stage == "early"
    if early:
        index_ref, own_ref, base_ref, a_ref, c_ref, z1_ref, z2_ref, *refs = refs
        h1_ref, h2_ref, h3_ref, *refs = refs
    else:
        index_ref, own_ref, base_ref, b1_ref, b3_ref, b2_ref, c_ref, z1_ref, z2_ref, *refs = refs
        h1_ref, h2_ref, h3_ref, v_ref, bw_ref, s_ref, pa_ref, pb1_ref, pb2_ref, *refs = refs
    flow_ref, a1_ref, r_ref, v0_ref, va_ref, vb_ref = refs
    odd = x_odd()
    stream = lax.axis_index("gx")
    last = lax.axis_size("gx") - 1
    mask_left = jnp.where(stream > 0, 1.0, 0.0)
    mask_right = jnp.where(stream < last, 1.0, 0.0)
    relayed = jnp.logical_or(stream == 3, stream == 4)
    rightward = z_even()
    lower = lower_half()
    shift = shift_of(index_ref)
    zero = jnp.zeros((8, 256), jnp.float32)

    def each_z(step):
        @pl.when(rightward)
        def _():
            step(z2_ref, z1_ref)

        @pl.when(jnp.logical_not(rightward))
        def _():
            step(z1_ref, z2_ref)

    def inside(at):
        return lambda zz: a_ref[at + zz]

    def outside(first_ref):
        def pick(at):
            if at < PART:
                return lambda zz: first_ref[at + zz]
            return lambda zz: b2_ref[at - PART + zz]

        return pick

    def each_x(step):
        if early:
            step(inside)
            return

        @pl.when(relayed)
        def _():
            step(outside(b3_ref))

        @pl.when(jnp.logical_not(relayed))
        def _():
            step(outside(b1_ref))

    def before(cells, halo, k):
        if k % 2 == 0:
            return jnp.where(lower, halo, swap(cells))
        return swap(jnp.where(lower, cells, halo))

    def after(cells, halo, k):
        if k % 2 == 0:
            return swap(jnp.where(lower, halo, cells))
        return jnp.where(lower, swap(cells), halo)

    def run(parity):
        low, high = KNOWN[stage, parity]
        own_layers = [x for x in range(4) if low <= x + 3 <= high]
        if low < 3:
            halo = [(dx, 3 - dx, 3 - dx) for dx in (1, 2, 3)]
        else:
            halo = [(dx, 6 + dx, dx - 1) for dx in (1, 2, 3)]

        for x in own_layers:
            for group in range(8):
                for tile in range(2):
                    lanes = slice(tile * 128, tile * 128 + 128)
                    flow_ref[x + 3, 8 + 8 * group : 16 + 8 * group, lanes] = base_ref[
                        pl.ds(group * 64 + tile * 4 + x, 8, stride=8), :
                    ]

        def flow_span(behind_ref, ahead_ref):
            for x in own_layers:
                for k in range(4):
                    at = 24 + k // 2
                    row = (k % 2) * 4 + x
                    flow_ref[x + 3, 7 - k, :] = behind_ref[at, row, :]
                    flow_ref[x + 3, 72 + k, :] = ahead_ref[at, row, :]

        each_z(flow_span)

        def flow_stream(pick):
            for dx, place, layer in halo:
                for group in range(8):
                    flow_ref[place, 8 + 8 * group : 16 + 8 * group, :] = pick(layer * 8)(group)
                for k in range(4):
                    flow_ref[place, 7 - k, :] = c_ref[len(CORNERS) + dx - 1, k, :]
                    flow_ref[place, 72 + k, :] = c_ref[len(CORNERS) + dx - 1, 4 + k, :]

        each_x(flow_stream)

        def coefficients(zz, _):
            for x in range(low, high + 1):
                first = jnp.broadcast_to(flow_ref[x, pl.ds(zz + 4, 1), :], (8, 256))
                second = jnp.broadcast_to(flow_ref[x, pl.ds(zz + 36, 1), :], (8, 256))
                flow = jnp.where(lower, first, second)
                scale = viscosity * (mask_left if x < 3 else mask_right if x > 6 else 1.0)
                a1_ref[x - low, zz] = scale / (shift + 6.0 * viscosity + flow)
                r_ref[x - low, zz] = 1.0 + flow * (1.0 / viscosity)
            return 0

        lax.fori_loop(0, 39, coefficients, 0, unroll=3)
        for _, place, _ in halo:
            for zz in (0, 1, 2, 3, 36, 37, 38):
                v0_ref[place - low, zz] = zero

        def swept(source, span, zz, depth):
            result = {}
            first, final = span
            behind = [source(first - 1, zz + k) for k in range(depth)]
            here = [source(first, zz + k - 1) for k in range(depth + 2)]
            for x in range(first, final + 1):
                if x < final:
                    ahead = [source(x + 1, zz + k - 1) for k in range(depth + 2)]
                else:
                    ahead = [None] + [source(x + 1, zz + k) for k in range(depth)]
                result[x] = []
                for k in range(depth):
                    total = ahead[k + 1] + either_side(here[k + 1])
                    total = total + (here[k] + here[k + 2])
                    total = total + r_ref[x - low, zz + k] * behind[k]
                    result[x].append(v0_ref[x - low, zz + k] + a1_ref[x - low, zz + k] * total)
                behind, here = here[1 : depth + 1], ahead
            return result

        def sweep(source, target, level, margin, hand):
            depth = 4
            first, extent = 3 - margin, 33 + 2 * margin

            def body(t, _):
                zz = first + jnp.minimum(t * depth, extent - depth)
                for x, column in swept(source, SWEPT[stage, parity][level], zz, depth).items():
                    for k, cells in enumerate(column):
                        if target is not None:
                            target[x - low, zz + k] = cells
                        hand(x, zz + k, cells)
                return 0

            lax.fori_loop(0, -(-extent // depth), body, 0, unroll=2)

        handed_first, handed_second, handed_third = HANDED[parity]
        for component in range(3):

            def interior(zz, _, component=component):
                for x in own_layers:
                    v0_ref[x + 3 - low, zz + 4] = own_ref[component, x, zz] * a1_ref[x + 3 - low, zz + 4]
                return 0

            lax.fori_loop(0, HALF, interior, 0, unroll=4)

            def span(behind_ref, ahead_ref, component=component):
                for x in own_layers:
                    at = (component * 4 + x) * 2
                    for k in range(4):
                        cells = before(own_ref[component, x, 31 - k], behind_ref[at + k // 2], k)
                        v0_ref[x + 3 - low, 3 - k] = cells * a1_ref[x + 3 - low, 3 - k]
                    for k in range(3):
                        cells = after(own_ref[component, x, k], ahead_ref[at + k // 2], k)
                        v0_ref[x + 3 - low, 36 + k] = cells * a1_ref[x + 3 - low, 36 + k]

            each_z(span)

            def sides(pick, component=component):
                for dx, place, layer in halo:
                    read = pick(FACTOR_AT + (component * 3 + layer) * HALF)

                    def body(zz, _, read=read, place=place):
                        v0_ref[place - low, zz + 4] = read(zz) * a1_ref[place - low, zz + 4]
                        return 0

                    lax.fori_loop(0, HALF, body, 0, unroll=4)
                    for entry, (c, away, side, pair) in enumerate(CORNERS):
                        if c != component or away != dx:
                            continue
                        for k in (2 * pair, 2 * pair + 1):
                            if side == 0:
                                cells = before(read(31 - k), c_ref[entry], k)
                                v0_ref[place - low, 3 - k] = cells * a1_ref[place - low, 3 - k]
                            else:
                                cells = after(read(k), c_ref[entry], k)
                                v0_ref[place - low, 36 + k] = cells * a1_ref[place - low, 36 + k]

            each_x(sides)

            def hand_first(x, zz, cells, component=component):
                if early and x in handed_first:
                    h1_ref[component, handed_first.index(x), zz] = cells

            def hand_second(x, zz, cells, component=component):
                if early and x in handed_second:
                    h2_ref[component, handed_second.index(x), zz] = cells

            def hand_third(x, zz, cells, component=component):
                h3_ref[component, zz - 3] = cells

            def from_first(x, zz, component=component):
                if not early and x in handed_first:
                    return h1_ref[component, handed_first.index(x), zz]
                return va_ref[x - low, zz]

            def from_second(x, zz, component=component):
                if not early and x in handed_second:
                    return h2_ref[component, handed_second.index(x), zz]
                return vb_ref[x - low, zz]

            sweep(lambda x, zz: v0_ref[x - low, zz], va_ref, 0, 2, hand_first)
            sweep(from_first, vb_ref, 1, 1, hand_second)
            if early:
                sweep(from_second, None, 2, 0, hand_third)
                continue

            def finished(zz, depth, component=component):
                found = swept(from_second, SWEPT[stage, parity][2], zz + 4, depth)
                found[handed_third] = [h3_ref[component, zz + 1 + k] for k in range(depth)]
                return [[found[x + 3][k] for x in range(4)] for k in range(depth)]

            def diverge(t, past, component=component):
                for k, cells in enumerate(finished(4 * t, 4)):
                    zz = 4 * t + k
                    for x in range(4):
                        v_ref[component, x, zz] = cells[x]
                        if component == 0:
                            bw_ref[x, zz] = -2.0 * (cells[x] if x == 0 else cells[x] - cells[x - 1])
                        elif component == 1:
                            bw_ref[x, zz] = bw_ref[x, zz] - (cells[x] - below(cells[x]))
                        else:
                            bw_ref[x, zz] = bw_ref[x, zz] - (cells[x] - past[x])
                    if component == 0:
                        bw_ref[4, zz] = cells[3]
                    past = tuple(cells) if component == 2 else 0
                return past

            start = tuple(finished(-1, 1)[0]) if component == 2 else 0
            lax.fori_loop(0, HALF // 4, diverge, start, unroll=2)

    for parity in (0, 1):

        @pl.when(odd == parity)
        def _(parity=parity):
            run(parity)

    if early:
        return

    def edges(zz, _):
        for layer in range(4):
            pa_ref[layer, zz] = bw_ref[layer + 1 - odd, zz]
            (pb1_ref if layer < 2 else pb2_ref)[layer % 2, zz] = bw_ref[layer + odd, zz]
        return 0

    lax.fori_loop(0, HALF, edges, 0, unroll=4)

    def states(layer, _):
        forward, backward = half_states(lambda t: bw_ref[layer, t])
        swapped_forward = [swap(entry) for entry in forward]
        swapped_backward = [swap(entry) for entry in backward]
        for i in range(POISSON):
            onward = forward[i] + turned(HALF_TABLE, swapped_forward, i)
            back = backward[i] + turned(HALF_TABLE, swapped_backward, i)
            s_ref[i, layer] = jnp.where(lower, back, onward)
        s_ref[POISSON, layer] = bw_ref[layer, 0]
        return 0

    lax.fori_loop(0, 5, states, 0)


def pressure_kernel(
    index_ref, cells_ref, v_ref, bw_ref, ba_ref, b1_ref, b3_ref, b2_ref, inc_ref, ia_ref, ib_ref, factor_ref,
    nf_hbm, solved_ref, sums_ref,
    f_ref, i_ref, u_ref, q_ref, t_ref, nf_ref, sent,
):
    odd = x_odd()
    stream = lax.axis_index("gx")
    span = lax.axis_index("gz")
    last = lax.axis_size("gx") - 1
    mask_left = jnp.where(stream > 0, 1.0, 0.0)
    mask_right = jnp.where(stream < last, 1.0, 0.0)
    lower = lower_half()
    shift = shift_of(index_ref)

    def gather(left, right, left_inc, right_inc):
        def body(zz, _):
            for x in range(3):
                f_ref[x, zz] = mask_left * left(x, zz)
                f_ref[x + 4, zz] = bw_ref[x + 1, zz]
                f_ref[x + 8, zz] = mask_right * right(x + 1, zz)
            f_ref[3, zz] = bw_ref[0, zz] + (2.0 * mask_left) * left(3, zz)
            f_ref[7, zz] = mask_right * (right(0, zz) + 2.0 * bw_ref[4, zz])
            return 0

        lax.fori_loop(0, HALF, body, 0, unroll=4)
        for i in range(POISSON + 1):
            for x in range(3):
                i_ref[i, x] = left_inc(i, x)
                i_ref[i, x + 4] = inc_ref[i, x + 1]
                i_ref[i, x + 8] = right_inc(i, x + 1)
            i_ref[i, 3] = inc_ref[i, 0] + 2.0 * left_inc(i, 3)
            i_ref[i, 7] = mask_right * (right_inc(i, 0) + 2.0 * inc_ref[i, 4])
        for x in range(11):
            f_ref[x, HALF] = swap(jnp.where(lower, i_ref[POISSON, x], f_ref[x, 0]))

    def enter_inside(i, layer):
        return ia_ref[i, layer]

    def enter_outside(i, layer):
        return ib_ref[i, layer]

    def inside(layer, zz):
        return ba_ref[layer, zz]

    def direct(layer, zz):
        return b1_ref[layer, zz] if layer < 2 else b2_ref[layer - 2, zz]

    def relayed(layer, zz):
        return b3_ref[layer, zz] if layer < 2 else b2_ref[layer - 2, zz]

    middle = jnp.logical_or(stream == 3, stream == 4)
    for parity in (0, 1):
        for through, outside in ((False, direct), (True, relayed)):

            @pl.when(jnp.logical_and(odd == parity, middle == through))
            def _(parity=parity, outside=outside):
                if parity == 0:
                    gather(outside, inside, enter_outside, enter_inside)
                else:
                    gather(inside, outside, enter_inside, enter_outside)

    def solve(x, _):
        forward, backward = half_states(lambda t: f_ref[x, t])
        arriving = [i_ref[i, x] for i in range(POISSON)]
        swapped = [swap(entry) for entry in arriving]
        onward = []
        back = []
        for i in range(POISSON):
            carried = turned(HALF_TABLE, swapped, i)
            onward.append(swap(jnp.where(lower, forward[i] + carried, arriving[i])))
            back.append(swap(jnp.where(lower, arriving[i], backward[i] + carried)))

        def ahead(zz, state):
            state = cascade(state, f_ref[x, zz])
            for i in range(POISSON):
                u_ref[i, zz] = state[i]
            return state

        lax.fori_loop(0, HALF, ahead, tuple(onward), unroll=8)
        end = cascade([u_ref[i, HALF - 1] for i in range(POISSON)], f_ref[x, HALF])
        for i in range(POISSON):
            u_ref[i, HALF] = end[i]

        def mix(zz, state):
            both = [f_ref[x, zz]] + [u_ref[i, zz] + state[i] for i in range(POISSON)]
            for power in range(POISSON):
                total = MIXES[power][0] * both[0]
                for i in range(1, power + 2):
                    total = total + MIXES[power][i] * both[i]
                q_ref[power, x, zz] = total

        mix(HALF, back)

        def behind(t, state):
            zz = HALF - 1 - t
            state = cascade(state, f_ref[x, zz])
            mix(zz, state)
            return state

        lax.fori_loop(0, HALF, behind, tuple(back), unroll=8)
        return 0

    lax.fori_loop(0, 11, solve, 0)
    for power in (2, 1, 0):

        def apply(zz, _, power=power):
            edge = 2 - power
            layers = {x: q_ref[power + 1, x, zz] for x in range(edge, 11 - edge)}
            for x in range(edge + 1, 10 - edge if power else 8):
                beside = 4.0 * (layers[x - 1] + layers[x + 1]) + either_side(layers[x])
                if x < 3:
                    beside = mask_left * beside
                if x > 6:
                    beside = mask_right * beside
                q_ref[power, x, zz] = q_ref[power, x, zz] + beside
            return 0

        lax.fori_loop(0, HALF + 1, apply, 0, unroll=11)

    def correct(m, _):
        for x in range(4):
            pair = []
            for zz in (2 * m, 2 * m + 1):
                centre = q_ref[0, x + 3, zz]
                pair.append(
                    (
                        v_ref[0, x, zz] - 2.0 * (q_ref[0, x + 4, zz] - centre),
                        v_ref[1, x, zz] - (above(centre) - centre),
                        v_ref[2, x, zz] - (q_ref[0, x + 3, zz + 1] - centre),
                    )
                )
            for component in range(3):
                first, second = pair[0][component], pair[1][component]
                early = jnp.where(lower, first, swap(second))
                late = jnp.where(lower, swap(first), second)
                for tile in range(2):
                    row = (component * 64 + 2 * m) * 32 + tile * 4 + x
                    lanes = slice(tile * 128, tile * 128 + 128)
                    solved_ref[pl.ds(row, 8, stride=8), :] = early[:, lanes]
                    solved_ref[pl.ds(row + 1024, 8, stride=8), :] = late[:, lanes]
        return 0

    lax.fori_loop(0, 16, correct, 0, unroll=2)
    couples = [(i, j) for i in range(4) for j in range(i, 4)]

    def update(block, sums):
        columns = []
        for i in range(4):
            rows = pl.ds(pl.multiple_of(block * 32 + 8 * i, 8), 8)
            cells = factor_ref[rows, :] + (2.0 * shift) * solved_ref[rows, :]
            nf_ref[rows, :] = cells
            columns.append(cells)
        return tuple(s + columns[i] * columns[j] for s, (i, j) in zip(sums, couples))

    sums = (jnp.zeros((8, 128), jnp.float32),) * len(couples)
    copies = []
    for part in range(4):
        sums = lax.fori_loop(part * 48, part * 48 + 48, update, sums, unroll=4)
        rows = pl.ds(part * 1536, 1536)
        copies.append(pltpu.make_async_copy(nf_ref.at[rows], nf_hbm.at[rows], sent.at[part]))
        copies[-1].start()
    t_ref[...] = jnp.zeros((32, 128), jnp.float32)
    for total, (i, j) in zip(sums, couples):
        t_ref[4 * i + j : 4 * i + j + 1, :] = jnp.sum(total, axis=0, keepdims=True)
    lanes = lax.broadcasted_iota(jnp.int32, (1, 128), 1)
    for sensor in range(4):
        component = cells_ref[sensor, 0]
        z = cells_ref[sensor, 1] - span * 64
        x = cells_ref[sensor, 2] - stream * 4
        y = cells_ref[sensor, 3]
        held = (z >= 0) & (z < 64) & (x >= 0) & (x < 4)
        z = jnp.clip(z, 0, 63)
        x = jnp.clip(x, 0, 3)
        tile = jnp.where(y >= 128, 1, 0)
        lane = jnp.where(held, y - 128 * tile, -1)
        for column in range(4):
            row = (component * 64 + z) * 32 + column * 8 + tile * 4 + x
            cells = solved_ref[pl.ds(row, 1), :]
            at = 16 + 4 * sensor + column
            t_ref[at : at + 1, :] = jnp.where(lanes == lane, cells, 0.0)
    totals = jnp.sum(t_ref[...], axis=1, keepdims=True)
    spread = lax.broadcasted_iota(jnp.int32, (32, 128), 1) == lax.broadcasted_iota(jnp.int32, (32, 128), 0)
    sums_ref[...] = jnp.sum(jnp.where(spread, totals, 0.0), axis=0, keepdims=True)
    for copy in copies:
        copy.wait()


def gain_kernel(index_ref, sums_ref, gain_ref, solved_ref, out_hbm, gram_ref, out_ref, sent):
    totals = jnp.sum(sums_ref[...], axis=0, keepdims=True)
    lanes = lax.broadcasted_iota(jnp.int32, (1, 128), 1)
    shift = shift_of(index_ref)

    def entry(at):
        return jnp.sum(jnp.where(lanes == at, totals, 0.0), axis=1, keepdims=True)

    table = [
        [jnp.broadcast_to(2.0 * shift * entry(16 + 4 * i + j), (8, 128)) for j in range(4)] for i in range(4)
    ]

    def body(block, _):
        rows = [pl.ds(pl.multiple_of(block * 32 + 8 * j, 8), 8) for j in range(4)]
        columns = [solved_ref[rows[j], :] for j in range(4)]
        for i in range(4):
            total = gain_ref[rows[i], :]
            for j in range(4):
                total = total + table[i][j] * columns[j]
            out_ref[rows[i], :] = total
        return 0

    copies = []
    for part in range(6):
        lax.fori_loop(part * 32, part * 32 + 32, body, 0, unroll=4)
        rows = pl.ds(part * 1024, 1024)
        copies.append(pltpu.make_async_copy(out_ref.at[rows], out_hbm.at[rows], sent.at[part]))
        copies[-1].start()
    row = lax.broadcasted_iota(jnp.int32, (4, 4), 0)
    column = lax.broadcasted_iota(jnp.int32, (4, 4), 1)
    gram = jnp.zeros((4, 4), jnp.float32)
    for i in range(4):
        for j in range(4):
            value = entry(4 * min(i, j) + max(i, j)) / 6291456.0
            gram = gram + jnp.where((row == i) & (column == j), value, 0.0)
    gram_ref[...] = gram
    for copy in copies:
        copy.wait()


def ring_sides():
    upper = lax.broadcasted_iota(jnp.int32, (8, 256), 0) // 4
    return upper == 1 - lax.rem(lax.axis_index("gz"), 2)


def joining_kernel(states_ref, partner_ref, joined_ref):
    first = ring_sides()
    for layer in range(5):
        own = [states_ref[i, layer] for i in range(POISSON)]
        near = [partner_ref[i, layer] for i in range(POISSON)]
        farther = [jnp.where(first, o, n) for o, n in zip(own, near)]
        for i in range(POISSON):
            nearer = jnp.where(first, near[i], own[i])
            joined_ref[i, layer] = nearer + turned(WHOLE_TABLES[0], farther, i)
        joined_ref[POISSON, layer] = states_ref[POISSON, layer]


def entering_kernel(states_ref, partner_ref, other_ref, inc_ref, a_ref, b_ref):
    first = ring_sides()
    odd = x_odd()
    even = 1 - odd
    rightward = z_even()
    once, twice, thrice, around = WHOLE_TABLES
    for layer in range(5):
        own = [states_ref[i, layer] for i in range(POISSON)]
        near = [partner_ref[i, layer] for i in range(POISSON)]
        far = [other_ref[i, layer] for i in range(POISSON)]
        entering = []
        for i in range(POISSON):
            cells = jnp.where(first, far[i] + turned(twice, near, i), near[i] + turned(once, far, i))
            entering.append(cells + turned(thrice, own, i))
        for i in range(POISSON):
            inc_ref[i, layer] = turned(around, entering, i)
        inc_ref[POISSON, layer] = jnp.where(rightward, partner_ref[POISSON, layer], other_ref[POISSON, layer])
    for layer in range(4):
        for i in range(POISSON + 1):
            a_ref[i, layer] = inc_ref[i, layer + even]
            b_ref[i, layer] = inc_ref[i, layer + odd]


def call(kernel, outputs, scratch, operands, smalls, flops, room, far_in=(), far_out=(), signals=(), least=0):
    arrays = [jax.ShapeDtypeStruct(shape, jnp.float32) for shape in outputs]
    places = [pl.BlockSpec(memory_space=pltpu.SMEM)] * smalls
    places += [pl.BlockSpec(memory_space=pltpu.VMEM)] * (len(operands) - smalls)
    results = [pl.BlockSpec(memory_space=pltpu.VMEM)] * len(outputs)
    for place in far_in:
        places[place] = pl.BlockSpec(memory_space=pltpu.HBM)
    for place in far_out:
        results[place] = pl.BlockSpec(memory_space=pltpu.HBM)
    moved = sum(4 * math.prod(shape) for shape in outputs) + sum(4 * math.prod(o.shape) for o in operands)
    return pl.pallas_call(
        kernel,
        out_shape=arrays,
        in_specs=places,
        out_specs=results,
        scratch_shapes=[pltpu.VMEM(shape, jnp.float32) for shape in scratch]
        + [pltpu.SemaphoreType.DMA((count,)) for count in signals],
        compiler_params=pltpu.CompilerParams(vmem_limit_bytes=room << 20),
        cost_estimate=pl.CostEstimate(flops=flops, bytes_accessed=moved, transcendentals=0),
    )(*operands)


def to_rows(cells):
    head = cells.shape[:-2]
    order = tuple(range(len(head)))
    split = cells.reshape(*head, 4, 2, 128).transpose(*order, len(head) + 1, len(head), len(head) + 2)
    return split.reshape(-1, 128)


def from_rows(rows, head):
    order = tuple(range(len(head)))
    split = rows.reshape(*head, 2, 4, 128).transpose(*order, len(head) + 1, len(head), len(head) + 2)
    return split.reshape(*head, 4, 256)


def fast_shards(factor, gain, base_flow, shift_index, sensor_cells):
    swap_in = [(0, 1), (1, 0), (2, 3), (3, 2), (4, 5), (5, 4), (6, 7), (7, 6)]
    swap_out = [(1, 2), (2, 1), (3, 4), (4, 3), (5, 6), (6, 5)]
    send_round = [(1, 2), (2, 1), (5, 6), (6, 5), (3, 7), (4, 0)]
    forward_round = [(7, 4), (0, 3)]
    near = [(0, 1), (1, 0), (2, 3), (3, 2)]
    far = [(1, 2), (2, 1), (3, 0), (0, 3)]
    factor_rows = to_rows(factor)
    base_rows = to_rows(base_flow)
    gain_rows = to_rows(gain)
    cell = (8, 256)
    own, a, b1, b2, z1, z2 = call(
        pack_kernel,
        [(3, 4, HALF, *cell), (312, *cell), (PART, *cell), (312 - PART, *cell), (26, *cell), (26, *cell)],
        [factor_rows.shape], [factor_rows, base_rows], 0, 10**6, 16, far_in=(0,), signals=(3,),
    )
    b1_in = lax.ppermute(b1, "gx", send_round)
    z1 = lax.ppermute(z1, "gz", near)
    z2 = lax.ppermute(z2, "gz", far)
    b2_in = lax.ppermute(b2, "gx", swap_out)
    a_in = lax.ppermute(a, "gx", swap_in)
    corners = len(CORNERS) + 3
    ca, cb = call(corner_kernel, [(corners, *cell)] * 2, [], [z1, z2], 0, 10**5, 4)
    ca = lax.ppermute(ca, "gx", swap_in)
    cb = lax.ppermute(cb, "gx", swap_out)
    b1_in, z1, z2 = lax.optimization_barrier((b1_in, z1, z2))
    b3_in = lax.ppermute(b1_in, "gx", forward_round)
    block = (7, 39, *cell)
    scratch = [(10, 80, 256)] + [block] * 5
    handed = call(
        functools.partial(velocity_kernel, "early"),
        [(3, 2, 39, *cell), (3, 2, 39, *cell), (3, HALF + 1, *cell)],
        scratch, [shift_index, own, base_rows, a_in, ca, z1, z2], 1, 10**8, 34,
    )
    velocity, sides, states, pa, pb1, pb2 = call(
        functools.partial(velocity_kernel, "late"),
        [(3, 4, HALF, *cell), (5, HALF, *cell), (POISSON + 1, 5, *cell), (4, HALF, *cell)]
        + [(2, HALF, *cell)] * 2,
        scratch,
        [shift_index, own, base_rows, b1_in, b3_in, b2_in, cb, z1, z2, *handed], 1, 10**8, 34,
    )
    pb1_in = lax.ppermute(pb1, "gx", send_round)
    pb2_in = lax.ppermute(pb2, "gx", swap_out)
    partner = lax.ppermute(states, "gz", near)
    (joined,) = call(joining_kernel, [states.shape], [], [states, partner], 0, 10**5, 4)
    other = lax.ppermute(joined, "gz", far)
    pb1_in, _ = lax.optimization_barrier((pb1_in, partner))
    pb3_in = lax.ppermute(pb1_in, "gx", forward_round)
    pa_in = lax.ppermute(pa, "gx", swap_in)
    entering, enter_a, enter_b = call(
        entering_kernel,
        [states.shape, (POISSON + 1, 4, *cell), (POISSON + 1, 4, *cell)],
        [], [states, partner, other], 0, 10**5, 4,
    )
    enter_b = lax.ppermute(enter_b, "gx", swap_out)
    enter_a = lax.ppermute(enter_a, "gx", swap_in)
    block = (11, HALF + 1, *cell)
    new_rows, solved, sums = call(
        pressure_kernel,
        [factor_rows.shape, factor_rows.shape, (1, 128)],
        [block, (POISSON + 1, 11, *cell), (POISSON, HALF + 1, *cell), (POISSON, *block), (32, 128)]
        + [factor_rows.shape],
        [shift_index, sensor_cells, velocity, sides, pa_in, pb1_in, pb3_in, pb2_in]
        + [entering, enter_a, enter_b, factor_rows],
        2, 10**8, 38, far_out=(0,), signals=(4,),
    )
    devices = lax.axis_size("gx") * lax.axis_size("gz")
    shared = lax.all_to_all(
        jnp.broadcast_to(sums[None], (devices, 1, 128)), ("gx", "gz"), split_axis=0, concat_axis=0, tiled=True
    )
    new_gain, gram = call(
        gain_kernel,
        [gain_rows.shape, (4, 4)],
        [gain_rows.shape], [shift_index, shared.reshape(devices, 128), gain_rows, solved], 1, 10**7, 14,
        far_out=(0,), signals=(6,),
    )
    head = factor.shape[:3]
    return (from_rows(new_rows, head), from_rows(new_gain, head), gram)


def solution(mesh):
    placed = (
        P(None, "gz", None, "gx", None),
        P(None, "gz", None, "gx", None),
        P("gz", "gx", None),
        P(),
        P(),
    )
    fits = mesh.shape["gx"] == 8 and mesh.shape["gz"] == 4
    return jax.shard_map(
        fast_shards if fits else shards,
        mesh=mesh,
        in_specs=placed,
        out_specs=(P(None, "gz", None, "gx", None), P(None, "gz", None, "gx", None), P()),
        check_vma=False,
    )
```

```python
import functools
import math

import jax
import jax.numpy as jnp
import numpy as np
from jax import lax
from jax.experimental import pallas as pl
from jax.experimental.pallas import tpu as pltpu
from jax.sharding import PartitionSpec as P

SWEEPS = 3
POISSON = 4
SHIFTS = 8


viscosity = 0.4
shift_table = (0.6, 0.8, 1.0, 1.25, 1.6, 2.0, 2.5, 3.2)
chebyshev_weights = (1.0 / 1.9352976, 1.0 / 1.4752809, 1.0 / 0.8247191, 1.0 / 0.3647024)
highest = lax.Precision.HIGHEST


def padded_2(cells, sides, width, closed):
    for axis, dim in sides:
        count = lax.axis_size(axis)
        ends = count if closed else count - 1
        head = lax.slice_in_dim(cells, 0, width, axis=dim)
        tail = lax.slice_in_dim(cells, cells.shape[dim] - width, cells.shape[dim], axis=dim)
        cells = jnp.concatenate(
            [
                lax.ppermute(tail, axis, [(i, (i + 1) % count) for i in range(ends)]),
                cells,
                lax.ppermute(head, axis, [((i + 1) % count, i) for i in range(ends)]),
            ],
            axis=dim,
        )
    return cells


def around_sum(padded):
    summed = padded[:, 1:-1, :, 2:, 1:-1] + padded[:, 1:-1, :, :-2, 1:-1]
    summed = summed + padded[:, 1:-1, :, 1:-1, 2:] + padded[:, 1:-1, :, 1:-1, :-2]
    return summed + padded[:, 2:, :, 1:-1, 1:-1] + padded[:, :-2, :, 1:-1, 1:-1]


def shards(factor, gain, base_flow, shift_index, sensor_cells):
    components, span_cells, columns, stream_cells, normal_cells = factor.shape
    stream_start = lax.axis_index("gx") * stream_cells
    span_start = lax.axis_index("gz") * span_cells
    stream_total = stream_cells * lax.axis_size("gx")
    span_total = span_cells * lax.axis_size("gz")
    shift_values = jnp.asarray(shift_table, jnp.float32)
    shift_value = jnp.sum(jnp.where(jnp.arange(SHIFTS) == shift_index[0], shift_values, 0.0))
    base_field = base_flow[None, :, None, :, :]
    diagonal = shift_value + 6.0 * viscosity + base_field
    source = -factor

    def stream_inside(extent, margin):
        positions = stream_start - margin + jnp.arange(extent)
        return ((positions >= 0) & (positions < stream_total)).astype(jnp.float32)

    def extend(grid_field):
        padded = padded_2(grid_field, (("gx", 3), ("gz", 1)), 1, True)
        padded = padded * stream_inside(stream_cells + 2, 1)[None, None, None, :, None]
        return jnp.pad(padded, ((0, 0), (0, 0), (0, 0), (0, 0), (1, 1)))

    velocity = source / diagonal
    for sweep_index in range(SWEEPS):
        padded = extend(velocity)
        velocity = (
            source + viscosity * around_sum(padded) + base_field * padded[:, 1:-1, :, :-2, 1:-1]
        ) / diagonal
    padded = extend(velocity)
    divergence = 2.0 * (velocity[0] - padded[0, 1:-1, :, :-2, 1:-1])
    divergence = divergence + (velocity[1] - padded[1, 1:-1, :, 1:-1, :-2])
    divergence = divergence + (velocity[2] - padded[2, :-2, :, 1:-1, 1:-1])
    span_index = jnp.arange(span_total)
    products = span_index[:, None] * span_index[None, :] % span_total
    angles = 2.0 * math.pi * products.astype(jnp.float32) / span_total
    hartley_table = (jnp.cos(angles) + jnp.sin(angles)) / math.sqrt(span_total)

    def turn_modes(exchanged):
        turned = jnp.einsum("kz,zay->kay", hartley_table, exchanged, precision=highest)
        return lax.all_to_all(turned, "gz", split_axis=0, concat_axis=1, tiled=True)

    def transform(grid_field):
        flat = grid_field.reshape(span_cells, columns * stream_cells, normal_cells)
        result = turn_modes(lax.all_to_all(flat, "gz", split_axis=1, concat_axis=0, tiled=True))
        return result.reshape(span_cells, columns, stream_cells, normal_cells)

    modes_rhs = -transform(divergence)
    wave_index = span_start + jnp.arange(span_cells)
    wavenumber = 2.0 * math.pi * wave_index.astype(jnp.float32) / span_total
    mode_diagonal = (10.0 + (2.0 - 2.0 * jnp.cos(wavenumber)))[:, None, None, None]
    pressure = chebyshev_weights[0] * modes_rhs / mode_diagonal
    for sweep_level in range(1, POISSON):
        padded = padded_2(pressure, (("gx", 2),), 1, False)
        padded = jnp.pad(padded, ((0, 0), (0, 0), (0, 0), (1, 1)))
        beside_all = (
            4.0 * (padded[:, :, 2:, 1:-1] + padded[:, :, :-2, 1:-1])
            + padded[:, :, 1:-1, 2:]
            + padded[:, :, 1:-1, :-2]
        )
        pressure = (
            pressure
            + chebyshev_weights[sweep_level]
            * (modes_rhs - (mode_diagonal * pressure - beside_all))
            / mode_diagonal
        )
    pressure = transform(pressure)
    padded = extend(pressure[None])[0]
    gradient = jnp.stack(
        [
            2.0 * (padded[1:-1, :, 2:, 1:-1] - pressure),
            padded[1:-1, :, 1:-1, 2:] - pressure,
            padded[2:, :, 1:-1, 1:-1] - pressure,
        ]
    )
    solved = velocity - gradient
    span_ids = span_start + jnp.arange(span_cells)
    stream_ids = stream_start + jnp.arange(stream_cells)
    normal_ids = jnp.arange(normal_cells)
    located = span_ids[None, :, None, None] == sensor_cells[:, 1][:, None, None, None]
    located = located & (stream_ids[None, None, :, None] == sensor_cells[:, 2][:, None, None, None])
    located = located & (normal_ids[None, None, None, :] == sensor_cells[:, 3][:, None, None, None])
    picked = jnp.einsum("szxy,czjxy->scj", located.astype(jnp.float32), solved, precision=highest)
    chooser = (jnp.arange(3)[None, :] == sensor_cells[:, 0:1]).astype(jnp.float32)
    readout_local = jnp.sum(picked * chooser[:, :, None], axis=1)
    new_factor = factor + 2.0 * shift_value * solved
    gram_local = jnp.einsum("czixy,czjxy->ij", new_factor, new_factor, precision=highest)
    gram_total, readout = lax.psum((gram_local, readout_local), ("gx", "gz"))
    gram = gram_total / (3.0 * stream_total * normal_cells * span_total)
    new_gain = gain + 2.0 * shift_value * jnp.einsum(
        "czjxy,ij->czixy", solved, readout, precision=highest
    )
    return (new_factor, new_gain, gram)


HALF = 32
PAIRS = 8


def recurrence_tables(centre, weights):
    ratio = centre / 2.0 - math.sqrt(centre * centre / 4.0 - 1.0)
    order = len(weights)
    step = ratio * np.tril(np.ones((order, order)))
    half = np.linalg.matrix_power(step, HALF)
    whole = np.linalg.matrix_power(step, 2 * HALF)
    angles = 2.0 * np.pi * np.arange(4096) / 4096
    series = [weights[0]]
    for weight in weights[1:]:
        longer = [0.0] + [weight * entry for entry in series]
        for place, entry in enumerate(series):
            longer[place] += (1.0 - weight) * entry
        longer[0] += weight
        series = longer
    mixes = []
    for power in range(1, order + 1):
        symbol = 1.0 / (centre - 2.0 * np.cos(angles)) ** power
        kernel = [np.mean(symbol * np.cos(angles * n)) for n in range(order + 1)]
        matrix = [[math.comb(n + i - 1, i - 1) for i in range(1, power + 1)] for n in range(1, power + 1)]
        sides = np.linalg.solve(
            np.array(matrix, np.float64), [kernel[n] / ratio**n for n in range(1, power + 1)]
        )
        middle = kernel[0] - 2.0 * np.sum(sides)
        mixes.append([float(series[power - 1] * entry) for entry in [middle, *sides]])
    square = whole @ whole
    around = np.linalg.inv(np.eye(order) - square @ square)
    wholes = [table.tolist() for table in (whole, square, square @ whole, around)]
    return float(ratio), half.tolist(), wholes, mixes


RATIO, HALF_TABLE, WHOLE_TABLES, MIXES = recurrence_tables(12.0, chebyshev_weights)


def lower_half():
    return lax.broadcasted_iota(jnp.int32, (8, 256), 0) < 4


def swap(cells):
    return pltpu.roll(cells, 4, 0)


def below(cells):
    lanes = lax.broadcasted_iota(jnp.int32, (8, 128), 1)
    low, high = pltpu.roll(cells[:, :128], 1, 1), pltpu.roll(cells[:, 128:], 1, 1)
    return jnp.concatenate([jnp.where(lanes > 0, low, 0.0), jnp.where(lanes > 0, high, low)], axis=1)


def above(cells):
    lanes = lax.broadcasted_iota(jnp.int32, (8, 128), 1)
    low, high = pltpu.roll(cells[:, :128], 127, 1), pltpu.roll(cells[:, 128:], 127, 1)
    return jnp.concatenate([jnp.where(lanes < 127, low, high), jnp.where(lanes < 127, high, 0.0)], axis=1)


def either_side(cells):
    lanes = lax.broadcasted_iota(jnp.int32, (8, 128), 1)
    low, high = cells[:, :128], cells[:, 128:]
    low_up, high_up = pltpu.roll(low, 1, 1), pltpu.roll(high, 1, 1)
    low_down, high_down = pltpu.roll(low, 127, 1), pltpu.roll(high, 127, 1)
    first = jnp.where(lanes > 0, low_up, 0.0) + jnp.where(lanes < 127, low_down, high_down)
    second = jnp.where(lanes > 0, high_up, low_up) + jnp.where(lanes < 127, high_down, 0.0)
    return jnp.concatenate([first, second], axis=1)


def shift_of(index_ref):
    index = index_ref[0]
    value = jnp.float32(shift_table[0])
    for place in range(1, SHIFTS):
        value = jnp.where(index == place, jnp.float32(shift_table[place]), value)
    return value


def x_odd():
    return lax.rem(lax.axis_index("gx"), 2)


def z_even():
    return lax.rem(lax.axis_index("gz"), 2) == 0


def cascade(state, cells):
    grown = []
    for entry in state:
        cells = RATIO * entry + cells
        grown.append(cells)
    return tuple(grown)


def half_states(read):
    zero = jnp.zeros((8, 256), jnp.float32)

    def body(t, carry):
        forward, backward = carry
        return cascade(forward, read(t)), cascade(backward, read(HALF - 1 - t))

    return lax.fori_loop(0, HALF, body, ((zero,) * POISSON, (zero,) * POISSON), unroll=8)


def turned(table, states, row):
    total = None
    for column in range(row + 1):
        term = table[row][column] * states[column]
        total = term if total is None else total + term
    return total


FACTOR_AT = 24
PART = 152
CORNERS = [(c, dx, side, 0) for c in range(3) for dx in (1, 2) for side in (0, 1)]
CORNERS += [(2, 1, 0, 1), (2, 3, 0, 0)]


def pack_kernel(factor_hbm, base_ref, own_ref, a_ref, b1_ref, b2_ref, z1_ref, z2_ref, factor_ref, arrived):
    share = factor_ref.shape[0] // 3
    copies = []
    for component in range(3):
        rows = pl.ds(component * share, share)
        copies.append(
            pltpu.make_async_copy(factor_hbm.at[rows], factor_ref.at[rows], arrived.at[component])
        )
        copies[-1].start()
    odd = x_odd()
    even = 1 - odd
    low = lax.broadcasted_iota(jnp.int32, (8, 128), 0) < 4
    scale = -1.0 / viscosity
    for component in range(3):

        def load(m, _, component=component):
            for x in range(4):
                for tile in range(2):
                    row = (component * 64 + 2 * m) * 32 + tile * 4 + x
                    first = factor_ref[pl.ds(row, 8, stride=8), :] * scale
                    second = factor_ref[pl.ds(row + 1024, 8, stride=8), :] * scale
                    lanes = slice(tile * 128, tile * 128 + 128)
                    own_ref[component, x, 2 * m, :, lanes] = jnp.where(low, first, swap(second))
                    own_ref[component, x, 2 * m + 1, :, lanes] = jnp.where(low, swap(first), second)
            return 0

        copies[component].wait()
        lax.fori_loop(0, 16, load, 0, unroll=2)

    def edges(zz, _):
        for component in range(3):
            for layer in range(3):
                at = FACTOR_AT + (component * 3 + layer) * HALF
                a_ref[at + zz] = own_ref[component, layer + even, zz]
                cells = own_ref[component, layer + odd, zz]
                if at < PART:
                    b1_ref[at + zz] = cells
                else:
                    b2_ref[at - PART + zz] = cells
        return 0

    lax.fori_loop(0, HALF, edges, 0, unroll=2)
    for layer in range(3):
        for group in range(8):
            for tile in range(2):
                lanes = slice(tile * 128, tile * 128 + 128)
                row = group * 64 + tile * 4 + layer
                a_ref[layer * 8 + group, :, lanes] = base_ref[pl.ds(row + even, 8, stride=8), :]
                b1_ref[layer * 8 + group, :, lanes] = base_ref[pl.ds(row + odd, 8, stride=8), :]
    lower = lower_half()
    rightward = z_even()
    for component in range(3):
        for x in range(4):
            for pair in range(2):
                cells = lambda zz: own_ref[component, x, zz]
                up = jnp.where(lower, swap(cells(31 - 2 * pair)), cells(30 - 2 * pair))
                down = jnp.where(lower, cells(2 * pair), swap(cells(2 * pair + 1)))
                at = (component * 4 + x) * 2 + pair
                z1_ref[at] = jnp.where(rightward, up, down)
                z2_ref[at] = jnp.where(rightward, down, up)
    for k in range(4):
        for tile in range(2):
            lanes = slice(tile * 128, tile * 128 + 128)
            up = base_ref[(63 - k) * 8 + tile * 4 : (63 - k) * 8 + tile * 4 + 4, :]
            down = base_ref[k * 8 + tile * 4 : k * 8 + tile * 4 + 4, :]
            rows = slice((k % 2) * 4, (k % 2) * 4 + 4)
            z1_ref[24 + k // 2, rows, lanes] = jnp.where(rightward, up, down)
            z2_ref[24 + k // 2, rows, lanes] = jnp.where(rightward, down, up)


def corner_kernel(z1_ref, z2_ref, a_ref, b_ref):
    odd = x_odd()
    rightward = z_even()

    def fill(behind_ref, ahead_ref):
        for place, (component, dx, side, pair) in enumerate(CORNERS):
            source = (behind_ref, ahead_ref)[side]
            right_x = 4 - dx
            left_x = dx - 1
            a_x = jnp.where(odd == 1, left_x, right_x)
            b_x = jnp.where(odd == 1, right_x, left_x)
            a_ref[place] = source[(component * 4 + a_x) * 2 + pair]
            b_ref[place] = source[(component * 4 + b_x) * 2 + pair]
        for dx in (1, 2, 3):
            for k in range(4):
                for side, source in enumerate((behind_ref, ahead_ref)):
                    from_right = source[24 + k // 2, (k % 2) * 4 + 4 - dx, :]
                    from_left = source[24 + k // 2, (k % 2) * 4 + dx - 1, :]
                    at = len(CORNERS) + dx - 1
                    a_ref[at, side * 4 + k, :] = jnp.where(odd == 1, from_left, from_right)
                    b_ref[at, side * 4 + k, :] = jnp.where(odd == 1, from_right, from_left)

    @pl.when(rightward)
    def _():
        fill(z2_ref, z1_ref)

    @pl.when(jnp.logical_not(rightward))
    def _():
        fill(z1_ref, z2_ref)


KNOWN = {("early", 0): (3, 9), ("early", 1): (0, 6), ("late", 0): (0, 5), ("late", 1): (4, 9)}
SWEPT = {
    ("early", 0): ((4, 8), (5, 7), (6, 6)),
    ("early", 1): ((1, 5), (2, 4), (3, 3)),
    ("late", 0): ((1, 3), (2, 4), (3, 5)),
    ("late", 1): ((6, 8), (5, 7), (4, 6)),
}
HANDED = (((4, 5), (5, 6), 6), ((4, 5), (3, 4), 3))


def velocity_kernel(stage, *refs):
    early = stage == "early"
    if early:
        index_ref, own_ref, base_ref, a_ref, c_ref, z1_ref, z2_ref, *refs = refs
        h1_ref, h2_ref, h3_ref, *refs = refs
    else:
        index_ref, own_ref, base_ref, b1_ref, b3_ref, b2_ref, c_ref, z1_ref, z2_ref, *refs = refs
        h1_ref, h2_ref, h3_ref, v_ref, bw_ref, s_ref, pa_ref, pb1_ref, pb2_ref, *refs = refs
    flow_ref, a1_ref, r_ref, v0_ref, va_ref, vb_ref = refs
    odd = x_odd()
    stream = lax.axis_index("gx")
    last = lax.axis_size("gx") - 1
    mask_left = jnp.where(stream > 0, 1.0, 0.0)
    mask_right = jnp.where(stream < last, 1.0, 0.0)
    relayed = jnp.logical_or(stream == 3, stream == 4)
    rightward = z_even()
    lower = lower_half()
    shift = shift_of(index_ref)
    zero = jnp.zeros((8, 256), jnp.float32)

    def each_z(step):
        @pl.when(rightward)
        def _():
            step(z2_ref, z1_ref)

        @pl.when(jnp.logical_not(rightward))
        def _():
            step(z1_ref, z2_ref)

    def inside(at):
        return lambda zz: a_ref[at + zz]

    def outside(first_ref):
        def pick(at):
            if at < PART:
                return lambda zz: first_ref[at + zz]
            return lambda zz: b2_ref[at - PART + zz]

        return pick

    def each_x(step):
        if early:
            step(inside)
            return

        @pl.when(relayed)
        def _():
            step(outside(b3_ref))

        @pl.when(jnp.logical_not(relayed))
        def _():
            step(outside(b1_ref))

    def before(cells, halo, k):
        if k % 2 == 0:
            return jnp.where(lower, halo, swap(cells))
        return swap(jnp.where(lower, cells, halo))

    def after(cells, halo, k):
        if k % 2 == 0:
            return swap(jnp.where(lower, halo, cells))
        return jnp.where(lower, swap(cells), halo)

    def run(parity):
        low, high = KNOWN[stage, parity]
        own_layers = [x for x in range(4) if low <= x + 3 <= high]
        if low < 3:
            halo = [(dx, 3 - dx, 3 - dx) for dx in (1, 2, 3)]
        else:
            halo = [(dx, 6 + dx, dx - 1) for dx in (1, 2, 3)]

        for x in own_layers:
            for group in range(8):
                for tile in range(2):
                    lanes = slice(tile * 128, tile * 128 + 128)
                    flow_ref[x + 3, 8 + 8 * group : 16 + 8 * group, lanes] = base_ref[
                        pl.ds(group * 64 + tile * 4 + x, 8, stride=8), :
                    ]

        def flow_span(behind_ref, ahead_ref):
            for x in own_layers:
                for k in range(4):
                    at = 24 + k // 2
                    row = (k % 2) * 4 + x
                    flow_ref[x + 3, 7 - k, :] = behind_ref[at, row, :]
                    flow_ref[x + 3, 72 + k, :] = ahead_ref[at, row, :]

        each_z(flow_span)

        def flow_stream(pick):
            for dx, place, layer in halo:
                for group in range(8):
                    flow_ref[place, 8 + 8 * group : 16 + 8 * group, :] = pick(layer * 8)(group)
                for k in range(4):
                    flow_ref[place, 7 - k, :] = c_ref[len(CORNERS) + dx - 1, k, :]
                    flow_ref[place, 72 + k, :] = c_ref[len(CORNERS) + dx - 1, 4 + k, :]

        each_x(flow_stream)

        def coefficients(zz, _):
            for x in range(low, high + 1):
                first = jnp.broadcast_to(flow_ref[x, pl.ds(zz + 4, 1), :], (8, 256))
                second = jnp.broadcast_to(flow_ref[x, pl.ds(zz + 36, 1), :], (8, 256))
                flow = jnp.where(lower, first, second)
                scale = viscosity * (mask_left if x < 3 else mask_right if x > 6 else 1.0)
                a1_ref[x - low, zz] = scale / (shift + 6.0 * viscosity + flow)
                r_ref[x - low, zz] = 1.0 + flow * (1.0 / viscosity)
            return 0

        lax.fori_loop(0, 39, coefficients, 0, unroll=3)
        for _, place, _ in halo:
            for zz in (0, 1, 2, 3, 36, 37, 38):
                v0_ref[place - low, zz] = zero

        def swept(source, span, zz, depth):
            result = {}
            first, final = span
            behind = [source(first - 1, zz + k) for k in range(depth)]
            here = [source(first, zz + k - 1) for k in range(depth + 2)]
            for x in range(first, final + 1):
                if x < final:
                    ahead = [source(x + 1, zz + k - 1) for k in range(depth + 2)]
                else:
                    ahead = [None] + [source(x + 1, zz + k) for k in range(depth)]
                result[x] = []
                for k in range(depth):
                    total = ahead[k + 1] + either_side(here[k + 1])
                    total = total + (here[k] + here[k + 2])
                    total = total + r_ref[x - low, zz + k] * behind[k]
                    result[x].append(v0_ref[x - low, zz + k] + a1_ref[x - low, zz + k] * total)
                behind, here = here[1 : depth + 1], ahead
            return result

        def sweep(source, target, level, margin, hand):
            depth = 4
            first, extent = 3 - margin, 33 + 2 * margin

            def body(t, _):
                zz = first + jnp.minimum(t * depth, extent - depth)
                for x, column in swept(source, SWEPT[stage, parity][level], zz, depth).items():
                    for k, cells in enumerate(column):
                        if target is not None:
                            target[x - low, zz + k] = cells
                        hand(x, zz + k, cells)
                return 0

            lax.fori_loop(0, -(-extent // depth), body, 0, unroll=3)

        handed_first, handed_second, handed_third = HANDED[parity]
        for component in range(3):

            def interior(zz, _, component=component):
                for x in own_layers:
                    v0_ref[x + 3 - low, zz + 4] = own_ref[component, x, zz] * a1_ref[x + 3 - low, zz + 4]
                return 0

            lax.fori_loop(0, HALF, interior, 0, unroll=4)

            def span(behind_ref, ahead_ref, component=component):
                for x in own_layers:
                    at = (component * 4 + x) * 2
                    for k in range(4):
                        cells = before(own_ref[component, x, 31 - k], behind_ref[at + k // 2], k)
                        v0_ref[x + 3 - low, 3 - k] = cells * a1_ref[x + 3 - low, 3 - k]
                    for k in range(3):
                        cells = after(own_ref[component, x, k], ahead_ref[at + k // 2], k)
                        v0_ref[x + 3 - low, 36 + k] = cells * a1_ref[x + 3 - low, 36 + k]

            each_z(span)

            def sides(pick, component=component):
                for dx, place, layer in halo:
                    read = pick(FACTOR_AT + (component * 3 + layer) * HALF)

                    def body(zz, _, read=read, place=place):
                        v0_ref[place - low, zz + 4] = read(zz) * a1_ref[place - low, zz + 4]
                        return 0

                    lax.fori_loop(0, HALF, body, 0, unroll=4)
                    for entry, (c, away, side, pair) in enumerate(CORNERS):
                        if c != component or away != dx:
                            continue
                        for k in (2 * pair, 2 * pair + 1):
                            if side == 0:
                                cells = before(read(31 - k), c_ref[entry], k)
                                v0_ref[place - low, 3 - k] = cells * a1_ref[place - low, 3 - k]
                            else:
                                cells = after(read(k), c_ref[entry], k)
                                v0_ref[place - low, 36 + k] = cells * a1_ref[place - low, 36 + k]

            each_x(sides)

            def hand_first(x, zz, cells, component=component):
                if early and x in handed_first:
                    h1_ref[component, handed_first.index(x), zz] = cells

            def hand_second(x, zz, cells, component=component):
                if early and x in handed_second:
                    h2_ref[component, handed_second.index(x), zz] = cells

            def hand_third(x, zz, cells, component=component):
                h3_ref[component, zz - 3] = cells

            def from_first(x, zz, component=component):
                if not early and x in handed_first:
                    return h1_ref[component, handed_first.index(x), zz]
                return va_ref[x - low, zz]

            def from_second(x, zz, component=component):
                if not early and x in handed_second:
                    return h2_ref[component, handed_second.index(x), zz]
                return vb_ref[x - low, zz]

            sweep(lambda x, zz: v0_ref[x - low, zz], va_ref, 0, 2, hand_first)
            sweep(from_first, vb_ref, 1, 1, hand_second)
            if early:
                sweep(from_second, None, 2, 0, hand_third)
                continue

            def finished(zz, depth, component=component):
                found = swept(from_second, SWEPT[stage, parity][2], zz + 4, depth)
                found[handed_third] = [h3_ref[component, zz + 1 + k] for k in range(depth)]
                return [[found[x + 3][k] for x in range(4)] for k in range(depth)]

            def diverge(t, past, component=component):
                for k, cells in enumerate(finished(4 * t, 4)):
                    zz = 4 * t + k
                    for x in range(4):
                        v_ref[component, x, zz] = cells[x]
                        if component == 0:
                            bw_ref[x, zz] = -2.0 * (cells[x] if x == 0 else cells[x] - cells[x - 1])
                        elif component == 1:
                            bw_ref[x, zz] = bw_ref[x, zz] - (cells[x] - below(cells[x]))
                        else:
                            bw_ref[x, zz] = bw_ref[x, zz] - (cells[x] - past[x])
                    if component == 0:
                        bw_ref[4, zz] = cells[3]
                    past = tuple(cells) if component == 2 else 0
                return past

            start = tuple(finished(-1, 1)[0]) if component == 2 else 0
            lax.fori_loop(0, HALF // 4, diverge, start, unroll=4)

    for parity in (0, 1):

        @pl.when(odd == parity)
        def _(parity=parity):
            run(parity)

    if early:
        return

    def edges(zz, _):
        for layer in range(4):
            pa_ref[layer, zz] = bw_ref[layer + 1 - odd, zz]
            (pb1_ref if layer < 2 else pb2_ref)[layer % 2, zz] = bw_ref[layer + odd, zz]
        return 0

    lax.fori_loop(0, HALF, edges, 0, unroll=4)

    def states(layer, _):
        forward, backward = half_states(lambda t: bw_ref[layer, t])
        swapped_forward = [swap(entry) for entry in forward]
        swapped_backward = [swap(entry) for entry in backward]
        for i in range(POISSON):
            onward = forward[i] + turned(HALF_TABLE, swapped_forward, i)
            back = backward[i] + turned(HALF_TABLE, swapped_backward, i)
            s_ref[i, layer] = jnp.where(lower, back, onward)
        s_ref[POISSON, layer] = bw_ref[layer, 0]
        return 0

    lax.fori_loop(0, 5, states, 0, unroll=5)


def pressure_kernel(
    index_ref, cells_ref, v_ref, bw_ref, ba_ref, b1_ref, b3_ref, b2_ref, inc_ref, ia_ref, ib_ref, factor_ref,
    nf_hbm, solved_ref, sums_ref,
    f_ref, i_ref, u_ref, q_ref, t_ref, nf_ref, sent,
):
    odd = x_odd()
    stream = lax.axis_index("gx")
    span = lax.axis_index("gz")
    last = lax.axis_size("gx") - 1
    mask_left = jnp.where(stream > 0, 1.0, 0.0)
    mask_right = jnp.where(stream < last, 1.0, 0.0)
    lower = lower_half()
    shift = shift_of(index_ref)

    def gather(left, right, left_inc, right_inc):
        def body(zz, _):
            for x in range(3):
                f_ref[x, zz] = mask_left * left(x, zz)
                f_ref[x + 4, zz] = bw_ref[x + 1, zz]
                f_ref[x + 8, zz] = mask_right * right(x + 1, zz)
            f_ref[3, zz] = bw_ref[0, zz] + (2.0 * mask_left) * left(3, zz)
            f_ref[7, zz] = mask_right * (right(0, zz) + 2.0 * bw_ref[4, zz])
            return 0

        lax.fori_loop(0, HALF, body, 0, unroll=4)
        for i in range(POISSON + 1):
            for x in range(3):
                i_ref[i, x] = left_inc(i, x)
                i_ref[i, x + 4] = inc_ref[i, x + 1]
                i_ref[i, x + 8] = right_inc(i, x + 1)
            i_ref[i, 3] = inc_ref[i, 0] + 2.0 * left_inc(i, 3)
            i_ref[i, 7] = mask_right * (right_inc(i, 0) + 2.0 * inc_ref[i, 4])
        for x in range(11):
            f_ref[x, HALF] = swap(jnp.where(lower, i_ref[POISSON, x], f_ref[x, 0]))

    def enter_inside(i, layer):
        return ia_ref[i, layer]

    def enter_outside(i, layer):
        return ib_ref[i, layer]

    def inside(layer, zz):
        return ba_ref[layer, zz]

    def direct(layer, zz):
        return b1_ref[layer, zz] if layer < 2 else b2_ref[layer - 2, zz]

    def relayed(layer, zz):
        return b3_ref[layer, zz] if layer < 2 else b2_ref[layer - 2, zz]

    middle = jnp.logical_or(stream == 3, stream == 4)
    for parity in (0, 1):
        for through, outside in ((False, direct), (True, relayed)):

            @pl.when(jnp.logical_and(odd == parity, middle == through))
            def _(parity=parity, outside=outside):
                if parity == 0:
                    gather(outside, inside, enter_outside, enter_inside)
                else:
                    gather(inside, outside, enter_inside, enter_outside)

    def solve(layers, least):
        count = len(layers)
        zero = (jnp.zeros((8, 256), jnp.float32),) * POISSON

        def halves(t, carry):
            return tuple(
                (cascade(up, f_ref[x, t]), cascade(down, f_ref[x, HALF - 1 - t]))
                for x, (up, down) in zip(layers, carry)
            )

        ends = lax.fori_loop(0, HALF, halves, ((zero, zero),) * count, unroll=8)
        onward = []
        back = []
        for x, (forward, backward) in zip(layers, ends):
            arriving = [i_ref[i, x] for i in range(POISSON)]
            swapped = [swap(entry) for entry in arriving]
            carried = [turned(HALF_TABLE, swapped, i) for i in range(POISSON)]
            onward.append(
                tuple(
                    swap(jnp.where(lower, forward[i] + carried[i], arriving[i])) for i in range(POISSON)
                )
            )
            back.append(
                tuple(
                    swap(jnp.where(lower, arriving[i], backward[i] + carried[i])) for i in range(POISSON)
                )
            )

        def ahead(zz, states):
            states = tuple(cascade(state, f_ref[x, zz]) for x, state in zip(layers, states))
            for slot, state in enumerate(states):
                for i in range(POISSON):
                    u_ref[slot, i, zz] = state[i]
            return states

        ahead(HALF, lax.fori_loop(0, HALF, ahead, tuple(onward), unroll=8))

        def mix(zz, states):
            for slot, (x, state) in enumerate(zip(layers, states)):
                both = [f_ref[x, zz]] + [u_ref[slot, i, zz] + state[i] for i in range(POISSON)]
                for power in range(least, POISSON):
                    total = MIXES[power][0] * both[0]
                    for i in range(1, power + 2):
                        total = total + MIXES[power][i] * both[i]
                    q_ref[power, x, zz] = total

        mix(HALF, back)

        def behind(t, states):
            zz = HALF - 1 - t
            states = tuple(cascade(state, f_ref[x, zz]) for x, state in zip(layers, states))
            mix(zz, states)
            return states

        lax.fori_loop(0, HALF, behind, tuple(back), unroll=8)

    solve((5,), 0)
    for distance in (-1, 0, 1, 2, 3):
        solve((3 - distance, 7 + distance), max(distance, 0))
    for power in (2, 1, 0):

        def apply(zz, _, power=power):
            edge = 2 - power
            layers = {x: q_ref[power + 1, x, zz] for x in range(edge, 11 - edge)}
            for x in range(edge + 1, 10 - edge if power else 8):
                beside = 4.0 * (layers[x - 1] + layers[x + 1]) + either_side(layers[x])
                if x < 3:
                    beside = mask_left * beside
                if x > 6:
                    beside = mask_right * beside
                q_ref[power, x, zz] = q_ref[power, x, zz] + beside
            return 0

        lax.fori_loop(0, HALF + 1, apply, 0, unroll=11)

    def correct(m, _):
        for x in range(4):
            pair = []
            for zz in (2 * m, 2 * m + 1):
                centre = q_ref[0, x + 3, zz]
                pair.append(
                    (
                        v_ref[0, x, zz] - 2.0 * (q_ref[0, x + 4, zz] - centre),
                        v_ref[1, x, zz] - (above(centre) - centre),
                        v_ref[2, x, zz] - (q_ref[0, x + 3, zz + 1] - centre),
                    )
                )
            for component in range(3):
                first, second = pair[0][component], pair[1][component]
                early = jnp.where(lower, first, swap(second))
                late = jnp.where(lower, swap(first), second)
                for tile in range(2):
                    row = (component * 64 + 2 * m) * 32 + tile * 4 + x
                    lanes = slice(tile * 128, tile * 128 + 128)
                    solved_ref[pl.ds(row, 8, stride=8), :] = early[:, lanes]
                    solved_ref[pl.ds(row + 1024, 8, stride=8), :] = late[:, lanes]
        return 0

    lax.fori_loop(0, 16, correct, 0, unroll=2)
    couples = [(i, j) for i in range(4) for j in range(i, 4)]

    def update(block, sums):
        columns = []
        for i in range(4):
            rows = pl.ds(pl.multiple_of(block * 32 + 8 * i, 8), 8)
            cells = factor_ref[rows, :] + (2.0 * shift) * solved_ref[rows, :]
            nf_ref[rows, :] = cells
            columns.append(cells)
        return tuple(s + columns[i] * columns[j] for s, (i, j) in zip(sums, couples))

    sums = (jnp.zeros((8, 128), jnp.float32),) * len(couples)
    copies = []
    for part in range(4):
        sums = lax.fori_loop(part * 48, part * 48 + 48, update, sums, unroll=4)
        rows = pl.ds(part * 1536, 1536)
        copies.append(pltpu.make_async_copy(nf_ref.at[rows], nf_hbm.at[rows], sent.at[part]))
        copies[-1].start()
    t_ref[...] = jnp.zeros((32, 128), jnp.float32)
    for total, (i, j) in zip(sums, couples):
        t_ref[4 * i + j : 4 * i + j + 1, :] = jnp.sum(total, axis=0, keepdims=True)
    lanes = lax.broadcasted_iota(jnp.int32, (1, 128), 1)
    for sensor in range(4):
        component = cells_ref[sensor, 0]
        z = cells_ref[sensor, 1] - span * 64
        x = cells_ref[sensor, 2] - stream * 4
        y = cells_ref[sensor, 3]
        held = (z >= 0) & (z < 64) & (x >= 0) & (x < 4)
        z = jnp.clip(z, 0, 63)
        x = jnp.clip(x, 0, 3)
        tile = jnp.where(y >= 128, 1, 0)
        lane = jnp.where(held, y - 128 * tile, -1)
        for column in range(4):
            row = (component * 64 + z) * 32 + column * 8 + tile * 4 + x
            cells = solved_ref[pl.ds(row, 1), :]
            at = 16 + 4 * sensor + column
            t_ref[at : at + 1, :] = jnp.where(lanes == lane, cells, 0.0)
    totals = jnp.sum(t_ref[...], axis=1, keepdims=True)
    spread = lax.broadcasted_iota(jnp.int32, (32, 128), 1) == lax.broadcasted_iota(jnp.int32, (32, 128), 0)
    sums_ref[...] = jnp.sum(jnp.where(spread, totals, 0.0), axis=0, keepdims=True)
    for copy in copies:
        copy.wait()


def gain_kernel(index_ref, sums_ref, gain_ref, solved_ref, out_hbm, gram_ref, out_ref, sent):
    totals = jnp.sum(sums_ref[...], axis=0, keepdims=True)
    lanes = lax.broadcasted_iota(jnp.int32, (1, 128), 1)
    shift = shift_of(index_ref)

    def entry(at):
        return jnp.sum(jnp.where(lanes == at, totals, 0.0), axis=1, keepdims=True)

    table = [
        [jnp.broadcast_to(2.0 * shift * entry(16 + 4 * i + j), (8, 128)) for j in range(4)] for i in range(4)
    ]

    def body(block, _):
        rows = [pl.ds(pl.multiple_of(block * 32 + 8 * j, 8), 8) for j in range(4)]
        columns = [solved_ref[rows[j], :] for j in range(4)]
        for i in range(4):
            total = gain_ref[rows[i], :]
            for j in range(4):
                total = total + table[i][j] * columns[j]
            out_ref[rows[i], :] = total
        return 0

    copies = []
    for part in range(6):
        lax.fori_loop(part * 32, part * 32 + 32, body, 0, unroll=4)
        rows = pl.ds(part * 1024, 1024)
        copies.append(pltpu.make_async_copy(out_ref.at[rows], out_hbm.at[rows], sent.at[part]))
        copies[-1].start()
    row = lax.broadcasted_iota(jnp.int32, (4, 4), 0)
    column = lax.broadcasted_iota(jnp.int32, (4, 4), 1)
    gram = jnp.zeros((4, 4), jnp.float32)
    for i in range(4):
        for j in range(4):
            value = entry(4 * min(i, j) + max(i, j)) / 6291456.0
            gram = gram + jnp.where((row == i) & (column == j), value, 0.0)
    gram_ref[...] = gram
    for copy in copies:
        copy.wait()


def ring_sides():
    upper = lax.broadcasted_iota(jnp.int32, (8, 256), 0) // 4
    return upper == 1 - lax.rem(lax.axis_index("gz"), 2)


def joining_kernel(states_ref, partner_ref, joined_ref):
    first = ring_sides()
    for layer in range(5):
        own = [states_ref[i, layer] for i in range(POISSON)]
        near = [partner_ref[i, layer] for i in range(POISSON)]
        farther = [jnp.where(first, o, n) for o, n in zip(own, near)]
        for i in range(POISSON):
            nearer = jnp.where(first, near[i], own[i])
            joined_ref[i, layer] = nearer + turned(WHOLE_TABLES[0], farther, i)
        joined_ref[POISSON, layer] = states_ref[POISSON, layer]


def entering_kernel(states_ref, partner_ref, other_ref, inc_ref, a_ref, b_ref):
    first = ring_sides()
    odd = x_odd()
    even = 1 - odd
    rightward = z_even()
    once, twice, thrice, around = WHOLE_TABLES
    for layer in range(5):
        own = [states_ref[i, layer] for i in range(POISSON)]
        near = [partner_ref[i, layer] for i in range(POISSON)]
        far = [other_ref[i, layer] for i in range(POISSON)]
        entering = []
        for i in range(POISSON):
            cells = jnp.where(first, far[i] + turned(twice, near, i), near[i] + turned(once, far, i))
            entering.append(cells + turned(thrice, own, i))
        for i in range(POISSON):
            inc_ref[i, layer] = turned(around, entering, i)
        inc_ref[POISSON, layer] = jnp.where(rightward, partner_ref[POISSON, layer], other_ref[POISSON, layer])
    for layer in range(4):
        for i in range(POISSON + 1):
            a_ref[i, layer] = inc_ref[i, layer + even]
            b_ref[i, layer] = inc_ref[i, layer + odd]


def call(kernel, outputs, scratch, operands, smalls, flops, room, far_in=(), far_out=(), signals=(), least=0):
    arrays = [jax.ShapeDtypeStruct(shape, jnp.float32) for shape in outputs]
    places = [pl.BlockSpec(memory_space=pltpu.SMEM)] * smalls
    places += [pl.BlockSpec(memory_space=pltpu.VMEM)] * (len(operands) - smalls)
    results = [pl.BlockSpec(memory_space=pltpu.VMEM)] * len(outputs)
    for place in far_in:
        places[place] = pl.BlockSpec(memory_space=pltpu.HBM)
    for place in far_out:
        results[place] = pl.BlockSpec(memory_space=pltpu.HBM)
    moved = sum(4 * math.prod(shape) for shape in outputs) + sum(4 * math.prod(o.shape) for o in operands)
    return pl.pallas_call(
        kernel,
        out_shape=arrays,
        in_specs=places,
        out_specs=results,
        scratch_shapes=[pltpu.VMEM(shape, jnp.float32) for shape in scratch]
        + [pltpu.SemaphoreType.DMA((count,)) for count in signals],
        compiler_params=pltpu.CompilerParams(vmem_limit_bytes=room << 20),
        cost_estimate=pl.CostEstimate(flops=flops, bytes_accessed=moved, transcendentals=0),
    )(*operands)


def to_rows(cells):
    head = cells.shape[:-2]
    order = tuple(range(len(head)))
    split = cells.reshape(*head, 4, 2, 128).transpose(*order, len(head) + 1, len(head), len(head) + 2)
    return split.reshape(-1, 128)


def from_rows(rows, head):
    order = tuple(range(len(head)))
    split = rows.reshape(*head, 2, 4, 128).transpose(*order, len(head) + 1, len(head), len(head) + 2)
    return split.reshape(*head, 4, 256)


def fast_shards(factor, gain, base_flow, shift_index, sensor_cells):
    swap_in = [(0, 1), (1, 0), (2, 3), (3, 2), (4, 5), (5, 4), (6, 7), (7, 6)]
    swap_out = [(1, 2), (2, 1), (3, 4), (4, 3), (5, 6), (6, 5)]
    send_round = [(1, 2), (2, 1), (5, 6), (6, 5), (3, 7), (4, 0)]
    forward_round = [(7, 4), (0, 3)]
    near = [(0, 1), (1, 0), (2, 3), (3, 2)]
    far = [(1, 2), (2, 1), (3, 0), (0, 3)]
    factor_rows = to_rows(factor)
    base_rows = to_rows(base_flow)
    gain_rows = to_rows(gain)
    cell = (8, 256)
    own, a, b1, b2, z1, z2 = call(
        pack_kernel,
        [(3, 4, HALF, *cell), (312, *cell), (PART, *cell), (312 - PART, *cell), (26, *cell), (26, *cell)],
        [factor_rows.shape], [factor_rows, base_rows], 0, 10**6, 16, far_in=(0,), signals=(3,),
    )
    b1_in = lax.ppermute(b1, "gx", send_round)
    z1 = lax.ppermute(z1, "gz", near)
    z2 = lax.ppermute(z2, "gz", far)
    b2_in = lax.ppermute(b2, "gx", swap_out)
    a_in = lax.ppermute(a, "gx", swap_in)
    corners = len(CORNERS) + 3
    ca, cb = call(corner_kernel, [(corners, *cell)] * 2, [], [z1, z2], 0, 10**5, 4)
    ca = lax.ppermute(ca, "gx", swap_in)
    cb = lax.ppermute(cb, "gx", swap_out)
    b1_in, z1, z2 = lax.optimization_barrier((b1_in, z1, z2))
    b3_in = lax.ppermute(b1_in, "gx", forward_round)
    block = (7, 39, *cell)
    scratch = [(10, 80, 256)] + [block] * 5
    handed = call(
        functools.partial(velocity_kernel, "early"),
        [(3, 2, 39, *cell), (3, 2, 39, *cell), (3, HALF + 1, *cell)],
        scratch, [shift_index, own, base_rows, a_in, ca, z1, z2], 1, 10**8, 34,
    )
    velocity, sides, states, pa, pb1, pb2 = call(
        functools.partial(velocity_kernel, "late"),
        [(3, 4, HALF, *cell), (5, HALF, *cell), (POISSON + 1, 5, *cell), (4, HALF, *cell)]
        + [(2, HALF, *cell)] * 2,
        scratch,
        [shift_index, own, base_rows, b1_in, b3_in, b2_in, cb, z1, z2, *handed], 1, 10**8, 34,
    )
    pb1_in = lax.ppermute(pb1, "gx", send_round)
    pb2_in = lax.ppermute(pb2, "gx", swap_out)
    partner = lax.ppermute(states, "gz", near)
    (joined,) = call(joining_kernel, [states.shape], [], [states, partner], 0, 10**5, 4)
    other = lax.ppermute(joined, "gz", far)
    pb1_in, _ = lax.optimization_barrier((pb1_in, partner))
    pb3_in = lax.ppermute(pb1_in, "gx", forward_round)
    pa_in = lax.ppermute(pa, "gx", swap_in)
    entering, enter_a, enter_b = call(
        entering_kernel,
        [states.shape, (POISSON + 1, 4, *cell), (POISSON + 1, 4, *cell)],
        [], [states, partner, other], 0, 10**5, 4,
    )
    enter_b = lax.ppermute(enter_b, "gx", swap_out)
    enter_a = lax.ppermute(enter_a, "gx", swap_in)
    block = (11, HALF + 1, *cell)
    new_rows, solved, sums = call(
        pressure_kernel,
        [factor_rows.shape, factor_rows.shape, (1, 128)],
        [block, (POISSON + 1, 11, *cell), (2, POISSON, HALF + 1, *cell), (POISSON, *block), (32, 128)]
        + [factor_rows.shape],
        [shift_index, sensor_cells, velocity, sides, pa_in, pb1_in, pb3_in, pb2_in]
        + [entering, enter_a, enter_b, factor_rows],
        2, 10**8, 38, far_out=(0,), signals=(4,),
    )
    devices = lax.axis_size("gx") * lax.axis_size("gz")
    shared = lax.all_to_all(
        jnp.broadcast_to(sums[None], (devices, 1, 128)), ("gx", "gz"), split_axis=0, concat_axis=0, tiled=True
    )
    new_gain, gram = call(
        gain_kernel,
        [gain_rows.shape, (4, 4)],
        [gain_rows.shape], [shift_index, shared.reshape(devices, 128), gain_rows, solved], 1, 10**7, 14,
        far_out=(0,), signals=(6,),
    )
    head = factor.shape[:3]
    return (from_rows(new_rows, head), from_rows(new_gain, head), gram)


def solution(mesh):
    placed = (
        P(None, "gz", None, "gx", None),
        P(None, "gz", None, "gx", None),
        P("gz", "gx", None),
        P(),
        P(),
    )
    fits = mesh.shape["gx"] == 8 and mesh.shape["gz"] == 4
    return jax.shard_map(
        fast_shards if fits else shards,
        mesh=mesh,
        in_specs=placed,
        out_specs=(P(None, "gz", None, "gx", None), P(None, "gz", None, "gx", None), P()),
        check_vma=False,
    )
```

```python
import functools
import math

import jax
import jax.numpy as jnp
import numpy as np
from jax import lax
from jax.experimental import pallas as pl
from jax.experimental.pallas import tpu as pltpu
from jax.sharding import PartitionSpec as P

SWEEPS = 3
POISSON = 4
SHIFTS = 8


viscosity = 0.4
shift_table = (0.6, 0.8, 1.0, 1.25, 1.6, 2.0, 2.5, 3.2)
chebyshev_weights = (1.0 / 1.9352976, 1.0 / 1.4752809, 1.0 / 0.8247191, 1.0 / 0.3647024)
highest = lax.Precision.HIGHEST


def padded_2(cells, sides, width, closed):
    for axis, dim in sides:
        count = lax.axis_size(axis)
        ends = count if closed else count - 1
        head = lax.slice_in_dim(cells, 0, width, axis=dim)
        tail = lax.slice_in_dim(cells, cells.shape[dim] - width, cells.shape[dim], axis=dim)
        cells = jnp.concatenate(
            [
                lax.ppermute(tail, axis, [(i, (i + 1) % count) for i in range(ends)]),
                cells,
                lax.ppermute(head, axis, [((i + 1) % count, i) for i in range(ends)]),
            ],
            axis=dim,
        )
    return cells


def around_sum(padded):
    summed = padded[:, 1:-1, :, 2:, 1:-1] + padded[:, 1:-1, :, :-2, 1:-1]
    summed = summed + padded[:, 1:-1, :, 1:-1, 2:] + padded[:, 1:-1, :, 1:-1, :-2]
    return summed + padded[:, 2:, :, 1:-1, 1:-1] + padded[:, :-2, :, 1:-1, 1:-1]


def shards(factor, gain, base_flow, shift_index, sensor_cells):
    components, span_cells, columns, stream_cells, normal_cells = factor.shape
    stream_start = lax.axis_index("gx") * stream_cells
    span_start = lax.axis_index("gz") * span_cells
    stream_total = stream_cells * lax.axis_size("gx")
    span_total = span_cells * lax.axis_size("gz")
    shift_values = jnp.asarray(shift_table, jnp.float32)
    shift_value = jnp.sum(jnp.where(jnp.arange(SHIFTS) == shift_index[0], shift_values, 0.0))
    base_field = base_flow[None, :, None, :, :]
    diagonal = shift_value + 6.0 * viscosity + base_field
    source = -factor

    def stream_inside(extent, margin):
        positions = stream_start - margin + jnp.arange(extent)
        return ((positions >= 0) & (positions < stream_total)).astype(jnp.float32)

    def extend(grid_field):
        padded = padded_2(grid_field, (("gx", 3), ("gz", 1)), 1, True)
        padded = padded * stream_inside(stream_cells + 2, 1)[None, None, None, :, None]
        return jnp.pad(padded, ((0, 0), (0, 0), (0, 0), (0, 0), (1, 1)))

    velocity = source / diagonal
    for sweep_index in range(SWEEPS):
        padded = extend(velocity)
        velocity = (
            source + viscosity * around_sum(padded) + base_field * padded[:, 1:-1, :, :-2, 1:-1]
        ) / diagonal
    padded = extend(velocity)
    divergence = 2.0 * (velocity[0] - padded[0, 1:-1, :, :-2, 1:-1])
    divergence = divergence + (velocity[1] - padded[1, 1:-1, :, 1:-1, :-2])
    divergence = divergence + (velocity[2] - padded[2, :-2, :, 1:-1, 1:-1])
    span_index = jnp.arange(span_total)
    products = span_index[:, None] * span_index[None, :] % span_total
    angles = 2.0 * math.pi * products.astype(jnp.float32) / span_total
    hartley_table = (jnp.cos(angles) + jnp.sin(angles)) / math.sqrt(span_total)

    def turn_modes(exchanged):
        turned = jnp.einsum("kz,zay->kay", hartley_table, exchanged, precision=highest)
        return lax.all_to_all(turned, "gz", split_axis=0, concat_axis=1, tiled=True)

    def transform(grid_field):
        flat = grid_field.reshape(span_cells, columns * stream_cells, normal_cells)
        result = turn_modes(lax.all_to_all(flat, "gz", split_axis=1, concat_axis=0, tiled=True))
        return result.reshape(span_cells, columns, stream_cells, normal_cells)

    modes_rhs = -transform(divergence)
    wave_index = span_start + jnp.arange(span_cells)
    wavenumber = 2.0 * math.pi * wave_index.astype(jnp.float32) / span_total
    mode_diagonal = (10.0 + (2.0 - 2.0 * jnp.cos(wavenumber)))[:, None, None, None]
    pressure = chebyshev_weights[0] * modes_rhs / mode_diagonal
    for sweep_level in range(1, POISSON):
        padded = padded_2(pressure, (("gx", 2),), 1, False)
        padded = jnp.pad(padded, ((0, 0), (0, 0), (0, 0), (1, 1)))
        beside_all = (
            4.0 * (padded[:, :, 2:, 1:-1] + padded[:, :, :-2, 1:-1])
            + padded[:, :, 1:-1, 2:]
            + padded[:, :, 1:-1, :-2]
        )
        pressure = (
            pressure
            + chebyshev_weights[sweep_level]
            * (modes_rhs - (mode_diagonal * pressure - beside_all))
            / mode_diagonal
        )
    pressure = transform(pressure)
    padded = extend(pressure[None])[0]
    gradient = jnp.stack(
        [
            2.0 * (padded[1:-1, :, 2:, 1:-1] - pressure),
            padded[1:-1, :, 1:-1, 2:] - pressure,
            padded[2:, :, 1:-1, 1:-1] - pressure,
        ]
    )
    solved = velocity - gradient
    span_ids = span_start + jnp.arange(span_cells)
    stream_ids = stream_start + jnp.arange(stream_cells)
    normal_ids = jnp.arange(normal_cells)
    located = span_ids[None, :, None, None] == sensor_cells[:, 1][:, None, None, None]
    located = located & (stream_ids[None, None, :, None] == sensor_cells[:, 2][:, None, None, None])
    located = located & (normal_ids[None, None, None, :] == sensor_cells[:, 3][:, None, None, None])
    picked = jnp.einsum("szxy,czjxy->scj", located.astype(jnp.float32), solved, precision=highest)
    chooser = (jnp.arange(3)[None, :] == sensor_cells[:, 0:1]).astype(jnp.float32)
    readout_local = jnp.sum(picked * chooser[:, :, None], axis=1)
    new_factor = factor + 2.0 * shift_value * solved
    gram_local = jnp.einsum("czixy,czjxy->ij", new_factor, new_factor, precision=highest)
    gram_total, readout = lax.psum((gram_local, readout_local), ("gx", "gz"))
    gram = gram_total / (3.0 * stream_total * normal_cells * span_total)
    new_gain = gain + 2.0 * shift_value * jnp.einsum(
        "czjxy,ij->czixy", solved, readout, precision=highest
    )
    return (new_factor, new_gain, gram)


HALF = 32
PAIRS = 8


def recurrence_tables(centre, weights):
    ratio = centre / 2.0 - math.sqrt(centre * centre / 4.0 - 1.0)
    order = len(weights)
    step = ratio * np.tril(np.ones((order, order)))
    half = np.linalg.matrix_power(step, HALF)
    whole = np.linalg.matrix_power(step, 2 * HALF)
    angles = 2.0 * np.pi * np.arange(4096) / 4096
    series = [weights[0]]
    for weight in weights[1:]:
        longer = [0.0] + [weight * entry for entry in series]
        for place, entry in enumerate(series):
            longer[place] += (1.0 - weight) * entry
        longer[0] += weight
        series = longer
    mixes = []
    for power in range(1, order + 1):
        symbol = 1.0 / (centre - 2.0 * np.cos(angles)) ** power
        kernel = [np.mean(symbol * np.cos(angles * n)) for n in range(order + 1)]
        matrix = [[math.comb(n + i - 1, i - 1) for i in range(1, power + 1)] for n in range(1, power + 1)]
        sides = np.linalg.solve(
            np.array(matrix, np.float64), [kernel[n] / ratio**n for n in range(1, power + 1)]
        )
        middle = kernel[0] - 2.0 * np.sum(sides)
        mixes.append([float(series[power - 1] * entry) for entry in [middle, *sides]])
    square = whole @ whole
    around = np.linalg.inv(np.eye(order) - square @ square)
    wholes = [table.tolist() for table in (whole, square, square @ whole, around)]
    return float(ratio), half.tolist(), wholes, mixes


RATIO, HALF_TABLE, WHOLE_TABLES, MIXES = recurrence_tables(12.0, chebyshev_weights)


def lower_half():
    return lax.broadcasted_iota(jnp.int32, (8, 256), 0) < 4


def swap(cells):
    return pltpu.roll(cells, 4, 0)


def below(cells):
    lanes = lax.broadcasted_iota(jnp.int32, (8, 128), 1)
    low, high = pltpu.roll(cells[:, :128], 1, 1), pltpu.roll(cells[:, 128:], 1, 1)
    return jnp.concatenate([jnp.where(lanes > 0, low, 0.0), jnp.where(lanes > 0, high, low)], axis=1)


def above(cells):
    lanes = lax.broadcasted_iota(jnp.int32, (8, 128), 1)
    low, high = pltpu.roll(cells[:, :128], 127, 1), pltpu.roll(cells[:, 128:], 127, 1)
    return jnp.concatenate([jnp.where(lanes < 127, low, high), jnp.where(lanes < 127, high, 0.0)], axis=1)


def either_side(cells):
    lanes = lax.broadcasted_iota(jnp.int32, (8, 128), 1)
    low, high = cells[:, :128], cells[:, 128:]
    low_up, high_up = pltpu.roll(low, 1, 1), pltpu.roll(high, 1, 1)
    low_down, high_down = pltpu.roll(low, 127, 1), pltpu.roll(high, 127, 1)
    first = jnp.where(lanes > 0, low_up, 0.0) + jnp.where(lanes < 127, low_down, high_down)
    second = jnp.where(lanes > 0, high_up, low_up) + jnp.where(lanes < 127, high_down, 0.0)
    return jnp.concatenate([first, second], axis=1)


def shift_of(index_ref):
    index = index_ref[0]
    value = jnp.float32(shift_table[0])
    for place in range(1, SHIFTS):
        value = jnp.where(index == place, jnp.float32(shift_table[place]), value)
    return value


def x_odd():
    return lax.rem(lax.axis_index("gx"), 2)


def z_even():
    return lax.rem(lax.axis_index("gz"), 2) == 0


def cascade(state, cells):
    grown = []
    for entry in state:
        cells = RATIO * entry + cells
        grown.append(cells)
    return tuple(grown)


def half_states(read):
    zero = jnp.zeros((8, 256), jnp.float32)

    def body(t, carry):
        forward, backward = carry
        return cascade(forward, read(t)), cascade(backward, read(HALF - 1 - t))

    return lax.fori_loop(0, HALF, body, ((zero,) * POISSON, (zero,) * POISSON), unroll=8)


def turned(table, states, row):
    total = None
    for column in range(row + 1):
        term = table[row][column] * states[column]
        total = term if total is None else total + term
    return total


FACTOR_AT = 24
PART = 152
CORNERS = [(c, dx, side, 0) for c in range(3) for dx in (1, 2) for side in (0, 1)]
CORNERS += [(2, 1, 0, 1), (2, 3, 0, 0)]


def pack_kernel(factor_hbm, base_ref, own_ref, a_ref, b1_ref, b2_ref, z1_ref, z2_ref, factor_ref, arrived):
    share = factor_ref.shape[0] // 3
    copies = []
    for component in range(3):
        rows = pl.ds(component * share, share)
        copies.append(
            pltpu.make_async_copy(factor_hbm.at[rows], factor_ref.at[rows], arrived.at[component])
        )
        copies[-1].start()
    odd = x_odd()
    even = 1 - odd
    low = lax.broadcasted_iota(jnp.int32, (8, 128), 0) < 4
    scale = -1.0 / viscosity
    for component in range(3):

        def load(m, _, component=component):
            for x in range(4):
                for tile in range(2):
                    row = (component * 64 + 2 * m) * 32 + tile * 4 + x
                    first = factor_ref[pl.ds(row, 8, stride=8), :] * scale
                    second = factor_ref[pl.ds(row + 1024, 8, stride=8), :] * scale
                    lanes = slice(tile * 128, tile * 128 + 128)
                    own_ref[component, x, 2 * m, :, lanes] = jnp.where(low, first, swap(second))
                    own_ref[component, x, 2 * m + 1, :, lanes] = jnp.where(low, swap(first), second)
            return 0

        copies[component].wait()
        lax.fori_loop(0, 16, load, 0, unroll=2)

    def edges(zz, _):
        for component in range(3):
            for layer in range(3):
                at = FACTOR_AT + (component * 3 + layer) * HALF
                a_ref[at + zz] = own_ref[component, layer + even, zz]
                cells = own_ref[component, layer + odd, zz]
                if at < PART:
                    b1_ref[at + zz] = cells
                else:
                    b2_ref[at - PART + zz] = cells
        return 0

    lax.fori_loop(0, HALF, edges, 0, unroll=2)
    for layer in range(3):
        for group in range(8):
            for tile in range(2):
                lanes = slice(tile * 128, tile * 128 + 128)
                row = group * 64 + tile * 4 + layer
                a_ref[layer * 8 + group, :, lanes] = base_ref[pl.ds(row + even, 8, stride=8), :]
                b1_ref[layer * 8 + group, :, lanes] = base_ref[pl.ds(row + odd, 8, stride=8), :]
    lower = lower_half()
    rightward = z_even()
    for component in range(3):
        for x in range(4):
            for pair in range(2):
                cells = lambda zz: own_ref[component, x, zz]
                up = jnp.where(lower, swap(cells(31 - 2 * pair)), cells(30 - 2 * pair))
                down = jnp.where(lower, cells(2 * pair), swap(cells(2 * pair + 1)))
                at = (component * 4 + x) * 2 + pair
                z1_ref[at] = jnp.where(rightward, up, down)
                z2_ref[at] = jnp.where(rightward, down, up)
    for k in range(4):
        for tile in range(2):
            lanes = slice(tile * 128, tile * 128 + 128)
            up = base_ref[(63 - k) * 8 + tile * 4 : (63 - k) * 8 + tile * 4 + 4, :]
            down = base_ref[k * 8 + tile * 4 : k * 8 + tile * 4 + 4, :]
            rows = slice((k % 2) * 4, (k % 2) * 4 + 4)
            z1_ref[24 + k // 2, rows, lanes] = jnp.where(rightward, up, down)
            z2_ref[24 + k // 2, rows, lanes] = jnp.where(rightward, down, up)


def corner_kernel(z1_ref, z2_ref, a_ref, b_ref):
    odd = x_odd()
    rightward = z_even()

    def fill(behind_ref, ahead_ref):
        for place, (component, dx, side, pair) in enumerate(CORNERS):
            source = (behind_ref, ahead_ref)[side]
            right_x = 4 - dx
            left_x = dx - 1
            a_x = jnp.where(odd == 1, left_x, right_x)
            b_x = jnp.where(odd == 1, right_x, left_x)
            a_ref[place] = source[(component * 4 + a_x) * 2 + pair]
            b_ref[place] = source[(component * 4 + b_x) * 2 + pair]
        for dx in (1, 2, 3):
            for k in range(4):
                for side, source in enumerate((behind_ref, ahead_ref)):
                    from_right = source[24 + k // 2, (k % 2) * 4 + 4 - dx, :]
                    from_left = source[24 + k // 2, (k % 2) * 4 + dx - 1, :]
                    at = len(CORNERS) + dx - 1
                    a_ref[at, side * 4 + k, :] = jnp.where(odd == 1, from_left, from_right)
                    b_ref[at, side * 4 + k, :] = jnp.where(odd == 1, from_right, from_left)

    @pl.when(rightward)
    def _():
        fill(z2_ref, z1_ref)

    @pl.when(jnp.logical_not(rightward))
    def _():
        fill(z1_ref, z2_ref)


KNOWN = {("early", 0): (3, 9), ("early", 1): (0, 6), ("late", 0): (0, 5), ("late", 1): (4, 9)}
SWEPT = {
    ("early", 0): ((4, 8), (5, 7), (6, 6)),
    ("early", 1): ((1, 5), (2, 4), (3, 3)),
    ("late", 0): ((1, 3), (2, 4), (3, 5)),
    ("late", 1): ((6, 8), (5, 7), (4, 6)),
}
HANDED = (((4, 5), (5, 6), 6), ((4, 5), (3, 4), 3))


def velocity_kernel(stage, *refs):
    early = stage == "early"
    if early:
        index_ref, own_ref, base_ref, a_ref, c_ref, z1_ref, z2_ref, *refs = refs
        h1_ref, h2_ref, h3_ref, *refs = refs
    else:
        index_ref, own_ref, base_ref, b1_ref, b3_ref, b2_ref, c_ref, z1_ref, z2_ref, *refs = refs
        h1_ref, h2_ref, h3_ref, v_ref, bw_ref, s_ref, pa_ref, pb1_ref, pb2_ref, *refs = refs
    flow_ref, a1_ref, r_ref, v0_ref, va_ref, vb_ref = refs
    odd = x_odd()
    stream = lax.axis_index("gx")
    last = lax.axis_size("gx") - 1
    mask_left = jnp.where(stream > 0, 1.0, 0.0)
    mask_right = jnp.where(stream < last, 1.0, 0.0)
    relayed = jnp.logical_or(stream == 3, stream == 4)
    rightward = z_even()
    lower = lower_half()
    shift = shift_of(index_ref)
    zero = jnp.zeros((8, 256), jnp.float32)

    def each_z(step):
        @pl.when(rightward)
        def _():
            step(z2_ref, z1_ref)

        @pl.when(jnp.logical_not(rightward))
        def _():
            step(z1_ref, z2_ref)

    def inside(at):
        return lambda zz: a_ref[at + zz]

    def outside(first_ref):
        def pick(at):
            if at < PART:
                return lambda zz: first_ref[at + zz]
            return lambda zz: b2_ref[at - PART + zz]

        return pick

    def each_x(step):
        if early:
            step(inside)
            return

        @pl.when(relayed)
        def _():
            step(outside(b3_ref))

        @pl.when(jnp.logical_not(relayed))
        def _():
            step(outside(b1_ref))

    def before(cells, halo, k):
        if k % 2 == 0:
            return jnp.where(lower, halo, swap(cells))
        return swap(jnp.where(lower, cells, halo))

    def after(cells, halo, k):
        if k % 2 == 0:
            return swap(jnp.where(lower, halo, cells))
        return jnp.where(lower, swap(cells), halo)

    def run(parity):
        low, high = KNOWN[stage, parity]
        own_layers = [x for x in range(4) if low <= x + 3 <= high]
        if low < 3:
            halo = [(dx, 3 - dx, 3 - dx) for dx in (1, 2, 3)]
        else:
            halo = [(dx, 6 + dx, dx - 1) for dx in (1, 2, 3)]

        for x in own_layers:
            for group in range(8):
                for tile in range(2):
                    lanes = slice(tile * 128, tile * 128 + 128)
                    flow_ref[x + 3, 8 + 8 * group : 16 + 8 * group, lanes] = base_ref[
                        pl.ds(group * 64 + tile * 4 + x, 8, stride=8), :
                    ]

        def flow_span(behind_ref, ahead_ref):
            for x in own_layers:
                for k in range(4):
                    at = 24 + k // 2
                    row = (k % 2) * 4 + x
                    flow_ref[x + 3, 7 - k, :] = behind_ref[at, row, :]
                    flow_ref[x + 3, 72 + k, :] = ahead_ref[at, row, :]

        each_z(flow_span)

        def flow_stream(pick):
            for dx, place, layer in halo:
                for group in range(8):
                    flow_ref[place, 8 + 8 * group : 16 + 8 * group, :] = pick(layer * 8)(group)
                for k in range(4):
                    flow_ref[place, 7 - k, :] = c_ref[len(CORNERS) + dx - 1, k, :]
                    flow_ref[place, 72 + k, :] = c_ref[len(CORNERS) + dx - 1, 4 + k, :]

        each_x(flow_stream)

        def coefficients(zz, _):
            for x in range(low, high + 1):
                first = jnp.broadcast_to(flow_ref[x, pl.ds(zz + 4, 1), :], (8, 256))
                second = jnp.broadcast_to(flow_ref[x, pl.ds(zz + 36, 1), :], (8, 256))
                flow = jnp.where(lower, first, second)
                scale = viscosity * (mask_left if x < 3 else mask_right if x > 6 else 1.0)
                a1_ref[x - low, zz] = scale / (shift + 6.0 * viscosity + flow)
                r_ref[x - low, zz] = 1.0 + flow * (1.0 / viscosity)
            return 0

        lax.fori_loop(0, 39, coefficients, 0, unroll=3)
        for _, place, _ in halo:
            for zz in (0, 1, 2, 3, 36, 37, 38):
                v0_ref[place - low, zz] = zero

        def swept(source, span, zz, depth):
            result = {}
            first, final = span
            behind = [source(first - 1, zz + k) for k in range(depth)]
            here = [source(first, zz + k - 1) for k in range(depth + 2)]
            for x in range(first, final + 1):
                if x < final:
                    ahead = [source(x + 1, zz + k - 1) for k in range(depth + 2)]
                else:
                    ahead = [None] + [source(x + 1, zz + k) for k in range(depth)]
                result[x] = []
                for k in range(depth):
                    total = ahead[k + 1] + either_side(here[k + 1])
                    total = total + (here[k] + here[k + 2])
                    total = total + r_ref[x - low, zz + k] * behind[k]
                    result[x].append(v0_ref[x - low, zz + k] + a1_ref[x - low, zz + k] * total)
                behind, here = here[1 : depth + 1], ahead
            return result

        def sweep(source, target, level, margin, hand):
            depth = 4
            first, extent = 3 - margin, 33 + 2 * margin

            def body(t, _):
                zz = first + jnp.minimum(t * depth, extent - depth)
                for x, column in swept(source, SWEPT[stage, parity][level], zz, depth).items():
                    for k, cells in enumerate(column):
                        if target is not None:
                            target[x - low, zz + k] = cells
                        hand(x, zz + k, cells)
                return 0

            lax.fori_loop(0, -(-extent // depth), body, 0, unroll=3)

        handed_first, handed_second, handed_third = HANDED[parity]
        for component in range(3):

            def interior(zz, _, component=component):
                for x in own_layers:
                    v0_ref[x + 3 - low, zz + 4] = own_ref[component, x, zz] * a1_ref[x + 3 - low, zz + 4]
                return 0

            lax.fori_loop(0, HALF, interior, 0, unroll=4)

            def span(behind_ref, ahead_ref, component=component):
                for x in own_layers:
                    at = (component * 4 + x) * 2
                    for k in range(4):
                        cells = before(own_ref[component, x, 31 - k], behind_ref[at + k // 2], k)
                        v0_ref[x + 3 - low, 3 - k] = cells * a1_ref[x + 3 - low, 3 - k]
                    for k in range(3):
                        cells = after(own_ref[component, x, k], ahead_ref[at + k // 2], k)
                        v0_ref[x + 3 - low, 36 + k] = cells * a1_ref[x + 3 - low, 36 + k]

            each_z(span)

            def sides(pick, component=component):
                for dx, place, layer in halo:
                    read = pick(FACTOR_AT + (component * 3 + layer) * HALF)

                    def body(zz, _, read=read, place=place):
                        v0_ref[place - low, zz + 4] = read(zz) * a1_ref[place - low, zz + 4]
                        return 0

                    lax.fori_loop(0, HALF, body, 0, unroll=4)
                    for entry, (c, away, side, pair) in enumerate(CORNERS):
                        if c != component or away != dx:
                            continue
                        for k in (2 * pair, 2 * pair + 1):
                            if side == 0:
                                cells = before(read(31 - k), c_ref[entry], k)
                                v0_ref[place - low, 3 - k] = cells * a1_ref[place - low, 3 - k]
                            else:
                                cells = after(read(k), c_ref[entry], k)
                                v0_ref[place - low, 36 + k] = cells * a1_ref[place - low, 36 + k]

            each_x(sides)

            def hand_first(x, zz, cells, component=component):
                if early and x in handed_first:
                    h1_ref[component, handed_first.index(x), zz] = cells

            def hand_second(x, zz, cells, component=component):
                if early and x in handed_second:
                    h2_ref[component, handed_second.index(x), zz] = cells

            def hand_third(x, zz, cells, component=component):
                h3_ref[component, zz - 3] = cells

            def from_first(x, zz, component=component):
                if not early and x in handed_first:
                    return h1_ref[component, handed_first.index(x), zz]
                return va_ref[x - low, zz]

            def from_second(x, zz, component=component):
                if not early and x in handed_second:
                    return h2_ref[component, handed_second.index(x), zz]
                return vb_ref[x - low, zz]

            sweep(lambda x, zz: v0_ref[x - low, zz], va_ref, 0, 2, hand_first)
            sweep(from_first, vb_ref, 1, 1, hand_second)
            if early:
                sweep(from_second, None, 2, 0, hand_third)
                continue

            def finished(zz, depth, component=component):
                found = swept(from_second, SWEPT[stage, parity][2], zz + 4, depth)
                found[handed_third] = [h3_ref[component, zz + 1 + k] for k in range(depth)]
                return [[found[x + 3][k] for x in range(4)] for k in range(depth)]

            def diverge(t, past, component=component):
                for k, cells in enumerate(finished(4 * t, 4)):
                    zz = 4 * t + k
                    for x in range(4):
                        v_ref[component, x, zz] = cells[x]
                        if component == 0:
                            bw_ref[x, zz] = -2.0 * (cells[x] if x == 0 else cells[x] - cells[x - 1])
                        elif component == 1:
                            bw_ref[x, zz] = bw_ref[x, zz] - (cells[x] - below(cells[x]))
                        else:
                            bw_ref[x, zz] = bw_ref[x, zz] - (cells[x] - past[x])
                    if component == 0:
                        bw_ref[4, zz] = cells[3]
                    past = tuple(cells) if component == 2 else 0
                return past

            start = tuple(finished(-1, 1)[0]) if component == 2 else 0
            lax.fori_loop(0, HALF // 4, diverge, start, unroll=4)

    for parity in (0, 1):

        @pl.when(odd == parity)
        def _(parity=parity):
            run(parity)

    if early:
        return

    def edges(zz, _):
        for layer in range(4):
            pa_ref[layer, zz] = bw_ref[layer + 1 - odd, zz]
            (pb1_ref if layer < 2 else pb2_ref)[layer % 2, zz] = bw_ref[layer + odd, zz]
        return 0

    lax.fori_loop(0, HALF, edges, 0, unroll=4)

    def states(layer, _):
        forward, backward = half_states(lambda t: bw_ref[layer, t])
        swapped_forward = [swap(entry) for entry in forward]
        swapped_backward = [swap(entry) for entry in backward]
        for i in range(POISSON):
            onward = forward[i] + turned(HALF_TABLE, swapped_forward, i)
            back = backward[i] + turned(HALF_TABLE, swapped_backward, i)
            s_ref[i, layer] = jnp.where(lower, back, onward)
        s_ref[POISSON, layer] = bw_ref[layer, 0]
        return 0

    lax.fori_loop(0, 5, states, 0, unroll=5)


def pressure_kernel(
    index_ref, cells_ref, v_ref, bw_ref, ba_ref, b1_ref, b3_ref, b2_ref, inc_ref, ia_ref, ib_ref, factor_ref,
    nf_hbm, solved_ref, sums_ref,
    f_ref, i_ref, u_ref, q_ref, t_ref, nf_ref, sent,
):
    odd = x_odd()
    stream = lax.axis_index("gx")
    span = lax.axis_index("gz")
    last = lax.axis_size("gx") - 1
    mask_left = jnp.where(stream > 0, 1.0, 0.0)
    mask_right = jnp.where(stream < last, 1.0, 0.0)
    lower = lower_half()
    shift = shift_of(index_ref)

    def gather(left, right, left_inc, right_inc):
        def body(zz, _):
            for x in range(3):
                f_ref[x, zz] = mask_left * left(x, zz)
                f_ref[x + 4, zz] = bw_ref[x + 1, zz]
                f_ref[x + 8, zz] = mask_right * right(x + 1, zz)
            f_ref[3, zz] = bw_ref[0, zz] + (2.0 * mask_left) * left(3, zz)
            f_ref[7, zz] = mask_right * (right(0, zz) + 2.0 * bw_ref[4, zz])
            return 0

        lax.fori_loop(0, HALF, body, 0, unroll=4)
        for i in range(POISSON + 1):
            for x in range(3):
                i_ref[i, x] = left_inc(i, x)
                i_ref[i, x + 4] = inc_ref[i, x + 1]
                i_ref[i, x + 8] = right_inc(i, x + 1)
            i_ref[i, 3] = inc_ref[i, 0] + 2.0 * left_inc(i, 3)
            i_ref[i, 7] = mask_right * (right_inc(i, 0) + 2.0 * inc_ref[i, 4])
        for x in range(11):
            f_ref[x, HALF] = swap(jnp.where(lower, i_ref[POISSON, x], f_ref[x, 0]))

    def enter_inside(i, layer):
        return ia_ref[i, layer]

    def enter_outside(i, layer):
        return ib_ref[i, layer]

    def inside(layer, zz):
        return ba_ref[layer, zz]

    def direct(layer, zz):
        return b1_ref[layer, zz] if layer < 2 else b2_ref[layer - 2, zz]

    def relayed(layer, zz):
        return b3_ref[layer, zz] if layer < 2 else b2_ref[layer - 2, zz]

    middle = jnp.logical_or(stream == 3, stream == 4)
    for parity in (0, 1):
        for through, outside in ((False, direct), (True, relayed)):

            @pl.when(jnp.logical_and(odd == parity, middle == through))
            def _(parity=parity, outside=outside):
                if parity == 0:
                    gather(outside, inside, enter_outside, enter_inside)
                else:
                    gather(inside, outside, enter_inside, enter_outside)

    def solve(layers, least):
        count = len(layers)
        zero = (jnp.zeros((8, 256), jnp.float32),) * POISSON

        def halves(t, carry):
            return tuple(
                (cascade(up, f_ref[x, t]), cascade(down, f_ref[x, HALF - 1 - t]))
                for x, (up, down) in zip(layers, carry)
            )

        ends = lax.fori_loop(0, HALF, halves, ((zero, zero),) * count, unroll=8)
        onward = []
        back = []
        for x, (forward, backward) in zip(layers, ends):
            arriving = [i_ref[i, x] for i in range(POISSON)]
            swapped = [swap(entry) for entry in arriving]
            carried = [turned(HALF_TABLE, swapped, i) for i in range(POISSON)]
            onward.append(
                tuple(
                    swap(jnp.where(lower, forward[i] + carried[i], arriving[i])) for i in range(POISSON)
                )
            )
            back.append(
                tuple(
                    swap(jnp.where(lower, arriving[i], backward[i] + carried[i])) for i in range(POISSON)
                )
            )

        def ahead(zz, states):
            states = tuple(cascade(state, f_ref[x, zz]) for x, state in zip(layers, states))
            for slot, state in enumerate(states):
                for i in range(POISSON):
                    u_ref[slot, i, zz] = state[i]
            return states

        ahead(HALF, lax.fori_loop(0, HALF, ahead, tuple(onward), unroll=8))

        def mix(zz, states):
            for slot, (x, state) in enumerate(zip(layers, states)):
                both = [f_ref[x, zz]] + [u_ref[slot, i, zz] + state[i] for i in range(POISSON)]
                for power in range(least, POISSON):
                    total = MIXES[power][0] * both[0]
                    for i in range(1, power + 2):
                        total = total + MIXES[power][i] * both[i]
                    q_ref[power, x, zz] = total

        mix(HALF, back)

        def behind(t, states):
            zz = HALF - 1 - t
            states = tuple(cascade(state, f_ref[x, zz]) for x, state in zip(layers, states))
            mix(zz, states)
            return states

        lax.fori_loop(0, HALF, behind, tuple(back), unroll=8)

    solve((5,), 0)
    for distance in (-1, 0, 1, 2, 3):
        solve((3 - distance, 7 + distance), max(distance, 0))
    for power in (2, 1, 0):

        def apply(zz, _, power=power):
            edge = 2 - power
            layers = {x: q_ref[power + 1, x, zz] for x in range(edge, 11 - edge)}
            for x in range(edge + 1, 10 - edge if power else 8):
                beside = 4.0 * (layers[x - 1] + layers[x + 1]) + either_side(layers[x])
                if x < 3:
                    beside = mask_left * beside
                if x > 6:
                    beside = mask_right * beside
                q_ref[power, x, zz] = q_ref[power, x, zz] + beside
            return 0

        lax.fori_loop(0, HALF + 1, apply, 0, unroll=HALF + 1)

    def correct(m, _):
        for x in range(4):
            pair = []
            for zz in (2 * m, 2 * m + 1):
                centre = q_ref[0, x + 3, zz]
                pair.append(
                    (
                        v_ref[0, x, zz] - 2.0 * (q_ref[0, x + 4, zz] - centre),
                        v_ref[1, x, zz] - (above(centre) - centre),
                        v_ref[2, x, zz] - (q_ref[0, x + 3, zz + 1] - centre),
                    )
                )
            for component in range(3):
                first, second = pair[0][component], pair[1][component]
                early = jnp.where(lower, first, swap(second))
                late = jnp.where(lower, swap(first), second)
                for tile in range(2):
                    row = (component * 64 + 2 * m) * 32 + tile * 4 + x
                    lanes = slice(tile * 128, tile * 128 + 128)
                    solved_ref[pl.ds(row, 8, stride=8), :] = early[:, lanes]
                    solved_ref[pl.ds(row + 1024, 8, stride=8), :] = late[:, lanes]
        return 0

    lax.fori_loop(0, 16, correct, 0, unroll=2)
    couples = [(i, j) for i in range(4) for j in range(i, 4)]

    def update(block, sums):
        columns = []
        for i in range(4):
            rows = pl.ds(pl.multiple_of(block * 32 + 8 * i, 8), 8)
            cells = factor_ref[rows, :] + (2.0 * shift) * solved_ref[rows, :]
            nf_ref[rows, :] = cells
            columns.append(cells)
        return tuple(s + columns[i] * columns[j] for s, (i, j) in zip(sums, couples))

    sums = (jnp.zeros((8, 128), jnp.float32),) * len(couples)
    copies = []
    for part in range(4):
        sums = lax.fori_loop(part * 48, part * 48 + 48, update, sums, unroll=4)
        rows = pl.ds(part * 1536, 1536)
        copies.append(pltpu.make_async_copy(nf_ref.at[rows], nf_hbm.at[rows], sent.at[part]))
        copies[-1].start()
    t_ref[...] = jnp.zeros((32, 128), jnp.float32)
    for total, (i, j) in zip(sums, couples):
        t_ref[4 * i + j : 4 * i + j + 1, :] = jnp.sum(total, axis=0, keepdims=True)
    lanes = lax.broadcasted_iota(jnp.int32, (1, 128), 1)
    for sensor in range(4):
        component = cells_ref[sensor, 0]
        z = cells_ref[sensor, 1] - span * 64
        x = cells_ref[sensor, 2] - stream * 4
        y = cells_ref[sensor, 3]
        held = (z >= 0) & (z < 64) & (x >= 0) & (x < 4)
        z = jnp.clip(z, 0, 63)
        x = jnp.clip(x, 0, 3)
        tile = jnp.where(y >= 128, 1, 0)
        lane = jnp.where(held, y - 128 * tile, -1)
        for column in range(4):
            row = (component * 64 + z) * 32 + column * 8 + tile * 4 + x
            cells = solved_ref[pl.ds(row, 1), :]
            at = 16 + 4 * sensor + column
            t_ref[at : at + 1, :] = jnp.where(lanes == lane, cells, 0.0)
    totals = jnp.sum(t_ref[...], axis=1, keepdims=True)
    spread = lax.broadcasted_iota(jnp.int32, (32, 128), 1) == lax.broadcasted_iota(jnp.int32, (32, 128), 0)
    sums_ref[...] = jnp.sum(jnp.where(spread, totals, 0.0), axis=0, keepdims=True)
    for copy in copies:
        copy.wait()


def gain_kernel(index_ref, sums_ref, gain_ref, solved_ref, out_hbm, gram_ref, out_ref, sent):
    totals = jnp.sum(sums_ref[...], axis=0, keepdims=True)
    lanes = lax.broadcasted_iota(jnp.int32, (1, 128), 1)
    shift = shift_of(index_ref)

    def entry(at):
        return jnp.sum(jnp.where(lanes == at, totals, 0.0), axis=1, keepdims=True)

    table = [
        [jnp.broadcast_to(2.0 * shift * entry(16 + 4 * i + j), (8, 128)) for j in range(4)] for i in range(4)
    ]

    def body(block, _):
        rows = [pl.ds(pl.multiple_of(block * 32 + 8 * j, 8), 8) for j in range(4)]
        columns = [solved_ref[rows[j], :] for j in range(4)]
        for i in range(4):
            total = gain_ref[rows[i], :]
            for j in range(4):
                total = total + table[i][j] * columns[j]
            out_ref[rows[i], :] = total
        return 0

    copies = []
    for part in range(6):
        lax.fori_loop(part * 32, part * 32 + 32, body, 0, unroll=4)
        rows = pl.ds(part * 1024, 1024)
        copies.append(pltpu.make_async_copy(out_ref.at[rows], out_hbm.at[rows], sent.at[part]))
        copies[-1].start()
    row = lax.broadcasted_iota(jnp.int32, (4, 4), 0)
    column = lax.broadcasted_iota(jnp.int32, (4, 4), 1)
    gram = jnp.zeros((4, 4), jnp.float32)
    for i in range(4):
        for j in range(4):
            value = entry(4 * min(i, j) + max(i, j)) / 6291456.0
            gram = gram + jnp.where((row == i) & (column == j), value, 0.0)
    gram_ref[...] = gram
    for copy in copies:
        copy.wait()


def ring_sides():
    upper = lax.broadcasted_iota(jnp.int32, (8, 256), 0) // 4
    return upper == 1 - lax.rem(lax.axis_index("gz"), 2)


def joining_kernel(states_ref, partner_ref, joined_ref):
    first = ring_sides()
    for layer in range(5):
        own = [states_ref[i, layer] for i in range(POISSON)]
        near = [partner_ref[i, layer] for i in range(POISSON)]
        farther = [jnp.where(first, o, n) for o, n in zip(own, near)]
        for i in range(POISSON):
            nearer = jnp.where(first, near[i], own[i])
            joined_ref[i, layer] = nearer + turned(WHOLE_TABLES[0], farther, i)
        joined_ref[POISSON, layer] = states_ref[POISSON, layer]


def entering_kernel(states_ref, partner_ref, other_ref, inc_ref, a_ref, b_ref):
    first = ring_sides()
    odd = x_odd()
    even = 1 - odd
    rightward = z_even()
    once, twice, thrice, around = WHOLE_TABLES
    for layer in range(5):
        own = [states_ref[i, layer] for i in range(POISSON)]
        near = [partner_ref[i, layer] for i in range(POISSON)]
        far = [other_ref[i, layer] for i in range(POISSON)]
        entering = []
        for i in range(POISSON):
            cells = jnp.where(first, far[i] + turned(twice, near, i), near[i] + turned(once, far, i))
            entering.append(cells + turned(thrice, own, i))
        for i in range(POISSON):
            inc_ref[i, layer] = turned(around, entering, i)
        inc_ref[POISSON, layer] = jnp.where(rightward, partner_ref[POISSON, layer], other_ref[POISSON, layer])
    for layer in range(4):
        for i in range(POISSON + 1):
            a_ref[i, layer] = inc_ref[i, layer + even]
            b_ref[i, layer] = inc_ref[i, layer + odd]


def call(kernel, outputs, scratch, operands, smalls, flops, room, far_in=(), far_out=(), signals=(), least=0):
    arrays = [jax.ShapeDtypeStruct(shape, jnp.float32) for shape in outputs]
    places = [pl.BlockSpec(memory_space=pltpu.SMEM)] * smalls
    places += [pl.BlockSpec(memory_space=pltpu.VMEM)] * (len(operands) - smalls)
    results = [pl.BlockSpec(memory_space=pltpu.VMEM)] * len(outputs)
    for place in far_in:
        places[place] = pl.BlockSpec(memory_space=pltpu.HBM)
    for place in far_out:
        results[place] = pl.BlockSpec(memory_space=pltpu.HBM)
    moved = sum(4 * math.prod(shape) for shape in outputs) + sum(4 * math.prod(o.shape) for o in operands)
    return pl.pallas_call(
        kernel,
        out_shape=arrays,
        in_specs=places,
        out_specs=results,
        scratch_shapes=[pltpu.VMEM(shape, jnp.float32) for shape in scratch]
        + [pltpu.SemaphoreType.DMA((count,)) for count in signals],
        compiler_params=pltpu.CompilerParams(vmem_limit_bytes=room << 20),
        cost_estimate=pl.CostEstimate(flops=flops, bytes_accessed=moved, transcendentals=0),
    )(*operands)


def to_rows(cells):
    head = cells.shape[:-2]
    order = tuple(range(len(head)))
    split = cells.reshape(*head, 4, 2, 128).transpose(*order, len(head) + 1, len(head), len(head) + 2)
    return split.reshape(-1, 128)


def from_rows(rows, head):
    order = tuple(range(len(head)))
    split = rows.reshape(*head, 2, 4, 128).transpose(*order, len(head) + 1, len(head), len(head) + 2)
    return split.reshape(*head, 4, 256)


def fast_shards(factor, gain, base_flow, shift_index, sensor_cells):
    swap_in = [(0, 1), (1, 0), (2, 3), (3, 2), (4, 5), (5, 4), (6, 7), (7, 6)]
    swap_out = [(1, 2), (2, 1), (3, 4), (4, 3), (5, 6), (6, 5)]
    send_round = [(1, 2), (2, 1), (5, 6), (6, 5), (3, 7), (4, 0)]
    forward_round = [(7, 4), (0, 3)]
    near = [(0, 1), (1, 0), (2, 3), (3, 2)]
    far = [(1, 2), (2, 1), (3, 0), (0, 3)]
    factor_rows = to_rows(factor)
    base_rows = to_rows(base_flow)
    gain_rows = to_rows(gain)
    cell = (8, 256)
    own, a, b1, b2, z1, z2 = call(
        pack_kernel,
        [(3, 4, HALF, *cell), (312, *cell), (PART, *cell), (312 - PART, *cell), (26, *cell), (26, *cell)],
        [factor_rows.shape], [factor_rows, base_rows], 0, 10**6, 16, far_in=(0,), signals=(3,),
    )
    b1_in = lax.ppermute(b1, "gx", send_round)
    z1 = lax.ppermute(z1, "gz", near)
    z2 = lax.ppermute(z2, "gz", far)
    b2_in = lax.ppermute(b2, "gx", swap_out)
    a_in = lax.ppermute(a, "gx", swap_in)
    corners = len(CORNERS) + 3
    ca, cb = call(corner_kernel, [(corners, *cell)] * 2, [], [z1, z2], 0, 10**5, 4)
    ca = lax.ppermute(ca, "gx", swap_in)
    cb = lax.ppermute(cb, "gx", swap_out)
    b1_in, z1, z2 = lax.optimization_barrier((b1_in, z1, z2))
    b3_in = lax.ppermute(b1_in, "gx", forward_round)
    block = (7, 39, *cell)
    scratch = [(10, 80, 256)] + [block] * 5
    handed = call(
        functools.partial(velocity_kernel, "early"),
        [(3, 2, 39, *cell), (3, 2, 39, *cell), (3, HALF + 1, *cell)],
        scratch, [shift_index, own, base_rows, a_in, ca, z1, z2], 1, 10**8, 34,
    )
    velocity, sides, states, pa, pb1, pb2 = call(
        functools.partial(velocity_kernel, "late"),
        [(3, 4, HALF, *cell), (5, HALF, *cell), (POISSON + 1, 5, *cell), (4, HALF, *cell)]
        + [(2, HALF, *cell)] * 2,
        scratch,
        [shift_index, own, base_rows, b1_in, b3_in, b2_in, cb, z1, z2, *handed], 1, 10**8, 34,
    )
    pb1_in = lax.ppermute(pb1, "gx", send_round)
    pb2_in = lax.ppermute(pb2, "gx", swap_out)
    partner = lax.ppermute(states, "gz", near)
    (joined,) = call(joining_kernel, [states.shape], [], [states, partner], 0, 10**5, 4)
    other = lax.ppermute(joined, "gz", far)
    pb1_in, _ = lax.optimization_barrier((pb1_in, partner))
    pa, _ = lax.optimization_barrier((pa, partner))
    pb3_in = lax.ppermute(pb1_in, "gx", forward_round)
    pa_in = lax.ppermute(pa, "gx", swap_in)
    entering, enter_a, enter_b = call(
        entering_kernel,
        [states.shape, (POISSON + 1, 4, *cell), (POISSON + 1, 4, *cell)],
        [], [states, partner, other], 0, 10**5, 4,
    )
    enter_b = lax.ppermute(enter_b, "gx", swap_out)
    enter_a = lax.ppermute(enter_a, "gx", swap_in)
    block = (11, HALF + 1, *cell)
    new_rows, solved, sums = call(
        pressure_kernel,
        [factor_rows.shape, factor_rows.shape, (1, 128)],
        [block, (POISSON + 1, 11, *cell), (2, POISSON, HALF + 1, *cell), (POISSON, *block), (32, 128)]
        + [factor_rows.shape],
        [shift_index, sensor_cells, velocity, sides, pa_in, pb1_in, pb3_in, pb2_in]
        + [entering, enter_a, enter_b, factor_rows],
        2, 10**8, 38, far_out=(0,), signals=(4,),
    )
    devices = lax.axis_size("gx") * lax.axis_size("gz")
    shared = lax.all_to_all(
        jnp.broadcast_to(sums[None], (devices, 1, 128)), ("gx", "gz"), split_axis=0, concat_axis=0, tiled=True
    )
    new_gain, gram = call(
        gain_kernel,
        [gain_rows.shape, (4, 4)],
        [gain_rows.shape], [shift_index, shared.reshape(devices, 128), gain_rows, solved], 1, 10**7, 14,
        far_out=(0,), signals=(6,),
    )
    head = factor.shape[:3]
    return (from_rows(new_rows, head), from_rows(new_gain, head), gram)


def solution(mesh):
    placed = (
        P(None, "gz", None, "gx", None),
        P(None, "gz", None, "gx", None),
        P("gz", "gx", None),
        P(),
        P(),
    )
    fits = mesh.shape["gx"] == 8 and mesh.shape["gz"] == 4
    return jax.shard_map(
        fast_shards if fits else shards,
        mesh=mesh,
        in_specs=placed,
        out_specs=(P(None, "gz", None, "gx", None), P(None, "gz", None, "gx", None), P()),
        check_vma=False,
    )
```
